32 devices in a mesh: row: 8 (over y, x, core), tensor: 4 (over z).
Axes of the slice: x: 2, y: 2, z: 4, core: 2. Of those that a mesh axis runs over, the one named last changes fastest.
Arguments:
- latents: bfloat16 [4, 16, 64, 2240], P(None, 'row', None, 'tensor'), may hold values from -6 to 6
- clip_height: int32 [4], replicated, may hold values from 8 to 16, as said below
- clip_width: int32 [4], replicated, may hold values from 32 to 64, as said below
- expand_weight: bfloat16 [2, 2240, 5600], P(None, None, 'tensor'), may hold values from -0.125 to 0.125
- expand_bias: float32 [2, 5600], P(None, 'tensor'), may hold values from -3 to 3
- depth_weight: float32 [3, 3, 2, 5600], P(None, None, None, 'tensor'), may hold values from -2 to 2
- depth_bias: float32 [2, 5600], P(None, 'tensor'), may hold values from -3 to 3
- project_weight: bfloat16 [5600, 2240], P('tensor'), may hold values from -0.109375 to 0.109375
Outputs:
- block_output: bfloat16 [4, 16, 64, 2240], P(None, 'row', None, 'tensor')
The draws below stay inside these ranges and needn't reach their ends.
Inputs may be any that keep to these rules, and one draw needn't show every extreme that they name: `clip_height`: one clip spans all 16 rows and another exactly 8 of them. `clip_width`: one clip spans all 64 columns and another exactly 32 of them.
All inputs are finite; a program needn't handle non-finite values.
Results may differ from the reference program's by a relative error of at most 0.0062.
Values may be sent and summed in bfloat16 or wider, within the bound.
No kernel may reach another device: no remote copies, remote signals or barrier semaphores. Data moves between devices by JAX's collectives and lax.ppermute only.
A program may use at most 128 MiB of HBM per device.

```python
import jax
import jax.numpy as jnp
from jax import lax

D = 2240
FF = 5600
BATCH = 4
CW = 64
NH = 16


def bucket_draw(key, upper_bound, item_count):
    levels = jax.random.randint(key, (item_count,), upper_bound // 2, upper_bound + 1)
    ranking = jax.random.permutation(jax.random.fold_in(key, 7), item_count)
    levels = jnp.where(ranking == 0, upper_bound, levels)
    levels = jnp.where(ranking == 1, upper_bound // 2, levels)
    return levels.astype(jnp.int32)


def draw_clip_height(key, part):
    return bucket_draw(jax.random.fold_in(key, 11), NH, BATCH)


def draw_clip_width(key, part):
    return bucket_draw(jax.random.fold_in(key, 13), CW, BATCH)


def with_spikes(result, key, source, target, shards_of, factor):
    def block_of(dim):
        return (jnp.arange(result.shape[dim]) // (result.shape[dim] // shards_of)).reshape((-1,) + (1,) * (result.ndim - 1 - dim))

    near = jax.random.permutation(key, shards_of)[block_of(target)]
    far = (block_of(target) + shards_of // 2) % shards_of
    return jnp.where((block_of(source) == near) | (block_of(source) == far), factor * result, result)


def steps_of(key, extent, shards, least, top_value):
    gain, own = 1.0, jax.random.fold_in(key, 6)
    for dim, shards_of in shards:
        steps = jnp.exp(jax.random.uniform(jax.random.fold_in(own, dim), (shards_of,), jnp.float32, least / len(shards), top_value / len(shards)))
        gain = gain * jnp.repeat(steps, extent[dim] // shards_of).reshape([-1 if axis == dim else 1 for axis in range(len(extent))])
    return gain


def noise(rng, dims, width, limit, pieces=(), kind=jnp.bfloat16):
    level = steps_of(rng, dims, pieces, -0.22, 0.18) if pieces else 1.0
    array = jax.random.normal(rng, dims, jnp.float32) * width * level
    return jnp.minimum(jnp.maximum(array, -limit), limit).astype(kind)


def noise_with(rng, extent, width, bound, split, heavy, kind=jnp.bfloat16):
    result = width * jax.random.normal(rng, extent, jnp.float32)
    if split:
        result = result * steps_of(rng, extent, split, -0.22, 0.18)
    return jnp.clip(with_spikes(result, jax.random.fold_in(rng, 3), *heavy), -bound, bound).astype(kind)


def setup_inputs(seed: int = 0) -> dict:
    splits = jax.random.split(jax.random.key(seed), 9)
    return {
        "latents": noise(splits[0], (BATCH, NH, CW, D), 1.0, 6.0, ((1, 8), (3, 4))),
        "clip_height": draw_clip_height(jax.random.fold_in(splits[8], 71), 0),
        "clip_width": draw_clip_width(jax.random.fold_in(splits[8], 71), 0),
        "expand_weight": noise(splits[3], (2, D, FF), D ** -0.5, 0.125, ((2, 4),)),
        "expand_bias": noise(splits[4], (2, FF), 0.5, 3.0, ((1, 4),), jnp.float32),
        "depth_weight": noise(splits[5], (3, 3, 2, FF), 9 ** -0.5, 2.0, ((3, 4),), jnp.float32),
        "depth_bias": noise(splits[6], (2, FF), 0.5, 3.0, ((1, 4),), jnp.float32),
        "project_weight": noise_with(splits[7], (FF, D), FF ** -0.5, 0.109375, ((0, 4),), (0, 1, 4, 2.0)),
    }


def reference(latents, clip_height, clip_width, expand_weight, expand_bias, depth_weight, depth_bias, project_weight):
    def per_sample(inputs):
        sample, height_limit, width_limit = inputs
        row_ids = jnp.arange(NH, dtype=jnp.int32)
        col_ids = jnp.arange(CW, dtype=jnp.int32)
        valid_mask = ((row_ids[:, None] < height_limit) & (col_ids[None, :] < width_limit)).astype(jnp.float32)[..., None]
        flat = sample.reshape(NH * CW, D)
        halves = [jnp.dot(flat, expand_weight[half], preferred_element_type=jnp.float32).reshape(NH, CW, FF) for half in range(2)]
        pre_act = jnp.stack(halves, axis=2) + expand_bias
        expanded = (jax.nn.silu(pre_act) * valid_mask[..., None]).astype(jnp.bfloat16)
        padded = jnp.pad(expanded, ((1, 1), (1, 1), (0, 0), (0, 0)))
        depth_out = jnp.zeros((NH, CW, 2, FF), jnp.float32) + depth_bias
        for tap_row in range(3):
            for tap_col in range(3):
                depth_out = depth_out + depth_weight[tap_row, tap_col] * padded[tap_row:tap_row + NH, tap_col:tap_col + CW]
        hidden = (depth_out[:, :, 0] * jax.nn.silu(depth_out[:, :, 1])).astype(jnp.bfloat16)
        projected = jnp.dot(hidden.reshape(NH * CW, FF), project_weight, preferred_element_type=jnp.float32).reshape(NH, CW, D)
        return (projected * valid_mask).astype(jnp.bfloat16)

    return lax.map(per_sample, (latents, clip_height, clip_width))
```

```python
import jax
import jax.numpy as jnp
from jax import lax
from jax.sharding import PartitionSpec as P


def halo_rows(cells):
    count = lax.axis_size("row")
    ends = count - 1
    head = cells[:, :1]
    tail = cells[:, -1:]
    above = lax.ppermute(tail, "row", [(i, i + 1) for i in range(ends)])
    below = lax.ppermute(head, "row", [(i + 1, i) for i in range(ends)])
    return jnp.concatenate([above, cells, below], axis=1)


def depthwise(padded, depth_weight, depth_bias, row_count, col_count):
    widened = jnp.pad(padded, ((0, 0), (0, 0), (1, 1), (0, 0), (0, 0)))
    out_shape = (widened.shape[0], row_count, col_count) + widened.shape[3:]
    depth_out = jnp.zeros(out_shape, jnp.float32) + depth_bias
    for tap_row in range(3):
        for tap_col in range(3):
            depth_out = (
                depth_out
                + depth_weight[tap_row, tap_col]
                * widened[:, tap_row : tap_row + row_count, tap_col : tap_col + col_count]
            )
    return depth_out


def on_device(
    latents,
    clip_height,
    clip_width,
    expand_weight,
    expand_bias,
    depth_weight,
    depth_bias,
    project_weight,
):
    batch_size, row_count, col_count, depth = latents.shape
    tokens = batch_size * row_count * col_count
    first_row = lax.axis_index("row") * row_count
    row_ids = first_row + jnp.arange(row_count, dtype=jnp.int32)
    col_ids = jnp.arange(col_count, dtype=jnp.int32)
    valid_mask = (
        (row_ids[None, :, None] < clip_height[:, None, None])
        & (col_ids[None, None, :] < clip_width[:, None, None])
    ).astype(jnp.float32)[..., None]
    channels = latents.reshape(tokens, depth).T
    gathered = lax.all_gather(channels, "tensor", axis=0, tiled=True)
    pre_act = jnp.einsum("dt,kdf->tkf", gathered, expand_weight, preferred_element_type=jnp.float32)
    pre_act = pre_act.reshape(batch_size, row_count, col_count, 2, -1)
    expanded = (jax.nn.silu(pre_act + expand_bias) * valid_mask[..., None]).astype(jnp.bfloat16)
    padded = halo_rows(expanded)
    depth_out = depthwise(padded, depth_weight, depth_bias, row_count, col_count)
    hidden = (depth_out[:, :, :, 0] * jax.nn.silu(depth_out[:, :, :, 1])).astype(jnp.bfloat16)
    partial_term = jnp.einsum(
        "tf,fd->dt", hidden.reshape(tokens, -1), project_weight, preferred_element_type=jnp.float32
    ).astype(jnp.bfloat16)
    summed = lax.psum_scatter(partial_term, "tensor", scatter_dimension=0, tiled=True)
    summed = summed.T.reshape(latents.shape).astype(jnp.float32)
    return (summed * valid_mask).astype(jnp.bfloat16)


def solution(mesh):
    in_specs = (
        P(None, "row", None, "tensor"),
        P(),
        P(),
        P(None, None, "tensor"),
        P(None, "tensor"),
        P(None, None, None, "tensor"),
        P(None, "tensor"),
        P("tensor", None),
    )
    out_specs = P(None, "row", None, "tensor")
    return jax.shard_map(
        on_device, mesh=mesh, in_specs=in_specs, out_specs=out_specs, check_vma=False
    )
```

```python
import jax
import jax.numpy as jnp
from jax import lax
from jax.sharding import PartitionSpec as P


def depthwise(padded, depth_weight, depth_bias, row_count, col_count):
    widened = jnp.pad(padded, ((0, 0), (0, 0), (1, 1), (0, 0), (0, 0)))
    out_shape = (widened.shape[0], row_count, col_count) + widened.shape[3:]
    depth_out = jnp.zeros(out_shape, jnp.float32) + depth_bias
    for tap_row in range(3):
        for tap_col in range(3):
            depth_out = (
                depth_out
                + depth_weight[tap_row, tap_col]
                * widened[:, tap_row : tap_row + row_count, tap_col : tap_col + col_count]
            )
    return depth_out


def on_device(
    latents,
    clip_height,
    clip_width,
    expand_weight,
    expand_bias,
    depth_weight,
    depth_bias,
    project_weight,
):
    batch_size, row_count, col_count, depth = latents.shape
    narrow = jnp.argmin(clip_width).astype(jnp.int32)
    order = [jnp.where(narrow <= s, s + 1, s) for s in range(batch_size - 1)] + [narrow]
    widths = [col_count] * (batch_size - 1) + [col_count // 2]
    half = batch_size // 2
    chunks = [list(range(half)), list(range(half, batch_size))]
    first_row = lax.axis_index("row") * row_count
    row_ids = first_row + jnp.arange(row_count, dtype=jnp.int32)
    col_ids = jnp.arange(col_count, dtype=jnp.int32)

    def masks_of(slots):
        return [
            (
                (row_ids[:, None] < clip_height[order[s]])
                & (col_ids[None, : widths[s]] < clip_width[order[s]])
            ).astype(jnp.float32)
            for s in slots
        ]

    gathered = []
    for slots in chunks:
        parts = [
            lax.dynamic_index_in_dim(latents, order[s], 0, keepdims=False)[:, : widths[s]].reshape(
                -1, depth
            )
            for s in slots
        ]
        channels = jnp.concatenate(parts, axis=0).T
        gathered.append(lax.all_gather(channels, "tensor", axis=0, tiled=True))
    out = jnp.zeros(latents.shape, jnp.bfloat16)
    for slots, full in zip(chunks, gathered):
        masks = masks_of(slots)
        flat_mask = jnp.concatenate([m.reshape(-1) for m in masks])
        pre_act = jnp.einsum("dt,kdf->tkf", full, expand_weight, preferred_element_type=jnp.float32)
        expanded = (jax.nn.silu(pre_act + expand_bias) * flat_mask[:, None, None]).astype(jnp.bfloat16)
        pieces, at = [], 0
        for s in slots:
            size = row_count * widths[s]
            pieces.append(expanded[at : at + size].reshape((row_count, widths[s]) + expanded.shape[1:]))
            at += size
        count = lax.axis_size("row")
        ends = count - 1
        head = jnp.concatenate([p[0] for p in pieces], axis=0)
        tail = jnp.concatenate([p[-1] for p in pieces], axis=0)
        above = lax.ppermute(tail, "row", [(i, i + 1) for i in range(ends)])
        below = lax.ppermute(head, "row", [(i + 1, i) for i in range(ends)])
        hidden, at = [], 0
        for s, piece in zip(slots, pieces):
            w = widths[s]
            padded = jnp.concatenate([above[None, at : at + w], piece, below[None, at : at + w]], axis=0)
            at += w
            depth_out = depthwise(padded[None], depth_weight, depth_bias, row_count, w)[0]
            gated = depth_out[:, :, 0] * jax.nn.silu(depth_out[:, :, 1])
            hidden.append(gated.astype(jnp.bfloat16).reshape(row_count * w, -1))
        partial_term = jnp.einsum(
            "tf,fd->dt", jnp.concatenate(hidden, axis=0), project_weight, preferred_element_type=jnp.float32
        ).astype(jnp.bfloat16)
        summed = lax.psum_scatter(partial_term, "tensor", scatter_dimension=0, tiled=True).T
        summed = (summed.astype(jnp.float32) * flat_mask[:, None]).astype(jnp.bfloat16)
        at = 0
        for s in slots:
            size = row_count * widths[s]
            block = summed[at : at + size].reshape(1, row_count, widths[s], depth)
            out = lax.dynamic_update_slice(out, block, (order[s], 0, 0, 0))
            at += size
    return out


def solution(mesh):
    in_specs = (
        P(None, "row", None, "tensor"),
        P(),
        P(),
        P(None, None, "tensor"),
        P(None, "tensor"),
        P(None, None, None, "tensor"),
        P(None, "tensor"),
        P("tensor", None),
    )
    out_specs = P(None, "row", None, "tensor")
    return jax.shard_map(
        on_device, mesh=mesh, in_specs=in_specs, out_specs=out_specs, check_vma=False
    )
```

```python
import functools

import jax
import jax.numpy as jnp
from jax import lax
from jax.experimental import pallas as pl
from jax.experimental.pallas import tpu as pltpu
from jax.sharding import PartitionSpec as P

LANES = 512
BLOCK = 256
GROUP = 16


def halo_rows(cells):
    count = lax.axis_size("row")
    ends = count - 1
    head = cells[:, :1]
    tail = cells[:, -1:]
    above = lax.ppermute(tail, "row", [(i, i + 1) for i in range(ends)])
    below = lax.ppermute(head, "row", [(i + 1, i) for i in range(ends)])
    return jnp.concatenate([above, cells, below], axis=1)


def depthwise(padded, depth_weight, depth_bias, row_count, col_count):
    widened = jnp.pad(padded, ((0, 0), (0, 0), (1, 1), (0, 0), (0, 0)))
    out_shape = (widened.shape[0], row_count, col_count) + widened.shape[3:]
    depth_out = jnp.zeros(out_shape, jnp.float32) + depth_bias
    for tap_row in range(3):
        for tap_col in range(3):
            depth_out = (
                depth_out
                + depth_weight[tap_row, tap_col]
                * widened[:, tap_row : tap_row + row_count, tap_col : tap_col + col_count]
            )
    return depth_out


def on_device_plain(
    latents,
    clip_height,
    clip_width,
    expand_weight,
    expand_bias,
    depth_weight,
    depth_bias,
    project_weight,
):
    batch_size, row_count, col_count, depth = latents.shape
    tokens = batch_size * row_count * col_count
    first_row = lax.axis_index("row") * row_count
    row_ids = first_row + jnp.arange(row_count, dtype=jnp.int32)
    col_ids = jnp.arange(col_count, dtype=jnp.int32)
    valid_mask = (
        (row_ids[None, :, None] < clip_height[:, None, None])
        & (col_ids[None, None, :] < clip_width[:, None, None])
    ).astype(jnp.float32)[..., None]
    channels = latents.reshape(tokens, depth).T
    gathered = lax.all_gather(channels, "tensor", axis=0, tiled=True)
    pre_act = jnp.einsum("dt,kdf->tkf", gathered, expand_weight, preferred_element_type=jnp.float32)
    pre_act = pre_act.reshape(batch_size, row_count, col_count, 2, -1)
    expanded = (jax.nn.silu(pre_act + expand_bias) * valid_mask[..., None]).astype(jnp.bfloat16)
    padded = halo_rows(expanded)
    depth_out = depthwise(padded, depth_weight, depth_bias, row_count, col_count)
    hidden = (depth_out[:, :, :, 0] * jax.nn.silu(depth_out[:, :, :, 1])).astype(jnp.bfloat16)
    partial_term = jnp.einsum(
        "tf,fd->dt", hidden.reshape(tokens, -1), project_weight, preferred_element_type=jnp.float32
    ).astype(jnp.bfloat16)
    summed = lax.psum_scatter(partial_term, "tensor", scatter_dimension=0, tiled=True)
    summed = summed.T.reshape(latents.shape).astype(jnp.float32)
    return (summed * valid_mask).astype(jnp.bfloat16)


def slot_clips(width_ref, batch_size):
    narrow, least = jnp.int32(0), width_ref[0]
    for b in range(1, batch_size):
        closer = width_ref[b] < least
        narrow = jnp.where(closer, b, narrow)
        least = jnp.where(closer, width_ref[b], least)
    return [jnp.where(narrow <= s, s + 1, s) for s in range(batch_size - 1)] + [narrow]


def slot_widths(batch_size, col_count):
    return [col_count] * (batch_size - 1) + [col_count // 2]


def slot_starts(widths):
    return [sum(widths[:s]) for s in range(len(widths))]


def row_of(place, parity):
    return jnp.where(parity == 0, (-1, 0, 1, 2)[place], (2, 1, 0, -1)[place])


def mask_column(height_ref, width_ref, row_id, widths):
    pieces = []
    for clip, width in zip(slot_clips(width_ref, len(widths)), widths):
        bound = jnp.where((row_id >= 0) & (row_id < height_ref[clip]), width_ref[clip], 0)
        col = lax.broadcasted_iota(jnp.int32, (width, 128), 0)
        pieces.append((col < bound).astype(jnp.float32))
    return jnp.concatenate(pieces, axis=0)


def rest_places(rest):
    return [(g // 2 * GROUP, g % 2 * BLOCK) for g in range(rest // GROUP)]


def pack_kernel(width_ref, x_ref, out_ref, *, widths):
    batch_size, _, _, depth = x_ref.shape
    kept, rest = sum(widths), depth - LANES
    parity = lax.rem(lax.axis_index("row"), 2)
    clips = slot_clips(width_ref, batch_size)
    for place in range(2):
        row = jnp.where(parity == 0, 1 - place, place)
        tails = []
        for clip, width, at in zip(clips, widths, slot_starts(widths)):
            out_ref[place, at : at + width, :] = x_ref[clip, row, :width, :LANES]
            tails.append(x_ref[clip, row, :width, LANES:].astype(jnp.float32))
        tails.append(jnp.zeros((BLOCK - kept, rest), jnp.float32))
        turned = jnp.concatenate(tails, axis=0).T.astype(jnp.bfloat16)
        out_ref[place, kept:, :] = jnp.zeros((out_ref.shape[1] - kept, LANES), jnp.bfloat16)
        for g, (down, over) in enumerate(rest_places(rest)):
            out_ref[place, kept + down : kept + down + GROUP, over : over + BLOCK] = turned[
                g * GROUP : (g + 1) * GROUP
            ]


def silu(v):
    h = 0.5 * v
    return h + h * jnp.tanh(h)


def fused_kernel(
    height_ref, width_ref, *refs, widths, shards, depth, hidden_count
):
    own_refs, inner_refs, outer_refs = refs[:shards], refs[shards : 2 * shards], refs[2 * shards : 3 * shards]
    w_ref, eb_ref, dw_ref, db_ref, p_ref, out_ref, x_scr, m_scr, e_scr, acc_scr = refs[3 * shards :]
    kept, rest = sum(widths), depth - LANES
    step, steps = pl.program_id(0), pl.num_programs(0)
    me = lax.axis_index("tensor")
    row_index = lax.axis_index("row")
    parity = lax.rem(row_index, 2)
    tile = w_ref.shape[2]

    @pl.when(step == 0)
    def _():
        for place in range(4):
            tails = []
            lines = slice(place * kept, (place + 1) * kept)
            for j in range(shards):
                packet = (
                    outer_refs[j].at[0],
                    own_refs[j].at[1],
                    own_refs[j].at[0],
                    inner_refs[j].at[0],
                )[place]
                x_scr[lines, j * LANES : (j + 1) * LANES] = packet[:kept, :]
                for down, over in rest_places(rest):
                    tails.append(packet[kept + down : kept + down + GROUP, over : over + BLOCK])
            turned = jnp.concatenate(tails, axis=0).astype(jnp.float32).T
            x_scr[lines, shards * LANES :] = turned[:kept].astype(jnp.bfloat16)
            row_id = row_index * 2 + row_of(place, parity)
            m_scr[lines, :] = mask_column(height_ref, width_ref, row_id, widths)
        acc_scr[...] = jnp.zeros_like(acc_scr)

    mask = jnp.concatenate([m_scr[...]] * (tile // 128), axis=1)
    for k in range(2):
        pre_act = None
        rest_rows = []
        for j in range(shards):
            base = pl.multiple_of(lax.bitwise_xor(me, j) * depth, GROUP)
            term = jnp.dot(
                x_scr[:, j * LANES : (j + 1) * LANES],
                w_ref[k, pl.ds(base, LANES), :],
                preferred_element_type=jnp.float32,
            )
            pre_act = term if pre_act is None else pre_act + term
            rest_rows.append(w_ref[k, pl.ds(pl.multiple_of(base + LANES, GROUP), rest), :])
        pre_act = pre_act + jnp.dot(
            x_scr[:, shards * LANES :],
            jnp.concatenate(rest_rows, axis=0),
            preferred_element_type=jnp.float32,
        )
        e_scr[k] = silu(pre_act + eb_ref[k : k + 1, :]) * mask

    line = lax.broadcasted_iota(jnp.int32, (kept, tile), 0)
    not_first, not_last = None, None
    for at, width in zip(slot_starts(widths), widths):
        first, last = line != at, line != at + width - 1
        not_first = first if not_first is None else not_first & first
        not_last = last if not_last is None else not_last & last
    for place in (1, 2):
        halves = []
        for k in range(2):
            sums = []
            for tap_col in range(3):
                total = None
                for i in range(3):
                    tap_row = jnp.where(parity == 0, i, 2 - i)
                    cells = e_scr[k, (place + i - 1) * kept : (place + i) * kept, :]
                    term = dw_ref[tap_row, tap_col, k : k + 1, :] * cells
                    total = term if total is None else total + term
                sums.append(total)
            left = jnp.where(not_first, pltpu.roll(sums[0], 1, 0), 0.0)
            right = jnp.where(not_last, pltpu.roll(sums[2], kept - 1, 0), 0.0)
            halves.append(sums[1] + left + right + db_ref[k : k + 1, :])
        hidden = halves[0] * silu(halves[1])
        valid = hidden_count - step * tile
        unit = lax.broadcasted_iota(jnp.int32, hidden.shape, 1)
        hidden = jnp.where(unit < valid, hidden, 0.0).astype(jnp.bfloat16)
        weight = p_ref[...]
        unit = lax.broadcasted_iota(jnp.int32, weight.shape, 0)
        weight = jnp.where(unit < valid, weight, jnp.zeros_like(weight))
        lines = slice((2 - place) * kept, (3 - place) * kept)
        acc_scr[lines, :] += jnp.dot(hidden, weight, preferred_element_type=jnp.float32)

    @pl.when(step == steps - 1)
    def _():
        for place in range(2):
            lines = slice(place * kept, (place + 1) * kept)
            for s in range(shards):
                sums = acc_scr[lines, s * depth : (s + 1) * depth]
                out_ref[s, place, :kept, :] = sums[:, :LANES].astype(jnp.bfloat16)
                tail = jnp.concatenate(
                    [sums[:, LANES:], jnp.zeros((BLOCK - kept, rest), jnp.float32)], axis=0
                )
                turned = tail.T.astype(jnp.bfloat16)
                out_ref[s, place, kept:, :] = jnp.zeros((out_ref.shape[2] - kept, LANES), jnp.bfloat16)
                for g, (down, over) in enumerate(rest_places(rest)):
                    out_ref[s, place, kept + down : kept + down + GROUP, over : over + BLOCK] = turned[
                        g * GROUP : (g + 1) * GROUP
                    ]


def unpack_kernel(height_ref, width_ref, sum_ref, out_ref, *, widths):
    batch_size, _, col_count, depth = out_ref.shape
    kept, rest = sum(widths), depth - LANES
    row_index = lax.axis_index("row")
    parity = lax.rem(row_index, 2)
    clips = slot_clips(width_ref, batch_size)
    for place in range(2):
        row = jnp.where(parity == 0, 1 - place, place)
        mask = mask_column(height_ref, width_ref, row_index * 2 + row, widths)
        parts = [
            sum_ref[place, kept + down : kept + down + GROUP, over : over + BLOCK]
            for down, over in rest_places(rest)
        ]
        tails = jnp.concatenate(parts, axis=0).astype(jnp.float32).T
        mains = sum_ref[place, :kept, :].astype(jnp.float32)
        wide_mask = jnp.concatenate([mask] * (LANES // 128), axis=1) > 0
        mains = jnp.where(wide_mask, mains, 0.0).astype(jnp.bfloat16)
        tails = jnp.where(mask[:, :rest] > 0, tails[:kept], 0.0).astype(jnp.bfloat16)
        for clip, width, at in zip(clips, widths, slot_starts(widths)):
            out_ref[clip, row, :width, :LANES] = mains[at : at + width]
            out_ref[clip, row, :width, LANES:] = tails[at : at + width]
            if width < col_count:
                out_ref[clip, row, width:, :] = jnp.zeros((col_count - width, depth), jnp.bfloat16)


VMEM = pl.BlockSpec(memory_space=pltpu.VMEM)


def on_device_packed(
    latents,
    clip_height,
    clip_width,
    expand_weight,
    expand_bias,
    depth_weight,
    depth_bias,
    project_weight,
):
    batch_size, row_count, col_count, depth = latents.shape
    shards, row_devices = lax.axis_size("tensor"), lax.axis_size("row")
    hidden_count = expand_weight.shape[2]
    widths = slot_widths(batch_size, col_count)
    kept, rest = sum(widths), depth - LANES
    lines = kept + -(-rest // (2 * GROUP)) * GROUP
    own = pl.pallas_call(
        functools.partial(pack_kernel, widths=widths),
        out_shape=jax.ShapeDtypeStruct((row_count, lines, LANES), jnp.bfloat16),
        grid_spec=pltpu.PrefetchScalarGridSpec(
            num_scalar_prefetch=1, grid=(), in_specs=[VMEM], out_specs=VMEM
        ),
        name="pack",
    )(clip_width, latents)

    packets = [own]
    for j in range(1, shards):
        packets.append(lax.ppermute(own, "tensor", [(i, i ^ j) for i in range(shards)]))
    sibling = [(i, i ^ 1) for i in range(row_devices)]
    beyond = [(i, i + 1) for i in range(1, row_devices - 1, 2)]
    beyond = beyond + [(b, a) for a, b in beyond]
    inner = [lax.ppermute(p[:1], "row", sibling) for p in packets]
    outer = [lax.ppermute(p[1:], "row", beyond) for p in packets]

    tile = 256
    steps = -(-hidden_count // tile)
    whole = lambda shape: pl.BlockSpec(shape, lambda f, *_: (0,) * len(shape))
    partial_sums = pl.pallas_call(
        functools.partial(
            fused_kernel, widths=widths, shards=shards, depth=depth, hidden_count=hidden_count
        ),
        out_shape=jax.ShapeDtypeStruct((shards, row_count, lines, LANES), jnp.bfloat16),
        grid_spec=pltpu.PrefetchScalarGridSpec(
            num_scalar_prefetch=2,
            grid=(steps,),
            in_specs=[whole(own.shape)] * shards
            + [whole((1, lines, LANES))] * (2 * shards)
            + [
                pl.BlockSpec((2, shards * depth, tile), lambda f, *_: (0, 0, f)),
                pl.BlockSpec((2, tile), lambda f, *_: (0, f)),
                pl.BlockSpec((3, 3, 2, tile), lambda f, *_: (0, 0, 0, f)),
                pl.BlockSpec((2, tile), lambda f, *_: (0, f)),
                pl.BlockSpec((tile, shards * depth), lambda f, *_: (f, 0)),
            ],
            out_specs=whole((shards, row_count, lines, LANES)),
            scratch_shapes=[
                pltpu.VMEM((4 * kept, shards * depth), jnp.bfloat16),
                pltpu.VMEM((4 * kept, 128), jnp.float32),
                pltpu.VMEM((2, 4 * kept, tile), jnp.float32),
                pltpu.VMEM((2 * kept, shards * depth), jnp.float32),
            ],
        ),
        compiler_params=pltpu.CompilerParams(vmem_limit_bytes=48 * 1024 * 1024),
        name="expand_conv_project",
    )(
        clip_height,
        clip_width,
        *packets,
        *inner,
        *outer,
        expand_weight,
        expand_bias,
        depth_weight,
        depth_bias,
        project_weight,
    )
    flat = partial_sums.reshape(shards, row_count * lines, LANES)
    summed = lax.psum_scatter(flat, "tensor", scatter_dimension=0, tiled=False)
    return pl.pallas_call(
        functools.partial(unpack_kernel, widths=widths),
        out_shape=jax.ShapeDtypeStruct(latents.shape, jnp.bfloat16),
        grid_spec=pltpu.PrefetchScalarGridSpec(
            num_scalar_prefetch=2, grid=(), in_specs=[VMEM], out_specs=VMEM
        ),
        name="unpack",
    )(clip_height, clip_width, summed.reshape(row_count, lines, LANES))


def on_device(latents, clip_height, clip_width, expand_weight, *rest_of):
    batch_size, row_count, col_count, depth = latents.shape
    kept = sum(slot_widths(batch_size, col_count))
    fits = (
        row_count == 2
        and lax.axis_size("row") % 2 == 0
        and lax.axis_size("tensor") == 4
        and depth > LANES
        and (depth - LANES) % GROUP == 0
        and depth % GROUP == 0
        and kept <= BLOCK
        and kept % GROUP == 0
    )
    run = on_device_packed if fits else on_device_plain
    return run(latents, clip_height, clip_width, expand_weight, *rest_of)


def solution(mesh):
    in_specs = (
        P(None, "row", None, "tensor"),
        P(),
        P(),
        P(None, None, "tensor"),
        P(None, "tensor"),
        P(None, None, None, "tensor"),
        P(None, "tensor"),
        P("tensor", None),
    )
    out_specs = P(None, "row", None, "tensor")
    return jax.shard_map(
        on_device, mesh=mesh, in_specs=in_specs, out_specs=out_specs, check_vma=False
    )
```

```python
import functools

import jax
import jax.numpy as jnp
from jax import lax
from jax.experimental import pallas as pl
from jax.experimental.pallas import tpu as pltpu
from jax.sharding import PartitionSpec as P

LANES = 512
GROUP = 16
TILE = 256


def halo_rows(cells):
    count = lax.axis_size("row")
    ends = count - 1
    head = cells[:, :1]
    tail = cells[:, -1:]
    above = lax.ppermute(tail, "row", [(i, i + 1) for i in range(ends)])
    below = lax.ppermute(head, "row", [(i + 1, i) for i in range(ends)])
    return jnp.concatenate([above, cells, below], axis=1)


def depthwise(padded, depth_weight, depth_bias, row_count, col_count):
    widened = jnp.pad(padded, ((0, 0), (0, 0), (1, 1), (0, 0), (0, 0)))
    out_shape = (widened.shape[0], row_count, col_count) + widened.shape[3:]
    depth_out = jnp.zeros(out_shape, jnp.float32) + depth_bias
    for tap_row in range(3):
        for tap_col in range(3):
            depth_out = (
                depth_out
                + depth_weight[tap_row, tap_col]
                * widened[:, tap_row : tap_row + row_count, tap_col : tap_col + col_count]
            )
    return depth_out


def on_device_plain(
    latents,
    clip_height,
    clip_width,
    expand_weight,
    expand_bias,
    depth_weight,
    depth_bias,
    project_weight,
):
    batch_size, row_count, col_count, depth = latents.shape
    tokens = batch_size * row_count * col_count
    first_row = lax.axis_index("row") * row_count
    row_ids = first_row + jnp.arange(row_count, dtype=jnp.int32)
    col_ids = jnp.arange(col_count, dtype=jnp.int32)
    valid_mask = (
        (row_ids[None, :, None] < clip_height[:, None, None])
        & (col_ids[None, None, :] < clip_width[:, None, None])
    ).astype(jnp.float32)[..., None]
    channels = latents.reshape(tokens, depth).T
    gathered = lax.all_gather(channels, "tensor", axis=0, tiled=True)
    pre_act = jnp.einsum("dt,kdf->tkf", gathered, expand_weight, preferred_element_type=jnp.float32)
    pre_act = pre_act.reshape(batch_size, row_count, col_count, 2, -1)
    expanded = (jax.nn.silu(pre_act + expand_bias) * valid_mask[..., None]).astype(jnp.bfloat16)
    padded = halo_rows(expanded)
    depth_out = depthwise(padded, depth_weight, depth_bias, row_count, col_count)
    hidden = (depth_out[:, :, :, 0] * jax.nn.silu(depth_out[:, :, :, 1])).astype(jnp.bfloat16)
    partial_term = jnp.einsum(
        "tf,fd->dt", hidden.reshape(tokens, -1), project_weight, preferred_element_type=jnp.float32
    ).astype(jnp.bfloat16)
    summed = lax.psum_scatter(partial_term, "tensor", scatter_dimension=0, tiled=True)
    summed = summed.T.reshape(latents.shape).astype(jnp.float32)
    return (summed * valid_mask).astype(jnp.bfloat16)


def slot_clips(width_ref, batch_size):
    narrow, least = jnp.int32(0), width_ref[0]
    for b in range(1, batch_size):
        closer = width_ref[b] < least
        narrow = jnp.where(closer, b, narrow)
        least = jnp.where(closer, width_ref[b], least)
    return [jnp.where(narrow <= s, s + 1, s) for s in range(batch_size - 1)] + [narrow]


def slot_widths(batch_size, col_count):
    return [col_count] * (batch_size - 1) + [col_count // 2]


class Chunk:
    def __init__(self, slots, widths, depth):
        self.slots = slots
        self.widths = [widths[s] for s in slots]
        self.starts = [sum(self.widths[:i]) for i in range(len(slots))]
        self.kept = sum(self.widths)
        self.block = -(-self.kept // 128) * 128
        self.depth, self.rest = depth, depth - LANES
        across = LANES // self.block
        groups = self.rest // GROUP
        self.places = [(g // across * GROUP, g % across * self.block) for g in range(groups)]
        self.lines = self.kept + -(-groups // across) * GROUP
        self.tokens = 2 * self.kept
        self.full, self.left = self.tokens // 128, self.tokens % 128
        self.upper = -(-depth // (2 * GROUP)) * GROUP
        self.unit = (self.full * depth + (self.upper if self.left else 0), 128)

    def clips(self, width_ref, batch_size):
        order = slot_clips(width_ref, batch_size)
        return [order[s] for s in self.slots]

    def mask_column(self, height_ref, width_ref, row_id):
        pieces = []
        clips = self.clips(width_ref, width_ref.shape[0])
        for clip, width in zip(clips, self.widths):
            bound = jnp.where((row_id >= 0) & (row_id < height_ref[clip]), width_ref[clip], 0)
            col = lax.broadcasted_iota(jnp.int32, (width, 128), 0)
            pieces.append((col < bound).astype(jnp.float32))
        return jnp.concatenate(pieces, axis=0)

    def put_unit(self, unit_ref, sums):
        depth, at = self.depth, self.full * self.depth
        for b in range(self.full):
            unit_ref[b * depth : (b + 1) * depth, :] = sums[:, b * 128 : (b + 1) * 128]
        if self.left:
            tail = sums[:, self.full * 128 :]
            lower = depth - self.upper
            unit_ref[at : at + self.upper, : self.left] = tail[: self.upper]
            unit_ref[at : at + lower, self.left :] = tail[self.upper :]
            if lower < self.upper:
                unit_ref[at + lower :, self.left :] = jnp.zeros(
                    (self.upper - lower, 128 - self.left), sums.dtype
                )

    def get_unit(self, unit):
        depth, at = self.depth, self.full * self.depth
        blocks = [unit[b * depth : (b + 1) * depth, :] for b in range(self.full)]
        if self.left:
            lower = depth - self.upper
            blocks.append(
                jnp.concatenate(
                    [unit[at : at + self.upper, : self.left], unit[at : at + lower, self.left :]], axis=0
                )
            )
        return jnp.concatenate(blocks, axis=1)


def parity_of():
    return lax.rem(lax.axis_index("row"), 2)


def row_of(place, parity):
    return jnp.where(parity == 0, (-1, 0, 1, 2)[place], (2, 1, 0, -1)[place])


def silu(v):
    h = 0.5 * v
    return h + h * jnp.tanh(h)


def pack_kernel(width_ref, x_ref, *out_refs, chunks):
    parity = parity_of()
    for chunk, out_ref in zip(chunks, out_refs):
        for place in range(2):
            row = jnp.where(parity == 0, 1 - place, place)
            tails = []
            for clip, width, at in zip(
                chunk.clips(width_ref, x_ref.shape[0]), chunk.widths, chunk.starts
            ):
                out_ref[place, at : at + width, :] = x_ref[clip, row, :width, :LANES]
                tails.append(x_ref[clip, row, :width, LANES:].astype(jnp.float32))
            if chunk.block > chunk.kept:
                tails.append(jnp.zeros((chunk.block - chunk.kept, chunk.rest), jnp.float32))
            turned = jnp.concatenate(tails, axis=0).T.astype(jnp.bfloat16)
            kept = chunk.kept
            out_ref[place, kept:, :] = jnp.zeros((chunk.lines - kept, LANES), jnp.bfloat16)
            for g, (down, over) in enumerate(chunk.places):
                out_ref[place, kept + down : kept + down + GROUP, over : over + chunk.block] = turned[
                    g * GROUP : (g + 1) * GROUP
                ]


def hidden_kernel(height_ref, width_ref, *refs, chunk, shards, groups, count):
    own_refs = refs[:shards]
    inner_refs = refs[shards : shards + count]
    outer_refs = refs[shards + count : shards + 2 * count]
    w_ref, eb_ref, dw_ref, db_ref, out_ref, x_scr, m_scr, e_scr = refs[shards + 2 * count :]
    kept, rest, depth = chunk.kept, chunk.rest, chunk.depth
    me = lax.axis_index("tensor")
    parity = parity_of()
    subs = w_ref.shape[2] // TILE

    @pl.when(pl.program_id(0) == 0)
    def _():
        spots = {j: (g, i) for g, js in enumerate(groups) for i, j in enumerate(js)}
        for place in range(4):
            tails = []
            lines = slice(place * kept, (place + 1) * kept)
            for j in range(shards):
                g, i = spots[j]
                packet = (
                    outer_refs[g].at[i],
                    own_refs[j].at[1],
                    own_refs[j].at[0],
                    inner_refs[g].at[i],
                )[place]
                x_scr[lines, j * LANES : (j + 1) * LANES] = packet[:kept, :]
                for down, over in chunk.places:
                    tails.append(packet[kept + down : kept + down + GROUP, over : over + chunk.block])
            turned = jnp.concatenate(tails, axis=0).astype(jnp.float32).T
            x_scr[lines, shards * LANES :] = turned[:kept].astype(jnp.bfloat16)
            row_id = lax.axis_index("row") * 2 + row_of(place, parity)
            m_scr[lines, :] = chunk.mask_column(height_ref, width_ref, row_id)

    bases = [pl.multiple_of(lax.bitwise_xor(me, j) * depth, GROUP) for j in range(shards)]
    for sub in range(subs):
        units = slice(sub * TILE, (sub + 1) * TILE)
        for k in range(2):
            weight = jnp.concatenate(
                [w_ref[k, pl.ds(base, LANES), units] for base in bases]
                + [w_ref[k, pl.ds(pl.multiple_of(base + LANES, GROUP), rest), units] for base in bases],
                axis=0,
            )
            pre_act = jnp.dot(x_scr[...], weight, preferred_element_type=jnp.float32)
            mask = jnp.concatenate([m_scr[...]] * (TILE // 128), axis=1)
            e_scr[sub, k] = silu(pre_act + eb_ref[k : k + 1, units]) * mask

    line = lax.broadcasted_iota(jnp.int32, (kept, TILE), 0)
    not_first, not_last = None, None
    for at, width in zip(chunk.starts, chunk.widths):
        first, last = line != at, line != at + width - 1
        not_first = first if not_first is None else not_first & first
        not_last = last if not_last is None else not_last & last
    for sub in range(subs):
        units = slice(sub * TILE, (sub + 1) * TILE)
        for place in (1, 2):
            halves = []
            for k in range(2):
                sums = []
                for tap_col in range(3):
                    total = None
                    for i in range(3):
                        tap_row = jnp.where(parity == 0, i, 2 - i)
                        cells = e_scr[sub, k, (place + i - 1) * kept : (place + i) * kept, :]
                        term = dw_ref[tap_row, tap_col, k : k + 1, units] * cells
                        total = term if total is None else total + term
                    sums.append(total)
                left = jnp.where(not_first, pltpu.roll(sums[0], 1, 0), 0.0)
                right = jnp.where(not_last, pltpu.roll(sums[2], kept - 1, 0), 0.0)
                halves.append(sums[1] + left + right + db_ref[k : k + 1, units])
            hidden = halves[0] * silu(halves[1])
            out_ref[(2 - place) * kept : (3 - place) * kept, units] = hidden.astype(jnp.bfloat16)


def project(weight_ref, hidden_ref):
    return lax.dot_general(
        weight_ref[...],
        hidden_ref[...],
        (((1,), (1,)), ((), ())),
        preferred_element_type=jnp.float32,
    )


def unit_kernel(place_ref, weight_ref, hidden_ref, *refs, chunk):
    out_ref = refs[-1]
    sums = project(weight_ref, hidden_ref)
    for ref in refs[:-1]:
        sums = sums + chunk.get_unit(ref[...].astype(jnp.float32))
    chunk.put_unit(out_ref, sums.astype(jnp.bfloat16))


def final_kernel(place_ref, height_ref, width_ref, weight_ref, hidden_ref, *refs, chunk, sources):
    out_ref = refs[-1]
    if len(refs) > sources + 1:
        out_ref[...] = refs[sources][...]
    sums = project(weight_ref, hidden_ref)
    for ref in refs[:sources]:
        sums = sums + chunk.get_unit(ref[...].astype(jnp.float32))
    cells = sums.T
    parity = parity_of()
    for place in range(2):
        row = jnp.where(parity == 0, 1 - place, place)
        row_id = lax.axis_index("row") * 2 + row
        mask = chunk.mask_column(height_ref, width_ref, row_id)[:, :1] > 0
        part = cells[place * chunk.kept : (place + 1) * chunk.kept]
        part = jnp.where(mask, part, 0.0).astype(jnp.bfloat16)
        clips = chunk.clips(width_ref, width_ref.shape[0])
        for clip, width, at in zip(clips, chunk.widths, chunk.starts):
            out_ref[clip, row, :width, :] = part[at : at + width]
            if width < out_ref.shape[2]:
                blank = jnp.zeros((out_ref.shape[2] - width, chunk.depth), jnp.bfloat16)
                out_ref[clip, row, width:, :] = blank


VMEM = pl.BlockSpec(memory_space=pltpu.VMEM)
MIB = 1024 * 1024


def after(value, *others):
    return lax.optimization_barrier((value,) + others)[0]


def on_device_packed(
    latents,
    clip_height,
    clip_width,
    expand_weight,
    expand_bias,
    depth_weight,
    depth_bias,
    project_weight,
):
    batch_size, row_count, col_count, depth = latents.shape
    shards, row_devices = lax.axis_size("tensor"), lax.axis_size("row")
    hidden_count = expand_weight.shape[2]
    full_depth = shards * depth
    chunks = chunks_of(batch_size, col_count, depth)
    own = pl.pallas_call(
        functools.partial(pack_kernel, chunks=chunks),
        out_shape=[jax.ShapeDtypeStruct((2, c.lines, LANES), jnp.bfloat16) for c in chunks],
        grid_spec=pltpu.PrefetchScalarGridSpec(
            num_scalar_prefetch=1, grid=(), in_specs=[VMEM], out_specs=[VMEM] * len(chunks)
        ),
        name="pack",
    )(clip_width, latents)
    me = lax.axis_index("tensor").astype(jnp.int32).reshape(1)
    project_turned = project_weight.T

    sibling = [(i, i ^ 1) for i in range(row_devices)]
    beyond = [(i, i + 1) for i in range(1, row_devices - 1, 2)]
    beyond = beyond + [(b, a) for a, b in beyond]
    near = [(i, i ^ 1) for i in range(4)]
    two_off = [(i, i ^ 2) for i in range(4)]
    middle = [(1, 2), (2, 1)]
    to_end = [(2, 3), (1, 0)]
    from_end = [(0, 1), (3, 2)]
    groups = ((0,), (1, 2), (3,))

    gathered, previous = [], None
    for chunk, mine in zip(chunks, own):
        if previous is not None:
            mine = after(mine, previous)
        second = lax.ppermute(mine, "tensor", two_off)
        first = lax.ppermute(mine, "tensor", near)
        across = lax.ppermute(after(mine, second), "tensor", middle)
        passed = lax.ppermute(second, "tensor", to_end)
        third = across + passed
        previous = second
        packets = [mine, first, second, third]
        inner, outer = [], []
        for js in groups:
            inner.append(
                lax.ppermute(jnp.concatenate([packets[j][:1] for j in js], axis=0), "row", sibling)
            )
            outer.append(
                lax.ppermute(jnp.concatenate([packets[j][1:] for j in js], axis=0), "row", beyond)
            )
        gathered.append((packets, inner, outer))

    out = None
    for chunk, (packets, inner, outer) in zip(chunks, gathered):
        wide = 2 * TILE
        whole = lambda shape: pl.BlockSpec(shape, lambda f, *_: (0,) * len(shape))
        lines = 4 * chunk.kept
        hidden = pl.pallas_call(
            functools.partial(
                hidden_kernel, chunk=chunk, shards=shards, groups=groups, count=len(groups)
            ),
            out_shape=jax.ShapeDtypeStruct((chunk.tokens, hidden_count), jnp.bfloat16),
            grid_spec=pltpu.PrefetchScalarGridSpec(
                num_scalar_prefetch=2,
                grid=(-(-hidden_count // wide),),
                in_specs=[whole(p.shape) for p in packets + inner + outer]
                + [
                    pl.BlockSpec((2, full_depth, wide), lambda f, *_: (0, 0, f)),
                    pl.BlockSpec((2, wide), lambda f, *_: (0, f)),
                    pl.BlockSpec((3, 3, 2, wide), lambda f, *_: (0, 0, 0, f)),
                    pl.BlockSpec((2, wide), lambda f, *_: (0, f)),
                ],
                out_specs=pl.BlockSpec((chunk.tokens, wide), lambda f, *_: (0, f)),
                scratch_shapes=[
                    pltpu.VMEM((lines, full_depth), jnp.bfloat16),
                    pltpu.VMEM((lines, 128), jnp.float32),
                    pltpu.VMEM((2, 2, lines, TILE), jnp.float32),
                ],
            ),
            compiler_params=pltpu.CompilerParams(vmem_limit_bytes=40 * MIB),
            cost_estimate=pl.CostEstimate(
                flops=4 * lines * full_depth * hidden_count,
                bytes_accessed=4 * full_depth * hidden_count,
                transcendentals=3 * lines * hidden_count,
            ),
            name="expand_conv",
        )(
            clip_height,
            clip_width,
            *packets,
            *inner,
            *outer,
            expand_weight,
            expand_bias,
            depth_weight,
            depth_bias,
        )

        weight_of = lambda j: pl.BlockSpec(
            (depth, hidden_count), lambda f, place, *_: (lax.bitwise_xor(place[0], j), 0)
        )
        cost = pl.CostEstimate(
            flops=2 * chunk.tokens * depth * hidden_count,
            bytes_accessed=2 * depth * hidden_count + 2 * chunk.tokens * hidden_count,
            transcendentals=0,
        )

        def unit(j, *added):
            return pl.pallas_call(
                functools.partial(unit_kernel, chunk=chunk),
                out_shape=jax.ShapeDtypeStruct(chunk.unit, jnp.bfloat16),
                grid_spec=pltpu.PrefetchScalarGridSpec(
                    num_scalar_prefetch=1,
                    grid=(1,),
                    in_specs=[weight_of(j), whole(hidden.shape)] + [whole(chunk.unit)] * len(added),
                    out_specs=whole(chunk.unit),
                ),
                compiler_params=pltpu.CompilerParams(vmem_limit_bytes=24 * MIB),
                cost_estimate=cost,
                name=f"project_{j}",
            )(me, project_turned, hidden, *added)

        far = unit(3)
        relayed = lax.ppermute(far, "tensor", from_end)
        arrived = [lax.ppermute(far, "tensor", middle)]
        close = unit(1)
        arrived.append(lax.ppermute(unit(2, relayed), "tensor", two_off))
        arrived.append(lax.ppermute(after(close, relayed), "tensor", near))
        extra = [] if out is None else [out]
        out = pl.pallas_call(
            functools.partial(final_kernel, chunk=chunk, sources=len(arrived)),
            out_shape=jax.ShapeDtypeStruct(latents.shape, jnp.bfloat16),
            grid_spec=pltpu.PrefetchScalarGridSpec(
                num_scalar_prefetch=3,
                grid=(1,),
                in_specs=[weight_of(0), whole(hidden.shape)]
                + [whole(chunk.unit)] * len(arrived)
                + [whole(latents.shape)] * len(extra),
                out_specs=whole(latents.shape),
            ),
            compiler_params=pltpu.CompilerParams(vmem_limit_bytes=24 * MIB),
            cost_estimate=cost,
            name="finish",
        )(me, clip_height, clip_width, project_turned, hidden, *arrived, *extra)
    return out


def chunks_of(batch_size, col_count, depth):
    widths = slot_widths(batch_size, col_count)
    half = batch_size // 2
    return [Chunk(slots, widths, depth) for slots in (list(range(half)), list(range(half, batch_size)))]


def on_device(latents, clip_height, clip_width, expand_weight, *rest_of):
    batch_size, row_count, col_count, depth = latents.shape
    fits = (
        batch_size >= 2
        and row_count == 2
        and lax.axis_size("row") % 2 == 0
        and lax.axis_size("tensor") == 4
        and depth > LANES
        and (depth - LANES) % GROUP == 0
        and depth % GROUP == 0
        and all(
            c.block in (128, 256, 512) and c.kept % GROUP == 0 and c.left in (0, 64)
            for c in chunks_of(batch_size, col_count, depth)
        )
    )
    run = on_device_packed if fits else on_device_plain
    return run(latents, clip_height, clip_width, expand_weight, *rest_of)


def solution(mesh):
    in_specs = (
        P(None, "row", None, "tensor"),
        P(),
        P(),
        P(None, None, "tensor"),
        P(None, "tensor"),
        P(None, None, None, "tensor"),
        P(None, "tensor"),
        P("tensor", None),
    )
    out_specs = P(None, "row", None, "tensor")
    return jax.shard_map(
        on_device, mesh=mesh, in_specs=in_specs, out_specs=out_specs, check_vma=False
    )
```

```python
import functools

import jax
import jax.numpy as jnp
from jax import lax
from jax.experimental import pallas as pl
from jax.experimental.pallas import tpu as pltpu
from jax.sharding import PartitionSpec as P

LANES = 512
GROUP = 16
TILE = 256


def halo_rows(cells):
    count = lax.axis_size("row")
    ends = count - 1
    head = cells[:, :1]
    tail = cells[:, -1:]
    above = lax.ppermute(tail, "row", [(i, i + 1) for i in range(ends)])
    below = lax.ppermute(head, "row", [(i + 1, i) for i in range(ends)])
    return jnp.concatenate([above, cells, below], axis=1)


def depthwise(padded, depth_weight, depth_bias, row_count, col_count):
    widened = jnp.pad(padded, ((0, 0), (0, 0), (1, 1), (0, 0), (0, 0)))
    out_shape = (widened.shape[0], row_count, col_count) + widened.shape[3:]
    depth_out = jnp.zeros(out_shape, jnp.float32) + depth_bias
    for tap_row in range(3):
        for tap_col in range(3):
            depth_out = (
                depth_out
                + depth_weight[tap_row, tap_col]
                * widened[:, tap_row : tap_row + row_count, tap_col : tap_col + col_count]
            )
    return depth_out


def on_device_plain(
    latents,
    clip_height,
    clip_width,
    expand_weight,
    expand_bias,
    depth_weight,
    depth_bias,
    project_weight,
):
    batch_size, row_count, col_count, depth = latents.shape
    tokens = batch_size * row_count * col_count
    first_row = lax.axis_index("row") * row_count
    row_ids = first_row + jnp.arange(row_count, dtype=jnp.int32)
    col_ids = jnp.arange(col_count, dtype=jnp.int32)
    valid_mask = (
        (row_ids[None, :, None] < clip_height[:, None, None])
        & (col_ids[None, None, :] < clip_width[:, None, None])
    ).astype(jnp.float32)[..., None]
    channels = latents.reshape(tokens, depth).T
    gathered = lax.all_gather(channels, "tensor", axis=0, tiled=True)
    pre_act = jnp.einsum("dt,kdf->tkf", gathered, expand_weight, preferred_element_type=jnp.float32)
    pre_act = pre_act.reshape(batch_size, row_count, col_count, 2, -1)
    expanded = (jax.nn.silu(pre_act + expand_bias) * valid_mask[..., None]).astype(jnp.bfloat16)
    padded = halo_rows(expanded)
    depth_out = depthwise(padded, depth_weight, depth_bias, row_count, col_count)
    hidden = (depth_out[:, :, :, 0] * jax.nn.silu(depth_out[:, :, :, 1])).astype(jnp.bfloat16)
    partial_term = jnp.einsum(
        "tf,fd->dt", hidden.reshape(tokens, -1), project_weight, preferred_element_type=jnp.float32
    ).astype(jnp.bfloat16)
    summed = lax.psum_scatter(partial_term, "tensor", scatter_dimension=0, tiled=True)
    summed = summed.T.reshape(latents.shape).astype(jnp.float32)
    return (summed * valid_mask).astype(jnp.bfloat16)


def slot_clips(width_ref, batch_size):
    narrow, least = jnp.int32(0), width_ref[0]
    for b in range(1, batch_size):
        closer = width_ref[b] < least
        narrow = jnp.where(closer, b, narrow)
        least = jnp.where(closer, width_ref[b], least)
    return [jnp.where(narrow <= s, s + 1, s) for s in range(batch_size - 1)] + [narrow]


def slot_widths(batch_size, col_count):
    return [col_count] * (batch_size - 1) + [col_count // 2]


class Chunk:
    def __init__(self, slots, widths, depth):
        self.slots = slots
        self.widths = [widths[s] for s in slots]
        self.starts = [sum(self.widths[:i]) for i in range(len(slots))]
        self.kept = sum(self.widths)
        self.block = -(-self.kept // 128) * 128
        self.depth, self.rest = depth, depth - LANES
        across = LANES // self.block
        groups = self.rest // GROUP
        self.places = [(g // across * GROUP, g % across * self.block) for g in range(groups)]
        self.lines = self.kept + -(-groups // across) * GROUP
        self.tokens = 2 * self.kept
        self.full, self.left = self.tokens // 128, self.tokens % 128
        self.upper = -(-depth // (2 * GROUP)) * GROUP
        self.unit = (self.full * depth + (self.upper if self.left else 0), 128)

    def clips(self, width_ref, batch_size):
        order = slot_clips(width_ref, batch_size)
        return [order[s] for s in self.slots]

    def mask_column(self, height_ref, width_ref, row_id):
        pieces = []
        clips = self.clips(width_ref, width_ref.shape[0])
        for clip, width in zip(clips, self.widths):
            bound = jnp.where((row_id >= 0) & (row_id < height_ref[clip]), width_ref[clip], 0)
            col = lax.broadcasted_iota(jnp.int32, (width, 128), 0)
            pieces.append((col < bound).astype(jnp.float32))
        return jnp.concatenate(pieces, axis=0)

    def put_unit(self, unit_ref, sums):
        depth, at = self.depth, self.full * self.depth
        for b in range(self.full):
            unit_ref[b * depth : (b + 1) * depth, :] = sums[:, b * 128 : (b + 1) * 128]
        if self.left:
            tail = sums[:, self.full * 128 :]
            lower = depth - self.upper
            unit_ref[at : at + self.upper, : self.left] = tail[: self.upper]
            unit_ref[at : at + lower, self.left :] = tail[self.upper :]
            if lower < self.upper:
                unit_ref[at + lower :, self.left :] = jnp.zeros(
                    (self.upper - lower, 128 - self.left), sums.dtype
                )

    def get_unit(self, unit):
        depth, at = self.depth, self.full * self.depth
        blocks = [unit[b * depth : (b + 1) * depth, :] for b in range(self.full)]
        if self.left:
            lower = depth - self.upper
            blocks.append(
                jnp.concatenate(
                    [unit[at : at + self.upper, : self.left], unit[at : at + lower, self.left :]], axis=0
                )
            )
        return jnp.concatenate(blocks, axis=1)


def parity_of():
    return lax.rem(lax.axis_index("row"), 2)


def row_of(place, parity):
    return jnp.where(parity == 0, (-1, 0, 1, 2)[place], (2, 1, 0, -1)[place])


def silu(v):
    h = 0.5 * v
    return h + h * jnp.tanh(h)


def pack_kernel(width_ref, x_ref, *out_refs, chunks):
    parity = parity_of()
    for chunk, out_ref in zip(chunks, out_refs):
        for place in range(2):
            row = jnp.where(parity == 0, 1 - place, place)
            tails = []
            for clip, width, at in zip(
                chunk.clips(width_ref, x_ref.shape[0]), chunk.widths, chunk.starts
            ):
                out_ref[place, at : at + width, :] = x_ref[clip, row, :width, :LANES]
                tails.append(x_ref[clip, row, :width, LANES:].astype(jnp.float32))
            if chunk.block > chunk.kept:
                tails.append(jnp.zeros((chunk.block - chunk.kept, chunk.rest), jnp.float32))
            turned = jnp.concatenate(tails, axis=0).T.astype(jnp.bfloat16)
            kept = chunk.kept
            out_ref[place, kept:, :] = jnp.zeros((chunk.lines - kept, LANES), jnp.bfloat16)
            for g, (down, over) in enumerate(chunk.places):
                out_ref[place, kept + down : kept + down + GROUP, over : over + chunk.block] = turned[
                    g * GROUP : (g + 1) * GROUP
                ]


def hidden_kernel(height_ref, width_ref, *refs, chunk, shards, groups, count):
    own_refs = refs[:shards]
    inner_refs = refs[shards : shards + count]
    outer_refs = refs[shards + count : shards + 2 * count]
    w_ref, eb_ref, dw_ref, db_ref, out_ref, x_scr, m_scr, e_scr = refs[shards + 2 * count :]
    kept, rest, depth = chunk.kept, chunk.rest, chunk.depth
    me = lax.axis_index("tensor")
    parity = parity_of()
    subs = w_ref.shape[2] // TILE

    @pl.when(pl.program_id(0) == 0)
    def _():
        spots = {j: (g, i) for g, js in enumerate(groups) for i, j in enumerate(js)}
        for place in range(4):
            tails = []
            lines = slice(place * kept, (place + 1) * kept)
            for j in range(shards):
                g, i = spots[j]
                packet = (
                    outer_refs[g].at[i],
                    own_refs[j].at[1],
                    own_refs[j].at[0],
                    inner_refs[g].at[i],
                )[place]
                x_scr[lines, j * LANES : (j + 1) * LANES] = packet[:kept, :]
                for down, over in chunk.places:
                    tails.append(packet[kept + down : kept + down + GROUP, over : over + chunk.block])
            turned = jnp.concatenate(tails, axis=0).astype(jnp.float32).T
            x_scr[lines, shards * LANES :] = turned[:kept].astype(jnp.bfloat16)
            row_id = lax.axis_index("row") * 2 + row_of(place, parity)
            m_scr[lines, :] = chunk.mask_column(height_ref, width_ref, row_id)

    bases = [pl.multiple_of(lax.bitwise_xor(me, j) * depth, GROUP) for j in range(shards)]
    for sub in range(subs):
        units = slice(sub * TILE, (sub + 1) * TILE)
        for k in range(2):
            weight = jnp.concatenate(
                [w_ref[k, pl.ds(base, LANES), units] for base in bases]
                + [w_ref[k, pl.ds(pl.multiple_of(base + LANES, GROUP), rest), units] for base in bases],
                axis=0,
            )
            pre_act = jnp.dot(x_scr[...], weight, preferred_element_type=jnp.float32)
            mask = jnp.concatenate([m_scr[...]] * (TILE // 128), axis=1)
            e_scr[sub, k] = silu(pre_act + eb_ref[k : k + 1, units]) * mask

    line = lax.broadcasted_iota(jnp.int32, (kept, TILE), 0)
    not_first, not_last = None, None
    for at, width in zip(chunk.starts, chunk.widths):
        first, last = line != at, line != at + width - 1
        not_first = first if not_first is None else not_first & first
        not_last = last if not_last is None else not_last & last
    for sub in range(subs):
        units = slice(sub * TILE, (sub + 1) * TILE)
        for place in (1, 2):
            halves = []
            for k in range(2):
                sums = []
                for tap_col in range(3):
                    total = None
                    for i in range(3):
                        tap_row = jnp.where(parity == 0, i, 2 - i)
                        cells = e_scr[sub, k, (place + i - 1) * kept : (place + i) * kept, :]
                        term = dw_ref[tap_row, tap_col, k : k + 1, units] * cells
                        total = term if total is None else total + term
                    sums.append(total)
                left = jnp.where(not_first, pltpu.roll(sums[0], 1, 0), 0.0)
                right = jnp.where(not_last, pltpu.roll(sums[2], kept - 1, 0), 0.0)
                halves.append(sums[1] + left + right + db_ref[k : k + 1, units])
            hidden = halves[0] * silu(halves[1])
            out_ref[(2 - place) * kept : (3 - place) * kept, units] = hidden.astype(jnp.bfloat16)


def project(weight_ref, hidden_ref):
    return lax.dot_general(
        weight_ref[...],
        hidden_ref[...],
        (((1,), (1,)), ((), ())),
        preferred_element_type=jnp.float32,
    )


def unit_kernel(place_ref, weight_ref, hidden_ref, *refs, chunk):
    out_ref = refs[-1]
    sums = project(weight_ref, hidden_ref)
    for ref in refs[:-1]:
        sums = sums + chunk.get_unit(ref[...].astype(jnp.float32))
    chunk.put_unit(out_ref, sums.astype(jnp.bfloat16))


def final_kernel(place_ref, height_ref, width_ref, weight_ref, hidden_ref, *refs, chunk, sources):
    out_ref = refs[-1]
    if len(refs) > sources + 1:
        out_ref[...] = refs[sources][...]
    sums = project(weight_ref, hidden_ref)
    for ref in refs[:sources]:
        sums = sums + chunk.get_unit(ref[...].astype(jnp.float32))
    cells = sums.T
    parity = parity_of()
    for place in range(2):
        row = jnp.where(parity == 0, 1 - place, place)
        row_id = lax.axis_index("row") * 2 + row
        mask = chunk.mask_column(height_ref, width_ref, row_id)[:, :1] > 0
        part = cells[place * chunk.kept : (place + 1) * chunk.kept]
        part = jnp.where(mask, part, 0.0).astype(jnp.bfloat16)
        clips = chunk.clips(width_ref, width_ref.shape[0])
        for clip, width, at in zip(clips, chunk.widths, chunk.starts):
            out_ref[clip, row, :width, :] = part[at : at + width]
            if width < out_ref.shape[2]:
                blank = jnp.zeros((out_ref.shape[2] - width, chunk.depth), jnp.bfloat16)
                out_ref[clip, row, width:, :] = blank


VMEM = pl.BlockSpec(memory_space=pltpu.VMEM)
MIB = 1024 * 1024


def after(value, *others):
    return lax.optimization_barrier((value,) + others)[0]


def on_device_packed(
    latents,
    clip_height,
    clip_width,
    expand_weight,
    expand_bias,
    depth_weight,
    depth_bias,
    project_weight,
):
    batch_size, row_count, col_count, depth = latents.shape
    shards, row_devices = lax.axis_size("tensor"), lax.axis_size("row")
    hidden_count = expand_weight.shape[2]
    full_depth = shards * depth
    chunks = chunks_of(batch_size, col_count, depth)
    own = pl.pallas_call(
        functools.partial(pack_kernel, chunks=chunks),
        out_shape=[jax.ShapeDtypeStruct((2, c.lines, LANES), jnp.bfloat16) for c in chunks],
        grid_spec=pltpu.PrefetchScalarGridSpec(
            num_scalar_prefetch=1, grid=(), in_specs=[VMEM], out_specs=[VMEM] * len(chunks)
        ),
        name="pack",
    )(clip_width, latents)
    me = lax.axis_index("tensor").astype(jnp.int32).reshape(1)
    project_turned = project_weight.T

    sibling = [(i, i ^ 1) for i in range(row_devices)]
    beyond = [(i, i + 1) for i in range(1, row_devices - 1, 2)]
    beyond = beyond + [(b, a) for a, b in beyond]
    near = [(i, i ^ 1) for i in range(4)]
    two_off = [(i, i ^ 2) for i in range(4)]
    middle = [(1, 2), (2, 1)]
    to_end = [(2, 3), (1, 0)]
    from_end = [(0, 1), (3, 2)]

    def halos(packets, groups):
        inner = [jnp.concatenate([packets[j][:1] for j in js], axis=0) for js in groups]
        outer = [jnp.concatenate([packets[j][1:] for j in js], axis=0) for js in groups]
        return (
            [lax.ppermute(x, "row", sibling) for x in inner],
            [lax.ppermute(x, "row", beyond) for x in outer],
        )

    def relay(mine):
        second = lax.ppermute(mine, "tensor", two_off)
        first = lax.ppermute(mine, "tensor", near)
        across = lax.ppermute(after(mine, second), "tensor", middle)
        passed = lax.ppermute(second, "tensor", to_end)
        return [mine, first, second, across + passed]

    def direct(mine):
        return [mine] + [
            lax.ppermute(mine, "tensor", [(i, i ^ j) for i in range(4)]) for j in range(1, 4)
        ]

    out = None
    packets = relay(own[0])
    groups = ((0,), (1, 2), (3,))
    inner, outer = halos(packets, groups)
    upcoming = direct(after(own[1], packets[3]))
    for number, chunk in enumerate(chunks):
        if number:
            packets, groups = list(lax.optimization_barrier((*upcoming, hidden))[:shards]), ((0, 1, 2, 3),)
            inner, outer = halos(packets, groups)
            packets[0] = after(packets[0], last_unit)
        wide = 2 * TILE
        whole = lambda shape: pl.BlockSpec(shape, lambda f, *_: (0,) * len(shape))
        lines = 4 * chunk.kept
        hidden = pl.pallas_call(
            functools.partial(
                hidden_kernel, chunk=chunk, shards=shards, groups=groups, count=len(groups)
            ),
            out_shape=jax.ShapeDtypeStruct((chunk.tokens, hidden_count), jnp.bfloat16),
            grid_spec=pltpu.PrefetchScalarGridSpec(
                num_scalar_prefetch=2,
                grid=(-(-hidden_count // wide),),
                in_specs=[whole(p.shape) for p in packets + inner + outer]
                + [
                    pl.BlockSpec((2, full_depth, wide), lambda f, *_: (0, 0, f)),
                    pl.BlockSpec((2, wide), lambda f, *_: (0, f)),
                    pl.BlockSpec((3, 3, 2, wide), lambda f, *_: (0, 0, 0, f)),
                    pl.BlockSpec((2, wide), lambda f, *_: (0, f)),
                ],
                out_specs=pl.BlockSpec((chunk.tokens, wide), lambda f, *_: (0, f)),
                scratch_shapes=[
                    pltpu.VMEM((lines, full_depth), jnp.bfloat16),
                    pltpu.VMEM((lines, 128), jnp.float32),
                    pltpu.VMEM((2, 2, lines, TILE), jnp.float32),
                ],
            ),
            compiler_params=pltpu.CompilerParams(vmem_limit_bytes=40 * MIB),
            cost_estimate=pl.CostEstimate(
                flops=4 * lines * full_depth * hidden_count,
                bytes_accessed=4 * full_depth * hidden_count,
                transcendentals=3 * lines * hidden_count,
            ),
            name="expand_conv",
        )(
            clip_height,
            clip_width,
            *packets,
            *inner,
            *outer,
            expand_weight,
            expand_bias,
            depth_weight,
            depth_bias,
        )

        weight_of = lambda j: pl.BlockSpec(
            (depth, hidden_count), lambda f, place, *_: (lax.bitwise_xor(place[0], j), 0)
        )
        cost = pl.CostEstimate(
            flops=2 * chunk.tokens * depth * hidden_count,
            bytes_accessed=2 * depth * hidden_count + 2 * chunk.tokens * hidden_count,
            transcendentals=0,
        )

        def unit(j, *added):
            return pl.pallas_call(
                functools.partial(unit_kernel, chunk=chunk),
                out_shape=jax.ShapeDtypeStruct(chunk.unit, jnp.bfloat16),
                grid_spec=pltpu.PrefetchScalarGridSpec(
                    num_scalar_prefetch=1,
                    grid=(1,),
                    in_specs=[weight_of(j), whole(hidden.shape)] + [whole(chunk.unit)] * len(added),
                    out_specs=whole(chunk.unit),
                ),
                compiler_params=pltpu.CompilerParams(vmem_limit_bytes=24 * MIB),
                cost_estimate=cost,
                name=f"project_{j}",
            )(me, project_turned, hidden, *added)

        if number:
            hidden = after(hidden, *arrived)
        far = unit(3)
        relayed = lax.ppermute(far, "tensor", from_end)
        across = lax.ppermute(far, "tensor", middle)
        close = unit(1)
        relayed, across = lax.optimization_barrier((relayed, across))
        last_unit = unit(2, relayed)
        arrived = [
            across,
            lax.ppermute(last_unit, "tensor", two_off),
            lax.ppermute(after(close, relayed), "tensor", near),
        ]
        extra = [] if out is None else [out]
        out = pl.pallas_call(
            functools.partial(final_kernel, chunk=chunk, sources=len(arrived)),
            out_shape=jax.ShapeDtypeStruct(latents.shape, jnp.bfloat16),
            grid_spec=pltpu.PrefetchScalarGridSpec(
                num_scalar_prefetch=3,
                grid=(1,),
                in_specs=[weight_of(0), whole(hidden.shape)]
                + [whole(chunk.unit)] * len(arrived)
                + [whole(latents.shape)] * len(extra),
                out_specs=whole(latents.shape),
            ),
            compiler_params=pltpu.CompilerParams(vmem_limit_bytes=24 * MIB),
            cost_estimate=cost,
            name="finish",
        )(me, clip_height, clip_width, project_turned, hidden, *arrived, *extra)
    return out


def chunks_of(batch_size, col_count, depth):
    widths = slot_widths(batch_size, col_count)
    half = batch_size // 2
    return [Chunk(slots, widths, depth) for slots in (list(range(half)), list(range(half, batch_size)))]


def on_device(latents, clip_height, clip_width, expand_weight, *rest_of):
    batch_size, row_count, col_count, depth = latents.shape
    fits = (
        batch_size >= 2
        and row_count == 2
        and lax.axis_size("row") % 2 == 0
        and lax.axis_size("tensor") == 4
        and depth > LANES
        and (depth - LANES) % GROUP == 0
        and depth % GROUP == 0
        and all(
            c.block in (128, 256, 512) and c.kept % GROUP == 0 and c.left in (0, 64)
            for c in chunks_of(batch_size, col_count, depth)
        )
    )
    run = on_device_packed if fits else on_device_plain
    return run(latents, clip_height, clip_width, expand_weight, *rest_of)


def solution(mesh):
    in_specs = (
        P(None, "row", None, "tensor"),
        P(),
        P(),
        P(None, None, "tensor"),
        P(None, "tensor"),
        P(None, None, None, "tensor"),
        P(None, "tensor"),
        P("tensor", None),
    )
    out_specs = P(None, "row", None, "tensor")
    return jax.shard_map(
        on_device, mesh=mesh, in_specs=in_specs, out_specs=out_specs, check_vma=False
    )
```

```python
import functools

import jax
import jax.numpy as jnp
from jax import lax
from jax.experimental import pallas as pl
from jax.experimental.pallas import tpu as pltpu
from jax.sharding import PartitionSpec as P

LANES = 512
GROUP = 16
TILE = 256


def halo_rows(cells):
    count = lax.axis_size("row")
    ends = count - 1
    head = cells[:, :1]
    tail = cells[:, -1:]
    above = lax.ppermute(tail, "row", [(i, i + 1) for i in range(ends)])
    below = lax.ppermute(head, "row", [(i + 1, i) for i in range(ends)])
    return jnp.concatenate([above, cells, below], axis=1)


def depthwise(padded, depth_weight, depth_bias, row_count, col_count):
    widened = jnp.pad(padded, ((0, 0), (0, 0), (1, 1), (0, 0), (0, 0)))
    out_shape = (widened.shape[0], row_count, col_count) + widened.shape[3:]
    depth_out = jnp.zeros(out_shape, jnp.float32) + depth_bias
    for tap_row in range(3):
        for tap_col in range(3):
            depth_out = (
                depth_out
                + depth_weight[tap_row, tap_col]
                * widened[:, tap_row : tap_row + row_count, tap_col : tap_col + col_count]
            )
    return depth_out


def on_device_plain(
    latents,
    clip_height,
    clip_width,
    expand_weight,
    expand_bias,
    depth_weight,
    depth_bias,
    project_weight,
):
    batch_size, row_count, col_count, depth = latents.shape
    tokens = batch_size * row_count * col_count
    first_row = lax.axis_index("row") * row_count
    row_ids = first_row + jnp.arange(row_count, dtype=jnp.int32)
    col_ids = jnp.arange(col_count, dtype=jnp.int32)
    valid_mask = (
        (row_ids[None, :, None] < clip_height[:, None, None])
        & (col_ids[None, None, :] < clip_width[:, None, None])
    ).astype(jnp.float32)[..., None]
    channels = latents.reshape(tokens, depth).T
    gathered = lax.all_gather(channels, "tensor", axis=0, tiled=True)
    pre_act = jnp.einsum("dt,kdf->tkf", gathered, expand_weight, preferred_element_type=jnp.float32)
    pre_act = pre_act.reshape(batch_size, row_count, col_count, 2, -1)
    expanded = (jax.nn.silu(pre_act + expand_bias) * valid_mask[..., None]).astype(jnp.bfloat16)
    padded = halo_rows(expanded)
    depth_out = depthwise(padded, depth_weight, depth_bias, row_count, col_count)
    hidden = (depth_out[:, :, :, 0] * jax.nn.silu(depth_out[:, :, :, 1])).astype(jnp.bfloat16)
    partial_term = jnp.einsum(
        "tf,fd->dt", hidden.reshape(tokens, -1), project_weight, preferred_element_type=jnp.float32
    ).astype(jnp.bfloat16)
    summed = lax.psum_scatter(partial_term, "tensor", scatter_dimension=0, tiled=True)
    summed = summed.T.reshape(latents.shape).astype(jnp.float32)
    return (summed * valid_mask).astype(jnp.bfloat16)


def slot_clips(width_ref, batch_size):
    narrow, least = jnp.int32(0), width_ref[0]
    for b in range(1, batch_size):
        closer = width_ref[b] < least
        narrow = jnp.where(closer, b, narrow)
        least = jnp.where(closer, width_ref[b], least)
    return [jnp.where(narrow <= s, s + 1, s) for s in range(batch_size - 1)] + [narrow]


def slot_widths(batch_size, col_count):
    return [col_count] * (batch_size - 1) + [col_count // 2]


class Chunk:
    def __init__(self, slots, widths, depth):
        self.slots = slots
        self.widths = [widths[s] for s in slots]
        self.starts = [sum(self.widths[:i]) for i in range(len(slots))]
        self.kept = sum(self.widths)
        self.block = -(-self.kept // 128) * 128
        self.depth, self.rest = depth, depth - LANES
        across = LANES // self.block
        groups = self.rest // GROUP
        self.places = [(g // across * GROUP, g % across * self.block) for g in range(groups)]
        self.lines = self.kept + -(-groups // across) * GROUP
        self.tokens = 2 * self.kept
        self.full, self.left = self.tokens // 128, self.tokens % 128
        self.upper = -(-depth // (2 * GROUP)) * GROUP
        self.unit = (self.full * depth + (self.upper if self.left else 0), 128)

    def clips(self, width_ref, batch_size):
        order = slot_clips(width_ref, batch_size)
        return [order[s] for s in self.slots]

    def mask_column(self, height_ref, width_ref, row_id):
        pieces = []
        clips = self.clips(width_ref, width_ref.shape[0])
        for clip, width in zip(clips, self.widths):
            bound = jnp.where((row_id >= 0) & (row_id < height_ref[clip]), width_ref[clip], 0)
            col = lax.broadcasted_iota(jnp.int32, (width, 128), 0)
            pieces.append((col < bound).astype(jnp.float32))
        return jnp.concatenate(pieces, axis=0)

    def put_unit(self, unit_ref, sums):
        depth, at = self.depth, self.full * self.depth
        for b in range(self.full):
            unit_ref[b * depth : (b + 1) * depth, :] = sums[:, b * 128 : (b + 1) * 128]
        if self.left:
            tail = sums[:, self.full * 128 :]
            lower = depth - self.upper
            unit_ref[at : at + self.upper, : self.left] = tail[: self.upper]
            unit_ref[at : at + lower, self.left :] = tail[self.upper :]
            if lower < self.upper:
                unit_ref[at + lower :, self.left :] = jnp.zeros(
                    (self.upper - lower, 128 - self.left), sums.dtype
                )

    def get_unit(self, unit):
        depth, at = self.depth, self.full * self.depth
        blocks = [unit[b * depth : (b + 1) * depth, :] for b in range(self.full)]
        if self.left:
            lower = depth - self.upper
            blocks.append(
                jnp.concatenate(
                    [unit[at : at + self.upper, : self.left], unit[at : at + lower, self.left :]], axis=0
                )
            )
        return jnp.concatenate(blocks, axis=1)


def parity_of():
    return lax.rem(lax.axis_index("row"), 2)


def row_of(place, parity):
    return jnp.where(parity == 0, (-1, 0, 1, 2)[place], (2, 1, 0, -1)[place])


def silu(v):
    h = 0.5 * v
    return h + h * jnp.tanh(h)


def pack_kernel(height_ref, width_ref, x_ref, *refs, chunks):
    parity = parity_of()
    out_refs, mask_refs = refs[: len(chunks)], refs[len(chunks) :]
    for chunk, out_ref, mask_ref in zip(chunks, out_refs, mask_refs):
        for place in range(4):
            row_id = lax.axis_index("row") * 2 + row_of(place, parity)
            mask_ref[place] = chunk.mask_column(height_ref, width_ref, row_id)
        for place in range(2):
            row = jnp.where(parity == 0, 1 - place, place)
            tails = []
            for clip, width, at in zip(
                chunk.clips(width_ref, x_ref.shape[0]), chunk.widths, chunk.starts
            ):
                out_ref[place, at : at + width, :] = x_ref[clip, row, :width, :LANES]
                tails.append(x_ref[clip, row, :width, LANES:].astype(jnp.float32))
            if chunk.block > chunk.kept:
                tails.append(jnp.zeros((chunk.block - chunk.kept, chunk.rest), jnp.float32))
            turned = jnp.concatenate(tails, axis=0).T.astype(jnp.bfloat16)
            kept = chunk.kept
            out_ref[place, kept:, :] = jnp.zeros((chunk.lines - kept, LANES), jnp.bfloat16)
            for g, (down, over) in enumerate(chunk.places):
                out_ref[place, kept + down : kept + down + GROUP, over : over + chunk.block] = turned[
                    g * GROUP : (g + 1) * GROUP
                ]


def tiles_of(hidden_count):
    return [slice(at, min(at + TILE, hidden_count)) for at in range(0, hidden_count, TILE)]


def gather_rows(x_scr, chunk, rows):
    kept = chunk.kept
    for place, packets in enumerate(rows):
        lines = slice(place * kept, (place + 1) * kept)
        tails = []
        for j, packet in enumerate(packets):
            x_scr[lines, j * LANES : (j + 1) * LANES] = packet[:kept, :]
            for down, over in chunk.places:
                tails.append(packet[kept + down : kept + down + GROUP, over : over + chunk.block])
        turned = jnp.concatenate(tails, axis=0).astype(jnp.float32).T
        x_scr[lines, len(packets) * LANES :] = turned[:kept].astype(jnp.bfloat16)


def load_kernel(w_ref, out_ref, token_ref, sems, *, shards, depth):
    me = lax.axis_index("tensor")
    rest = depth - LANES
    copies = []
    for k in range(2):
        for j in range(shards):
            base = lax.bitwise_xor(me, j) * depth
            for part, (source, size, target) in enumerate(
                ((base, LANES, j * LANES), (base + LANES, rest, shards * LANES + j * rest))
            ):
                copies.append(
                    pltpu.make_async_copy(
                        w_ref.at[k, pl.ds(pl.multiple_of(source, GROUP), size)],
                        out_ref.at[k, pl.ds(target, size)],
                        sems.at[k, j, part],
                    )
                )
    for copy in copies:
        copy.start()
    token_ref[...] = jnp.zeros_like(token_ref)
    for copy in copies:
        copy.wait()


def expand(x_scr, w_ref, par_ref, k, units):
    pre_act = jnp.dot(x_scr[...], w_ref[k, :, units], preferred_element_type=jnp.float32)
    return silu(pre_act + par_ref[18 + k : 19 + k, units])


def masked(cells, mask):
    width = cells.shape[1]
    return cells * jnp.concatenate([mask] * -(-width // 128), axis=1)[:, :width]


def own_kernel(*refs, chunk, shards):
    packet_refs, (mask_ref, par_ref, w_ref, out_ref, x_scr) = refs[:shards], refs[shards:]
    kept = chunk.kept
    gather_rows(x_scr, chunk, [[p.at[1] for p in packet_refs], [p.at[0] for p in packet_refs]])
    mask = jnp.concatenate([mask_ref[1], mask_ref[2]], axis=0)
    for units in tiles_of(w_ref.shape[2]):
        for k in range(2):
            out_ref[k, :, units] = masked(expand(x_scr, w_ref, par_ref, k, units), mask)


def hidden_kernel(*refs, chunk, shards, groups):
    count = len(groups)
    inner_refs, outer_refs = refs[:count], refs[count : 2 * count]
    own_ref, mask_ref, par_ref, w_ref, out_ref, x_scr = refs[2 * count :]
    kept = chunk.kept
    parity = parity_of()
    spots = {j: (g, i) for g, js in enumerate(groups) for i, j in enumerate(js)}
    gather_rows(
        x_scr,
        chunk,
        [[refs_of[spots[j][0]].at[spots[j][1]] for j in range(shards)] for refs_of in (outer_refs, inner_refs)],
    )
    mask = jnp.concatenate([mask_ref[0], mask_ref[3]], axis=0)

    def around(units):
        return [
            masked(expand(x_scr, w_ref, par_ref, k, units), mask) for k in range(2)
        ]

    def convolve(units, cells):
        width = units.stop - units.start
        line = lax.broadcasted_iota(jnp.int32, (kept, width), 0)
        not_first, not_last = None, None
        for at, size in zip(chunk.starts, chunk.widths):
            first, last = line != at, line != at + size - 1
            not_first = first if not_first is None else not_first & first
            not_last = last if not_last is None else not_last & last
        halves = ([], [])
        for k in range(2):
            rows = [
                cells[k][:kept],
                own_ref[k, :kept, units],
                own_ref[k, kept:, units],
                cells[k][kept:],
            ]
            taps = [
                [
                    jnp.where(
                        parity == 0,
                        par_ref[i * 6 + col * 2 + k : i * 6 + col * 2 + k + 1, units],
                        par_ref[(2 - i) * 6 + col * 2 + k : (2 - i) * 6 + col * 2 + k + 1, units],
                    )
                    for col in range(3)
                ]
                for i in range(3)
            ]
            for place in range(2):
                sums = []
                for tap_col in range(3):
                    total = None
                    for i in range(3):
                        term = taps[i][tap_col] * rows[place + i]
                        total = term if total is None else total + term
                    sums.append(total)
                left = jnp.where(not_first, pltpu.roll(sums[0], 1, 0), 0.0)
                right = jnp.where(not_last, pltpu.roll(sums[2], kept - 1, 0), 0.0)
                halves[k].append(sums[1] + left + right + par_ref[20 + k : 21 + k, units])
        for place in range(2):
            hidden = halves[0][place] * silu(halves[1][place])
            out_ref[(1 - place) * kept : (2 - place) * kept, units] = hidden.astype(jnp.bfloat16)

    tiles = tiles_of(w_ref.shape[2])
    cells = around(tiles[0])
    for t, units in enumerate(tiles):
        coming = around(tiles[t + 1]) if t + 1 < len(tiles) else None
        convolve(units, cells)
        cells = coming


def project(weight_ref, hidden_ref):
    return lax.dot_general(
        weight_ref[...],
        hidden_ref[...],
        (((1,), (1,)), ((), ())),
        preferred_element_type=jnp.float32,
    )


def unit_kernel(place_ref, weight_ref, hidden_ref, *refs, chunk):
    out_ref = refs[-1]
    sums = project(weight_ref, hidden_ref)
    for ref in refs[:-1]:
        sums = sums + chunk.get_unit(ref[...].astype(jnp.float32))
    chunk.put_unit(out_ref, sums.astype(jnp.bfloat16))


def final_kernel(place_ref, width_ref, mask_ref, weight_ref, hidden_ref, *refs, chunk, sources):
    out_ref = refs[-1]
    if len(refs) > sources + 1:
        out_ref[...] = refs[sources][...]
    sums = project(weight_ref, hidden_ref)
    for ref in refs[:sources]:
        sums = sums + chunk.get_unit(ref[...].astype(jnp.float32))
    cells = sums.T
    parity = parity_of()
    for place in range(2):
        row = jnp.where(parity == 0, 1 - place, place)
        mask = mask_ref[2 - place][:, :1] > 0
        part = cells[place * chunk.kept : (place + 1) * chunk.kept]
        part = jnp.where(mask, part, 0.0).astype(jnp.bfloat16)
        clips = chunk.clips(width_ref, width_ref.shape[0])
        for clip, width, at in zip(clips, chunk.widths, chunk.starts):
            out_ref[clip, row, :width, :] = part[at : at + width]
            if width < out_ref.shape[2]:
                blank = jnp.zeros((out_ref.shape[2] - width, chunk.depth), jnp.bfloat16)
                out_ref[clip, row, width:, :] = blank


VMEM = pl.BlockSpec(memory_space=pltpu.VMEM)
MIB = 1024 * 1024


def after(value, *others):
    return lax.optimization_barrier((value,) + others)[0]


def on_device_packed(
    latents,
    clip_height,
    clip_width,
    expand_weight,
    expand_bias,
    depth_weight,
    depth_bias,
    project_weight,
):
    batch_size, row_count, col_count, depth = latents.shape
    shards, row_devices = lax.axis_size("tensor"), lax.axis_size("row")
    hidden_count = expand_weight.shape[2]
    full_depth = shards * depth
    chunks = chunks_of(batch_size, col_count, depth)
    count = len(chunks)
    packed = pl.pallas_call(
        functools.partial(pack_kernel, chunks=chunks),
        out_shape=[jax.ShapeDtypeStruct((2, c.lines, LANES), jnp.bfloat16) for c in chunks]
        + [jax.ShapeDtypeStruct((4, c.kept, 128), jnp.float32) for c in chunks],
        grid_spec=pltpu.PrefetchScalarGridSpec(
            num_scalar_prefetch=2, grid=(), in_specs=[VMEM], out_specs=[VMEM] * (2 * count)
        ),
        name="pack",
    )(clip_height, clip_width, latents)
    own, masks = packed[:count], packed[count:]
    parameters = jnp.concatenate(
        [depth_weight.reshape(18, hidden_count), expand_bias, depth_bias], axis=0
    )
    me = lax.axis_index("tensor").astype(jnp.int32).reshape(1)
    project_turned = project_weight.T

    sibling = [(i, i ^ 1) for i in range(row_devices)]
    beyond = [(i, i + 1) for i in range(1, row_devices - 1, 2)]
    beyond = beyond + [(b, a) for a, b in beyond]
    near = [(i, i ^ 1) for i in range(4)]
    two_off = [(i, i ^ 2) for i in range(4)]
    middle = [(1, 2), (2, 1)]
    to_end = [(2, 3), (1, 0)]
    from_end = [(0, 1), (3, 2)]

    def halos(packets, groups):
        inner = [jnp.concatenate([packets[j][:1] for j in js], axis=0) for js in groups]
        outer = [jnp.concatenate([packets[j][1:] for j in js], axis=0) for js in groups]
        return (
            [lax.ppermute(x, "row", sibling) for x in inner],
            [lax.ppermute(x, "row", beyond) for x in outer],
        )

    def relay(mine, token):
        second = lax.ppermute(mine, "tensor", two_off)
        first = lax.ppermute(mine, "tensor", near)
        across = lax.ppermute(after(mine, second, token), "tensor", middle)
        passed = lax.ppermute(after(second, token), "tensor", to_end)
        return [mine, first, second, across + passed]

    def direct(mine):
        return [mine] + [
            lax.ppermute(mine, "tensor", [(i, i ^ j) for i in range(4)]) for j in range(1, 4)
        ]

    out = None
    weights, token = pl.pallas_call(
        functools.partial(load_kernel, shards=shards, depth=depth),
        out_shape=[
            jax.ShapeDtypeStruct(expand_weight.shape, jnp.bfloat16),
            jax.ShapeDtypeStruct((8, 128), jnp.float32),
        ],
        in_specs=[pl.BlockSpec(memory_space=pl.ANY)],
        out_specs=[VMEM, VMEM],
        scratch_shapes=[pltpu.SemaphoreType.DMA((2, shards, 2))],
        name="load_weights",
    )(after(expand_weight, own[0]))
    packets = relay(own[0], token)
    groups = ((0,), (1, 2), (3,))
    inner, outer = halos(packets, groups)
    upcoming = direct(after(own[1], packets[3]))
    for number, chunk in enumerate(chunks):
        if number:
            packets, groups = list(lax.optimization_barrier((*upcoming, hidden))[:shards]), ((0, 1, 2, 3),)
            inner, outer = halos(packets, groups)
            packets[0] = after(packets[0], far)
        whole = lambda shape: pl.BlockSpec(shape, lambda f, *_: (0,) * len(shape))
        rows = pl.pallas_call(
            functools.partial(own_kernel, chunk=chunk, shards=shards),
            out_shape=jax.ShapeDtypeStruct((2, chunk.tokens, hidden_count), jnp.float32),
            in_specs=[VMEM] * (shards + 3),
            out_specs=VMEM,
            scratch_shapes=[pltpu.VMEM((chunk.tokens, full_depth), jnp.bfloat16)],
            compiler_params=pltpu.CompilerParams(vmem_limit_bytes=16 * MIB),
            cost_estimate=pl.CostEstimate(
                flops=4 * chunk.tokens * full_depth * hidden_count,
                bytes_accessed=4 * full_depth * hidden_count,
                transcendentals=2 * chunk.tokens * hidden_count,
            ),
            name="expand_own",
        )(*packets, masks[number], parameters, weights)
        if number:
            inner[0] = after(inner[0], last_unit)
        hidden = pl.pallas_call(
            functools.partial(hidden_kernel, chunk=chunk, shards=shards, groups=groups),
            out_shape=jax.ShapeDtypeStruct((chunk.tokens, hidden_count), jnp.bfloat16),
            in_specs=[VMEM] * (2 * len(groups) + 4),
            out_specs=VMEM,
            scratch_shapes=[pltpu.VMEM((chunk.tokens, full_depth), jnp.bfloat16)],
            compiler_params=pltpu.CompilerParams(vmem_limit_bytes=16 * MIB),
            cost_estimate=pl.CostEstimate(
                flops=4 * chunk.tokens * full_depth * hidden_count,
                bytes_accessed=4 * full_depth * hidden_count,
                transcendentals=3 * chunk.tokens * hidden_count,
            ),
            name="expand_conv",
        )(*inner, *outer, rows, masks[number], parameters, weights)

        weight_of = lambda j: pl.BlockSpec(
            (depth, hidden_count), lambda f, place, *_: (lax.bitwise_xor(place[0], j), 0)
        )
        cost = pl.CostEstimate(
            flops=2 * chunk.tokens * depth * hidden_count,
            bytes_accessed=2 * depth * hidden_count + 2 * chunk.tokens * hidden_count,
            transcendentals=0,
        )

        def unit(j, *added):
            return pl.pallas_call(
                functools.partial(unit_kernel, chunk=chunk),
                out_shape=jax.ShapeDtypeStruct(chunk.unit, jnp.bfloat16),
                grid_spec=pltpu.PrefetchScalarGridSpec(
                    num_scalar_prefetch=1,
                    grid=(1,),
                    in_specs=[weight_of(j), whole(hidden.shape)] + [whole(chunk.unit)] * len(added),
                    out_specs=whole(chunk.unit),
                ),
                compiler_params=pltpu.CompilerParams(vmem_limit_bytes=24 * MIB),
                cost_estimate=cost,
                name=f"project_{j}",
            )(me, project_turned, hidden, *added)

        if number:
            hidden = after(hidden, *arrived)
        far = unit(3)
        relayed = lax.ppermute(far, "tensor", from_end)
        across = lax.ppermute(far, "tensor", middle)
        close = unit(1)
        relayed, across = lax.optimization_barrier((relayed, across))
        last_unit = unit(2, relayed)
        arrived = [
            across,
            lax.ppermute(last_unit, "tensor", two_off),
            lax.ppermute(after(close, relayed), "tensor", near),
        ]
        extra = [] if out is None else [out]
        out = pl.pallas_call(
            functools.partial(final_kernel, chunk=chunk, sources=len(arrived)),
            out_shape=jax.ShapeDtypeStruct(latents.shape, jnp.bfloat16),
            grid_spec=pltpu.PrefetchScalarGridSpec(
                num_scalar_prefetch=2,
                grid=(1,),
                in_specs=[whole(masks[number].shape), weight_of(0), whole(hidden.shape)]
                + [whole(chunk.unit)] * len(arrived)
                + [whole(latents.shape)] * len(extra),
                out_specs=whole(latents.shape),
            ),
            compiler_params=pltpu.CompilerParams(vmem_limit_bytes=24 * MIB),
            cost_estimate=cost,
            name="finish",
        )(me, clip_width, masks[number], project_turned, hidden, *arrived, *extra)
    return out


def chunks_of(batch_size, col_count, depth):
    widths = slot_widths(batch_size, col_count)
    half = batch_size // 2
    return [Chunk(slots, widths, depth) for slots in (list(range(half)), list(range(half, batch_size)))]


def on_device(latents, clip_height, clip_width, expand_weight, *rest_of):
    batch_size, row_count, col_count, depth = latents.shape
    fits = (
        batch_size >= 2
        and row_count == 2
        and lax.axis_size("row") % 2 == 0
        and lax.axis_size("tensor") == 4
        and depth > LANES
        and (depth - LANES) % GROUP == 0
        and depth % GROUP == 0
        and all(
            c.block in (128, 256, 512) and c.kept % GROUP == 0 and c.left in (0, 64)
            for c in chunks_of(batch_size, col_count, depth)
        )
    )
    run = on_device_packed if fits else on_device_plain
    return run(latents, clip_height, clip_width, expand_weight, *rest_of)


def solution(mesh):
    in_specs = (
        P(None, "row", None, "tensor"),
        P(),
        P(),
        P(None, None, "tensor"),
        P(None, "tensor"),
        P(None, None, None, "tensor"),
        P(None, "tensor"),
        P("tensor", None),
    )
    out_specs = P(None, "row", None, "tensor")
    return jax.shard_map(
        on_device, mesh=mesh, in_specs=in_specs, out_specs=out_specs, check_vma=False
    )
```

```python
import functools

import jax
import jax.numpy as jnp
from jax import lax
from jax.experimental import pallas as pl
from jax.experimental.pallas import tpu as pltpu
from jax.sharding import PartitionSpec as P

LANES = 512
GROUP = 16
TILE = 256


def halo_rows(cells):
    count = lax.axis_size("row")
    ends = count - 1
    head = cells[:, :1]
    tail = cells[:, -1:]
    above = lax.ppermute(tail, "row", [(i, i + 1) for i in range(ends)])
    below = lax.ppermute(head, "row", [(i + 1, i) for i in range(ends)])
    return jnp.concatenate([above, cells, below], axis=1)


def depthwise(padded, depth_weight, depth_bias, row_count, col_count):
    widened = jnp.pad(padded, ((0, 0), (0, 0), (1, 1), (0, 0), (0, 0)))
    out_shape = (widened.shape[0], row_count, col_count) + widened.shape[3:]
    depth_out = jnp.zeros(out_shape, jnp.float32) + depth_bias
    for tap_row in range(3):
        for tap_col in range(3):
            depth_out = (
                depth_out
                + depth_weight[tap_row, tap_col]
                * widened[:, tap_row : tap_row + row_count, tap_col : tap_col + col_count]
            )
    return depth_out


def on_device_plain(
    latents,
    clip_height,
    clip_width,
    expand_weight,
    expand_bias,
    depth_weight,
    depth_bias,
    project_weight,
):
    batch_size, row_count, col_count, depth = latents.shape
    tokens = batch_size * row_count * col_count
    first_row = lax.axis_index("row") * row_count
    row_ids = first_row + jnp.arange(row_count, dtype=jnp.int32)
    col_ids = jnp.arange(col_count, dtype=jnp.int32)
    valid_mask = (
        (row_ids[None, :, None] < clip_height[:, None, None])
        & (col_ids[None, None, :] < clip_width[:, None, None])
    ).astype(jnp.float32)[..., None]
    channels = latents.reshape(tokens, depth).T
    gathered = lax.all_gather(channels, "tensor", axis=0, tiled=True)
    pre_act = jnp.einsum("dt,kdf->tkf", gathered, expand_weight, preferred_element_type=jnp.float32)
    pre_act = pre_act.reshape(batch_size, row_count, col_count, 2, -1)
    expanded = (jax.nn.silu(pre_act + expand_bias) * valid_mask[..., None]).astype(jnp.bfloat16)
    padded = halo_rows(expanded)
    depth_out = depthwise(padded, depth_weight, depth_bias, row_count, col_count)
    hidden = (depth_out[:, :, :, 0] * jax.nn.silu(depth_out[:, :, :, 1])).astype(jnp.bfloat16)
    partial_term = jnp.einsum(
        "tf,fd->dt", hidden.reshape(tokens, -1), project_weight, preferred_element_type=jnp.float32
    ).astype(jnp.bfloat16)
    summed = lax.psum_scatter(partial_term, "tensor", scatter_dimension=0, tiled=True)
    summed = summed.T.reshape(latents.shape).astype(jnp.float32)
    return (summed * valid_mask).astype(jnp.bfloat16)


def slot_clips(width_ref, batch_size):
    narrow, least = jnp.int32(0), width_ref[0]
    for b in range(1, batch_size):
        closer = width_ref[b] < least
        narrow = jnp.where(closer, b, narrow)
        least = jnp.where(closer, width_ref[b], least)
    return [jnp.where(narrow <= s, s + 1, s) for s in range(batch_size - 1)] + [narrow]


def slot_widths(batch_size, col_count):
    return [col_count] * (batch_size - 1) + [col_count // 2]


class Chunk:
    def __init__(self, slots, widths, depth):
        self.slots = slots
        self.widths = [widths[s] for s in slots]
        self.starts = [sum(self.widths[:i]) for i in range(len(slots))]
        self.kept = sum(self.widths)
        self.block = -(-self.kept // 128) * 128
        self.depth, self.rest = depth, depth - LANES
        across = LANES // self.block
        groups = self.rest // GROUP
        self.places = [(g // across * GROUP, g % across * self.block) for g in range(groups)]
        self.lines = self.kept + -(-groups // across) * GROUP
        self.tokens = 2 * self.kept
        self.full, self.left = self.tokens // 128, self.tokens % 128
        self.upper = -(-depth // (2 * GROUP)) * GROUP
        self.unit = (self.full * depth + (self.upper if self.left else 0), 128)

    def clips(self, width_ref, batch_size):
        order = slot_clips(width_ref, batch_size)
        return [order[s] for s in self.slots]

    def mask_column(self, height_ref, width_ref, row_id):
        pieces = []
        clips = self.clips(width_ref, width_ref.shape[0])
        for clip, width in zip(clips, self.widths):
            bound = jnp.where((row_id >= 0) & (row_id < height_ref[clip]), width_ref[clip], 0)
            col = lax.broadcasted_iota(jnp.int32, (width, 128), 0)
            pieces.append((col < bound).astype(jnp.float32))
        return jnp.concatenate(pieces, axis=0)

    def put_unit(self, unit_ref, sums):
        depth, at = self.depth, self.full * self.depth
        for b in range(self.full):
            unit_ref[b * depth : (b + 1) * depth, :] = sums[:, b * 128 : (b + 1) * 128]
        if self.left:
            tail = sums[:, self.full * 128 :]
            lower = depth - self.upper
            unit_ref[at : at + self.upper, : self.left] = tail[: self.upper]
            unit_ref[at : at + lower, self.left :] = tail[self.upper :]
            if lower < self.upper:
                unit_ref[at + lower :, self.left :] = jnp.zeros(
                    (self.upper - lower, 128 - self.left), sums.dtype
                )

    def get_unit(self, unit):
        depth, at = self.depth, self.full * self.depth
        blocks = [unit[b * depth : (b + 1) * depth, :] for b in range(self.full)]
        if self.left:
            lower = depth - self.upper
            blocks.append(
                jnp.concatenate(
                    [unit[at : at + self.upper, : self.left], unit[at : at + lower, self.left :]], axis=0
                )
            )
        return jnp.concatenate(blocks, axis=1)


def parity_of():
    return lax.rem(lax.axis_index("row"), 2)


def row_of(place, parity):
    return jnp.where(parity == 0, (-1, 0, 1, 2)[place], (2, 1, 0, -1)[place])


def silu(v):
    h = 0.5 * v
    return h + h * jnp.tanh(h)


def pack_kernel(height_ref, width_ref, x_ref, *refs, chunks):
    parity = parity_of()
    out_refs, mask_refs = refs[: len(chunks)], refs[len(chunks) :]
    for chunk, out_ref, mask_ref in zip(chunks, out_refs, mask_refs):
        for place in range(4):
            row_id = lax.axis_index("row") * 2 + row_of(place, parity)
            mask_ref[place] = chunk.mask_column(height_ref, width_ref, row_id)
        for place in range(2):
            row = jnp.where(parity == 0, 1 - place, place)
            tails = []
            for clip, width, at in zip(
                chunk.clips(width_ref, x_ref.shape[0]), chunk.widths, chunk.starts
            ):
                out_ref[place, at : at + width, :] = x_ref[clip, row, :width, :LANES]
                tails.append(x_ref[clip, row, :width, LANES:].astype(jnp.float32))
            if chunk.block > chunk.kept:
                tails.append(jnp.zeros((chunk.block - chunk.kept, chunk.rest), jnp.float32))
            turned = jnp.concatenate(tails, axis=0).T.astype(jnp.bfloat16)
            kept = chunk.kept
            out_ref[place, kept:, :] = jnp.zeros((chunk.lines - kept, LANES), jnp.bfloat16)
            for g, (down, over) in enumerate(chunk.places):
                out_ref[place, kept + down : kept + down + GROUP, over : over + chunk.block] = turned[
                    g * GROUP : (g + 1) * GROUP
                ]


def tiles_of(hidden_count):
    return [slice(at, min(at + TILE, hidden_count)) for at in range(0, hidden_count, TILE)]


def gather_rows(x_scr, chunk, rows):
    kept = chunk.kept
    for place, packets in enumerate(rows):
        lines = slice(place * kept, (place + 1) * kept)
        tails = []
        for j, packet in enumerate(packets):
            x_scr[lines, j * LANES : (j + 1) * LANES] = packet[:kept, :]
            for down, over in chunk.places:
                tails.append(packet[kept + down : kept + down + GROUP, over : over + chunk.block])
        turned = jnp.concatenate(tails, axis=0).astype(jnp.float32).T
        x_scr[lines, len(packets) * LANES :] = turned[:kept].astype(jnp.bfloat16)


def weight_copies(w_ref, w_scr, sems):
    return [
        pltpu.make_async_copy(w_ref.at[:, :, units], w_scr.at[:, :, units], sems.at[t])
        for t, units in enumerate(tiles_of(w_ref.shape[2]))
    ]


def expand(x_scr, w_scr, par_ref, chunk, k, units):
    me = lax.axis_index("tensor")
    shards = w_scr.shape[1] // chunk.depth
    bases = [pl.multiple_of(lax.bitwise_xor(me, j) * chunk.depth, GROUP) for j in range(shards)]
    weight = jnp.concatenate(
        [w_scr[k, pl.ds(base, LANES), units] for base in bases]
        + [w_scr[k, pl.ds(pl.multiple_of(base + LANES, GROUP), chunk.rest), units] for base in bases],
        axis=0,
    )
    pre_act = jnp.dot(x_scr[...], weight, preferred_element_type=jnp.float32)
    return silu(pre_act + par_ref[18 + k : 19 + k, units])


def masked(cells, mask):
    width = cells.shape[1]
    return cells * jnp.concatenate([mask] * -(-width // 128), axis=1)[:, :width]


def own_kernel(*refs, chunk, shards):
    packet_refs, (mask_ref, par_ref, w_ref, out_ref, x_scr, w_scr, sems) = refs[:shards], refs[shards:]
    kept = chunk.kept
    copies = weight_copies(w_ref, w_scr, sems)
    for copy in copies:
        copy.start()
    gather_rows(x_scr, chunk, [[p.at[1] for p in packet_refs], [p.at[0] for p in packet_refs]])
    mask = jnp.concatenate([mask_ref[1], mask_ref[2]], axis=0)
    for copy, units in zip(copies, tiles_of(w_ref.shape[2])):
        copy.wait()
        for k in range(2):
            out_ref[k, :, units] = masked(expand(x_scr, w_scr, par_ref, chunk, k, units), mask)


def hidden_kernel(*refs, chunk, shards, groups):
    count = len(groups)
    inner_refs, outer_refs = refs[:count], refs[count : 2 * count]
    own_ref, mask_ref, par_ref, w_ref, out_ref, x_scr, w_scr, sems = refs[2 * count :]
    kept = chunk.kept
    copies = weight_copies(w_ref, w_scr, sems)
    for copy in copies:
        copy.start()
    parity = parity_of()
    spots = {j: (g, i) for g, js in enumerate(groups) for i, j in enumerate(js)}
    gather_rows(
        x_scr,
        chunk,
        [[refs_of[spots[j][0]].at[spots[j][1]] for j in range(shards)] for refs_of in (outer_refs, inner_refs)],
    )
    mask = jnp.concatenate([mask_ref[0], mask_ref[3]], axis=0)

    tiles = tiles_of(w_ref.shape[2])

    def around(t):
        copies[t].wait()
        return [masked(expand(x_scr, w_scr, par_ref, chunk, k, tiles[t]), mask) for k in range(2)]

    def convolve(units, cells):
        width = units.stop - units.start
        line = lax.broadcasted_iota(jnp.int32, (kept, width), 0)
        not_first, not_last = None, None
        for at, size in zip(chunk.starts, chunk.widths):
            first, last = line != at, line != at + size - 1
            not_first = first if not_first is None else not_first & first
            not_last = last if not_last is None else not_last & last
        halves = ([], [])
        for k in range(2):
            rows = [
                cells[k][:kept],
                own_ref[k, :kept, units],
                own_ref[k, kept:, units],
                cells[k][kept:],
            ]
            taps = [
                [
                    jnp.where(
                        parity == 0,
                        par_ref[i * 6 + col * 2 + k : i * 6 + col * 2 + k + 1, units],
                        par_ref[(2 - i) * 6 + col * 2 + k : (2 - i) * 6 + col * 2 + k + 1, units],
                    )
                    for col in range(3)
                ]
                for i in range(3)
            ]
            for place in range(2):
                sums = []
                for tap_col in range(3):
                    total = None
                    for i in range(3):
                        term = taps[i][tap_col] * rows[place + i]
                        total = term if total is None else total + term
                    sums.append(total)
                left = jnp.where(not_first, pltpu.roll(sums[0], 1, 0), 0.0)
                right = jnp.where(not_last, pltpu.roll(sums[2], kept - 1, 0), 0.0)
                halves[k].append(sums[1] + left + right + par_ref[20 + k : 21 + k, units])
        for place in range(2):
            hidden = halves[0][place] * silu(halves[1][place])
            out_ref[(1 - place) * kept : (2 - place) * kept, units] = hidden.astype(jnp.bfloat16)

    cells = around(0)
    for t, units in enumerate(tiles):
        coming = around(t + 1) if t + 1 < len(tiles) else None
        convolve(units, cells)
        cells = coming


def project(weight_ref, hidden_ref):
    return lax.dot_general(
        weight_ref[...],
        hidden_ref[...],
        (((1,), (1,)), ((), ())),
        preferred_element_type=jnp.float32,
    )


def unit_kernel(place_ref, weight_ref, hidden_ref, *refs, chunk):
    out_ref = refs[-1]
    sums = project(weight_ref, hidden_ref)
    for ref in refs[:-1]:
        sums = sums + chunk.get_unit(ref[...].astype(jnp.float32))
    chunk.put_unit(out_ref, sums.astype(jnp.bfloat16))


def final_kernel(place_ref, width_ref, mask_ref, weight_ref, hidden_ref, *refs, chunk, sources):
    out_ref = refs[-1]
    if len(refs) > sources + 1:
        out_ref[...] = refs[sources][...]
    sums = project(weight_ref, hidden_ref)
    for ref in refs[:sources]:
        sums = sums + chunk.get_unit(ref[...].astype(jnp.float32))
    cells = sums.T
    parity = parity_of()
    for place in range(2):
        row = jnp.where(parity == 0, 1 - place, place)
        mask = mask_ref[2 - place][:, :1] > 0
        part = cells[place * chunk.kept : (place + 1) * chunk.kept]
        part = jnp.where(mask, part, 0.0).astype(jnp.bfloat16)
        clips = chunk.clips(width_ref, width_ref.shape[0])
        for clip, width, at in zip(clips, chunk.widths, chunk.starts):
            out_ref[clip, row, :width, :] = part[at : at + width]
            if width < out_ref.shape[2]:
                blank = jnp.zeros((out_ref.shape[2] - width, chunk.depth), jnp.bfloat16)
                out_ref[clip, row, width:, :] = blank


VMEM = pl.BlockSpec(memory_space=pltpu.VMEM)
MIB = 1024 * 1024


def after(value, *others):
    return lax.optimization_barrier((value,) + others)[0]


def on_device_packed(
    latents,
    clip_height,
    clip_width,
    expand_weight,
    expand_bias,
    depth_weight,
    depth_bias,
    project_weight,
):
    batch_size, row_count, col_count, depth = latents.shape
    shards, row_devices = lax.axis_size("tensor"), lax.axis_size("row")
    hidden_count = expand_weight.shape[2]
    full_depth = shards * depth
    chunks = chunks_of(batch_size, col_count, depth)
    count = len(chunks)
    packed = pl.pallas_call(
        functools.partial(pack_kernel, chunks=chunks),
        out_shape=[jax.ShapeDtypeStruct((2, c.lines, LANES), jnp.bfloat16) for c in chunks]
        + [jax.ShapeDtypeStruct((4, c.kept, 128), jnp.float32) for c in chunks],
        grid_spec=pltpu.PrefetchScalarGridSpec(
            num_scalar_prefetch=2, grid=(), in_specs=[VMEM], out_specs=[VMEM] * (2 * count)
        ),
        compiler_params=pltpu.CompilerParams(vmem_limit_bytes=8 * MIB),
        name="pack",
    )(clip_height, clip_width, latents)
    own, masks = packed[:count], packed[count:]
    parameters = jnp.concatenate(
        [depth_weight.reshape(18, hidden_count), expand_bias, depth_bias], axis=0
    )
    me = lax.axis_index("tensor").astype(jnp.int32).reshape(1)
    project_turned = project_weight.T

    sibling = [(i, i ^ 1) for i in range(row_devices)]
    beyond = [(i, i + 1) for i in range(1, row_devices - 1, 2)]
    beyond = beyond + [(b, a) for a, b in beyond]
    near = [(i, i ^ 1) for i in range(4)]
    two_off = [(i, i ^ 2) for i in range(4)]
    middle = [(1, 2), (2, 1)]
    to_end = [(2, 3), (1, 0)]
    from_end = [(0, 1), (3, 2)]

    def halo_rows_of(packets, js):
        inner = jnp.concatenate([packets[j][:1] for j in js], axis=0)
        outer = jnp.concatenate([packets[j][1:] for j in js], axis=0)
        return inner, outer

    def send_rows(inner, outer):
        return lax.ppermute(inner, "row", sibling), lax.ppermute(outer, "row", beyond)

    def first_phase(mine):
        return [mine, lax.ppermute(mine, "tensor", near), lax.ppermute(mine, "tensor", two_off)]

    def second_phase(parts, *others):
        mine, second = lax.optimization_barrier((parts[0], parts[2], *others))[:2]
        return lax.ppermute(second, "tensor", to_end) + lax.ppermute(mine, "tensor", middle)

    out = None
    groups = ((0, 1, 2), (3,))
    packets = first_phase(own[0])
    ready = halo_rows_of(packets, groups[0])
    upcoming = first_phase(after(own[1], *ready))
    packets.append(second_phase(packets))
    for number, chunk in enumerate(chunks):
        if number:
            packets = upcoming
            ready = halo_rows_of(packets, groups[0])
        early = send_rows(*ready)
        late = send_rows(*halo_rows_of(packets, groups[1]))
        inner, outer = zip(early, late)
        if number:
            packets[3] = after(packets[3], far)
        else:
            packets[3] = after(packets[3], *early)
        whole = lambda shape: pl.BlockSpec(shape, lambda f, *_: (0,) * len(shape))
        streamed = [
            pltpu.VMEM((chunk.tokens, full_depth), jnp.bfloat16),
            pltpu.VMEM(expand_weight.shape, jnp.bfloat16),
            pltpu.SemaphoreType.DMA((len(tiles_of(hidden_count)),)),
        ]
        rows = pl.pallas_call(
            functools.partial(own_kernel, chunk=chunk, shards=shards),
            out_shape=jax.ShapeDtypeStruct((2, chunk.tokens, hidden_count), jnp.float32),
            in_specs=[VMEM] * (shards + 2) + [pl.BlockSpec(memory_space=pl.ANY)],
            out_specs=VMEM,
            scratch_shapes=streamed,
            compiler_params=pltpu.CompilerParams(vmem_limit_bytes=44 * MIB),
            cost_estimate=pl.CostEstimate(
                flops=1000,
                bytes_accessed=1000,
                transcendentals=0,
            ),
            name="expand_own",
        )(*packets, masks[number], parameters, expand_weight)
        inner = list(inner)
        if number:
            inner[0] = after(inner[0], last_unit)
        else:
            inner[0], *upcoming = lax.optimization_barrier((inner[0], *upcoming))
            upcoming.append(second_phase(upcoming, rows))
        hidden = pl.pallas_call(
            functools.partial(hidden_kernel, chunk=chunk, shards=shards, groups=groups),
            out_shape=jax.ShapeDtypeStruct((chunk.tokens, hidden_count), jnp.bfloat16),
            in_specs=[VMEM] * (2 * len(groups) + 3) + [pl.BlockSpec(memory_space=pl.ANY)],
            out_specs=VMEM,
            scratch_shapes=streamed,
            compiler_params=pltpu.CompilerParams(vmem_limit_bytes=44 * MIB),
            cost_estimate=pl.CostEstimate(
                flops=1000,
                bytes_accessed=1000,
                transcendentals=0,
            ),
            name="expand_conv",
        )(*inner, *outer, rows, masks[number], parameters, expand_weight)

        weight_of = lambda j: pl.BlockSpec(
            (depth, hidden_count), lambda f, place, *_: (lax.bitwise_xor(place[0], j), 0)
        )
        cost = pl.CostEstimate(
            flops=2 * chunk.tokens * depth * hidden_count,
            bytes_accessed=2 * depth * hidden_count + 2 * chunk.tokens * hidden_count,
            transcendentals=0,
        )

        def unit(j, *added):
            return pl.pallas_call(
                functools.partial(unit_kernel, chunk=chunk),
                out_shape=jax.ShapeDtypeStruct(chunk.unit, jnp.bfloat16),
                grid_spec=pltpu.PrefetchScalarGridSpec(
                    num_scalar_prefetch=1,
                    grid=(1,),
                    in_specs=[weight_of(j), whole(hidden.shape)] + [whole(chunk.unit)] * len(added),
                    out_specs=whole(chunk.unit),
                ),
                compiler_params=pltpu.CompilerParams(vmem_limit_bytes=16 * MIB),
                cost_estimate=cost,
                name=f"project_{j}",
            )(me, project_turned, hidden, *added)

        if number:
            hidden = after(hidden, *arrived)
        else:
            hidden, upcoming[3] = lax.optimization_barrier((hidden, upcoming[3]))
        far = unit(3)
        relayed = lax.ppermute(far, "tensor", from_end)
        across = lax.ppermute(far, "tensor", middle)
        close = unit(1)
        relayed, across = lax.optimization_barrier((relayed, across))
        last_unit = unit(2, relayed)
        arrived = [
            across,
            lax.ppermute(last_unit, "tensor", two_off),
            lax.ppermute(after(close, relayed), "tensor", near),
        ]
        extra = [] if out is None else [out]
        out = pl.pallas_call(
            functools.partial(final_kernel, chunk=chunk, sources=len(arrived)),
            out_shape=jax.ShapeDtypeStruct(latents.shape, jnp.bfloat16),
            grid_spec=pltpu.PrefetchScalarGridSpec(
                num_scalar_prefetch=2,
                grid=(1,),
                in_specs=[whole(masks[number].shape), weight_of(0), whole(hidden.shape)]
                + [whole(chunk.unit)] * len(arrived)
                + [whole(latents.shape)] * len(extra),
                out_specs=whole(latents.shape),
            ),
            compiler_params=pltpu.CompilerParams(vmem_limit_bytes=16 * MIB),
            cost_estimate=cost,
            name="finish",
        )(me, clip_width, masks[number], project_turned, hidden, *arrived, *extra)
    return out


def chunks_of(batch_size, col_count, depth):
    widths = slot_widths(batch_size, col_count)
    half = batch_size // 2
    return [Chunk(slots, widths, depth) for slots in (list(range(half)), list(range(half, batch_size)))]


def on_device(latents, clip_height, clip_width, expand_weight, *rest_of):
    batch_size, row_count, col_count, depth = latents.shape
    fits = (
        batch_size >= 2
        and row_count == 2
        and lax.axis_size("row") % 2 == 0
        and lax.axis_size("tensor") == 4
        and depth > LANES
        and (depth - LANES) % GROUP == 0
        and depth % GROUP == 0
        and all(
            c.block in (128, 256, 512) and c.kept % GROUP == 0 and c.left in (0, 64)
            for c in chunks_of(batch_size, col_count, depth)
        )
    )
    run = on_device_packed if fits else on_device_plain
    return run(latents, clip_height, clip_width, expand_weight, *rest_of)


def solution(mesh):
    in_specs = (
        P(None, "row", None, "tensor"),
        P(),
        P(),
        P(None, None, "tensor"),
        P(None, "tensor"),
        P(None, None, None, "tensor"),
        P(None, "tensor"),
        P("tensor", None),
    )
    out_specs = P(None, "row", None, "tensor")
    return jax.shard_map(
        on_device, mesh=mesh, in_specs=in_specs, out_specs=out_specs, check_vma=False
    )
```

```python
import functools

import jax
import jax.numpy as jnp
from jax import lax
from jax.experimental import pallas as pl
from jax.experimental.pallas import tpu as pltpu
from jax.sharding import PartitionSpec as P

LANES = 512
GROUP = 16
TILE = 256


def halo_rows(cells):
    count = lax.axis_size("row")
    ends = count - 1
    head = cells[:, :1]
    tail = cells[:, -1:]
    above = lax.ppermute(tail, "row", [(i, i + 1) for i in range(ends)])
    below = lax.ppermute(head, "row", [(i + 1, i) for i in range(ends)])
    return jnp.concatenate([above, cells, below], axis=1)


def depthwise(padded, depth_weight, depth_bias, row_count, col_count):
    widened = jnp.pad(padded, ((0, 0), (0, 0), (1, 1), (0, 0), (0, 0)))
    out_shape = (widened.shape[0], row_count, col_count) + widened.shape[3:]
    depth_out = jnp.zeros(out_shape, jnp.float32) + depth_bias
    for tap_row in range(3):
        for tap_col in range(3):
            depth_out = (
                depth_out
                + depth_weight[tap_row, tap_col]
                * widened[:, tap_row : tap_row + row_count, tap_col : tap_col + col_count]
            )
    return depth_out


def on_device_plain(
    latents,
    clip_height,
    clip_width,
    expand_weight,
    expand_bias,
    depth_weight,
    depth_bias,
    project_weight,
):
    batch_size, row_count, col_count, depth = latents.shape
    tokens = batch_size * row_count * col_count
    first_row = lax.axis_index("row") * row_count
    row_ids = first_row + jnp.arange(row_count, dtype=jnp.int32)
    col_ids = jnp.arange(col_count, dtype=jnp.int32)
    valid_mask = (
        (row_ids[None, :, None] < clip_height[:, None, None])
        & (col_ids[None, None, :] < clip_width[:, None, None])
    ).astype(jnp.float32)[..., None]
    channels = latents.reshape(tokens, depth).T
    gathered = lax.all_gather(channels, "tensor", axis=0, tiled=True)
    pre_act = jnp.einsum("dt,kdf->tkf", gathered, expand_weight, preferred_element_type=jnp.float32)
    pre_act = pre_act.reshape(batch_size, row_count, col_count, 2, -1)
    expanded = (jax.nn.silu(pre_act + expand_bias) * valid_mask[..., None]).astype(jnp.bfloat16)
    padded = halo_rows(expanded)
    depth_out = depthwise(padded, depth_weight, depth_bias, row_count, col_count)
    hidden = (depth_out[:, :, :, 0] * jax.nn.silu(depth_out[:, :, :, 1])).astype(jnp.bfloat16)
    partial_term = jnp.einsum(
        "tf,fd->dt", hidden.reshape(tokens, -1), project_weight, preferred_element_type=jnp.float32
    ).astype(jnp.bfloat16)
    summed = lax.psum_scatter(partial_term, "tensor", scatter_dimension=0, tiled=True)
    summed = summed.T.reshape(latents.shape).astype(jnp.float32)
    return (summed * valid_mask).astype(jnp.bfloat16)


def slot_clips(width_ref, batch_size):
    narrow, least = jnp.int32(0), width_ref[0]
    for b in range(1, batch_size):
        closer = width_ref[b] < least
        narrow = jnp.where(closer, b, narrow)
        least = jnp.where(closer, width_ref[b], least)
    return [jnp.where(narrow <= s, s + 1, s) for s in range(batch_size - 1)] + [narrow]


def slot_widths(batch_size, col_count):
    return [col_count] * (batch_size - 1) + [col_count // 2]


class Chunk:
    def __init__(self, slots, widths, depth):
        self.slots = slots
        self.widths = [widths[s] for s in slots]
        self.starts = [sum(self.widths[:i]) for i in range(len(slots))]
        self.kept = sum(self.widths)
        self.block = -(-self.kept // 128) * 128
        self.depth, self.rest = depth, depth - LANES
        across = LANES // self.block
        groups = self.rest // GROUP
        self.places = [(g // across * GROUP, g % across * self.block) for g in range(groups)]
        self.lines = self.kept + -(-groups // across) * GROUP
        self.tokens = 2 * self.kept
        self.full, self.left = self.tokens // 128, self.tokens % 128
        self.upper = -(-depth // (2 * GROUP)) * GROUP
        self.unit = (self.full * depth + (self.upper if self.left else 0), 128)

    def clips(self, width_ref, batch_size):
        order = slot_clips(width_ref, batch_size)
        return [order[s] for s in self.slots]

    def mask_column(self, height_ref, width_ref, row_id):
        pieces = []
        clips = self.clips(width_ref, width_ref.shape[0])
        for clip, width in zip(clips, self.widths):
            bound = jnp.where((row_id >= 0) & (row_id < height_ref[clip]), width_ref[clip], 0)
            col = lax.broadcasted_iota(jnp.int32, (width, 128), 0)
            pieces.append((col < bound).astype(jnp.float32))
        return jnp.concatenate(pieces, axis=0)

    def put_unit(self, unit_ref, sums):
        depth, at = self.depth, self.full * self.depth
        for b in range(self.full):
            unit_ref[b * depth : (b + 1) * depth, :] = sums[:, b * 128 : (b + 1) * 128]
        if self.left:
            tail = sums[:, self.full * 128 :]
            lower = depth - self.upper
            unit_ref[at : at + self.upper, : self.left] = tail[: self.upper]
            unit_ref[at : at + lower, self.left :] = tail[self.upper :]
            if lower < self.upper:
                unit_ref[at + lower :, self.left :] = jnp.zeros(
                    (self.upper - lower, 128 - self.left), sums.dtype
                )

    def get_unit(self, unit):
        depth, at = self.depth, self.full * self.depth
        blocks = [unit[b * depth : (b + 1) * depth, :] for b in range(self.full)]
        if self.left:
            lower = depth - self.upper
            blocks.append(
                jnp.concatenate(
                    [unit[at : at + self.upper, : self.left], unit[at : at + lower, self.left :]], axis=0
                )
            )
        return jnp.concatenate(blocks, axis=1)


def parity_of():
    return lax.rem(lax.axis_index("row"), 2)


def row_of(place, parity):
    return jnp.where(parity == 0, (-1, 0, 1, 2)[place], (2, 1, 0, -1)[place])


def silu(v):
    h = 0.5 * v
    return h + h * jnp.tanh(h)


def pack_kernel(height_ref, width_ref, x_ref, *refs, chunks):
    parity = parity_of()
    out_refs, mask_refs = refs[: len(chunks)], refs[len(chunks) :]
    for chunk, out_ref, mask_ref in zip(chunks, out_refs, mask_refs):
        for place in range(4):
            row_id = lax.axis_index("row") * 2 + row_of(place, parity)
            mask_ref[place] = chunk.mask_column(height_ref, width_ref, row_id)
        for place in range(2):
            row = jnp.where(parity == 0, 1 - place, place)
            tails = []
            for clip, width, at in zip(
                chunk.clips(width_ref, x_ref.shape[0]), chunk.widths, chunk.starts
            ):
                out_ref[place, at : at + width, :] = x_ref[clip, row, :width, :LANES]
                tails.append(x_ref[clip, row, :width, LANES:].astype(jnp.float32))
            if chunk.block > chunk.kept:
                tails.append(jnp.zeros((chunk.block - chunk.kept, chunk.rest), jnp.float32))
            turned = jnp.concatenate(tails, axis=0).T.astype(jnp.bfloat16)
            kept = chunk.kept
            out_ref[place, kept:, :] = jnp.zeros((chunk.lines - kept, LANES), jnp.bfloat16)
            for g, (down, over) in enumerate(chunk.places):
                out_ref[place, kept + down : kept + down + GROUP, over : over + chunk.block] = turned[
                    g * GROUP : (g + 1) * GROUP
                ]


def tiles_of(hidden_count):
    return [slice(at, min(at + TILE, hidden_count)) for at in range(0, hidden_count, TILE)]


def gather_rows(x_scr, chunk, rows):
    kept = chunk.kept
    for place, packets in enumerate(rows):
        lines = slice(place * kept, (place + 1) * kept)
        tails = []
        for j, packet in enumerate(packets):
            x_scr[lines, j * LANES : (j + 1) * LANES] = packet[:kept, :]
            for down, over in chunk.places:
                tails.append(packet[kept + down : kept + down + GROUP, over : over + chunk.block])
        turned = jnp.concatenate(tails, axis=0).astype(jnp.float32).T
        x_scr[lines, len(packets) * LANES :] = turned[:kept].astype(jnp.bfloat16)


def load_kernel(w_ref, out_ref, token_ref, sems, *, shards, depth):
    me = lax.axis_index("tensor")
    rest = depth - LANES
    copies = []
    for k in range(2):
        for j in range(shards):
            base = lax.bitwise_xor(me, j) * depth
            for part, (source, size, target) in enumerate(
                ((base, LANES, j * LANES), (base + LANES, rest, shards * LANES + j * rest))
            ):
                copies.append(
                    pltpu.make_async_copy(
                        w_ref.at[k, pl.ds(pl.multiple_of(source, GROUP), size)],
                        out_ref.at[k, pl.ds(target, size)],
                        sems.at[k, j, part],
                    )
                )
    for copy in copies:
        copy.start()
    token_ref[...] = jnp.zeros_like(token_ref)
    for copy in copies:
        copy.wait()


def expand(x_scr, w_ref, par_ref, k, units):
    pre_act = jnp.dot(x_scr[...], w_ref[k, :, units], preferred_element_type=jnp.float32)
    return silu(pre_act + par_ref[18 + k : 19 + k, units])


def masked(cells, mask):
    width = cells.shape[1]
    return cells * jnp.concatenate([mask] * -(-width // 128), axis=1)[:, :width]


def own_kernel(*refs, chunk, shards):
    packet_refs, (mask_ref, par_ref, w_ref, out_ref, x_scr) = refs[:shards], refs[shards:]
    kept = chunk.kept
    gather_rows(x_scr, chunk, [[p.at[1] for p in packet_refs], [p.at[0] for p in packet_refs]])
    mask = jnp.concatenate([mask_ref[1], mask_ref[2]], axis=0)
    for units in tiles_of(w_ref.shape[2]):
        for k in range(2):
            out_ref[k, :, units] = masked(expand(x_scr, w_ref, par_ref, k, units), mask)


def hidden_kernel(*refs, chunk, shards, groups):
    count = len(groups)
    inner_refs, outer_refs = refs[:count], refs[count : 2 * count]
    own_ref, mask_ref, par_ref, w_ref, out_ref, x_scr = refs[2 * count :]
    kept = chunk.kept
    parity = parity_of()
    spots = {j: (g, i) for g, js in enumerate(groups) for i, j in enumerate(js)}
    gather_rows(
        x_scr,
        chunk,
        [[refs_of[spots[j][0]].at[spots[j][1]] for j in range(shards)] for refs_of in (outer_refs, inner_refs)],
    )
    mask = jnp.concatenate([mask_ref[0], mask_ref[3]], axis=0)

    def around(units):
        return [
            masked(expand(x_scr, w_ref, par_ref, k, units), mask) for k in range(2)
        ]

    def convolve(units, cells):
        width = units.stop - units.start
        line = lax.broadcasted_iota(jnp.int32, (kept, width), 0)
        not_first, not_last = None, None
        for at, size in zip(chunk.starts, chunk.widths):
            first, last = line != at, line != at + size - 1
            not_first = first if not_first is None else not_first & first
            not_last = last if not_last is None else not_last & last
        halves = ([], [])
        for k in range(2):
            rows = [
                cells[k][:kept],
                own_ref[k, :kept, units],
                own_ref[k, kept:, units],
                cells[k][kept:],
            ]
            taps = [
                [
                    jnp.where(
                        parity == 0,
                        par_ref[i * 6 + col * 2 + k : i * 6 + col * 2 + k + 1, units],
                        par_ref[(2 - i) * 6 + col * 2 + k : (2 - i) * 6 + col * 2 + k + 1, units],
                    )
                    for col in range(3)
                ]
                for i in range(3)
            ]
            for place in range(2):
                sums = []
                for tap_col in range(3):
                    total = None
                    for i in range(3):
                        term = taps[i][tap_col] * rows[place + i]
                        total = term if total is None else total + term
                    sums.append(total)
                left = jnp.where(not_first, pltpu.roll(sums[0], 1, 0), 0.0)
                right = jnp.where(not_last, pltpu.roll(sums[2], kept - 1, 0), 0.0)
                halves[k].append(sums[1] + left + right + par_ref[20 + k : 21 + k, units])
        for place in range(2):
            hidden = halves[0][place] * silu(halves[1][place])
            out_ref[(1 - place) * kept : (2 - place) * kept, units] = hidden.astype(jnp.bfloat16)

    tiles = tiles_of(w_ref.shape[2])
    cells = around(tiles[0])
    for t, units in enumerate(tiles):
        coming = around(tiles[t + 1]) if t + 1 < len(tiles) else None
        convolve(units, cells)
        cells = coming


def project(weight_ref, hidden_ref):
    return lax.dot_general(
        weight_ref[...],
        hidden_ref[...],
        (((1,), (1,)), ((), ())),
        preferred_element_type=jnp.float32,
    )


def unit_kernel(place_ref, weight_ref, hidden_ref, *refs, chunk):
    out_ref = refs[-1]
    sums = project(weight_ref, hidden_ref)
    for ref in refs[:-1]:
        sums = sums + chunk.get_unit(ref[...].astype(jnp.float32))
    chunk.put_unit(out_ref, sums.astype(jnp.bfloat16))


def final_kernel(place_ref, width_ref, mask_ref, weight_ref, hidden_ref, *refs, chunk, sources):
    out_ref = refs[-1]
    if len(refs) > sources + 1:
        out_ref[...] = refs[sources][...]
    sums = project(weight_ref, hidden_ref)
    for ref in refs[:sources]:
        sums = sums + chunk.get_unit(ref[...].astype(jnp.float32))
    cells = sums.T
    parity = parity_of()
    for place in range(2):
        row = jnp.where(parity == 0, 1 - place, place)
        mask = mask_ref[2 - place][:, :1] > 0
        part = cells[place * chunk.kept : (place + 1) * chunk.kept]
        part = jnp.where(mask, part, 0.0).astype(jnp.bfloat16)
        clips = chunk.clips(width_ref, width_ref.shape[0])
        for clip, width, at in zip(clips, chunk.widths, chunk.starts):
            out_ref[clip, row, :width, :] = part[at : at + width]
            if width < out_ref.shape[2]:
                blank = jnp.zeros((out_ref.shape[2] - width, chunk.depth), jnp.bfloat16)
                out_ref[clip, row, width:, :] = blank


VMEM = pl.BlockSpec(memory_space=pltpu.VMEM)
MIB = 1024 * 1024


def after(value, *others):
    return lax.optimization_barrier((value,) + others)[0]


def on_device_packed(
    latents,
    clip_height,
    clip_width,
    expand_weight,
    expand_bias,
    depth_weight,
    depth_bias,
    project_weight,
):
    batch_size, row_count, col_count, depth = latents.shape
    shards, row_devices = lax.axis_size("tensor"), lax.axis_size("row")
    hidden_count = expand_weight.shape[2]
    full_depth = shards * depth
    chunks = chunks_of(batch_size, col_count, depth)
    count = len(chunks)
    packed = pl.pallas_call(
        functools.partial(pack_kernel, chunks=chunks),
        out_shape=[jax.ShapeDtypeStruct((2, c.lines, LANES), jnp.bfloat16) for c in chunks]
        + [jax.ShapeDtypeStruct((4, c.kept, 128), jnp.float32) for c in chunks],
        grid_spec=pltpu.PrefetchScalarGridSpec(
            num_scalar_prefetch=2, grid=(), in_specs=[VMEM], out_specs=[VMEM] * (2 * count)
        ),
        name="pack",
    )(clip_height, clip_width, latents)
    own, masks = packed[:count], packed[count:]
    parameters = jnp.concatenate(
        [depth_weight.reshape(18, hidden_count), expand_bias, depth_bias], axis=0
    )
    me = lax.axis_index("tensor").astype(jnp.int32).reshape(1)
    project_turned = project_weight.T

    sibling = [(i, i ^ 1) for i in range(row_devices)]
    beyond = [(i, i + 1) for i in range(1, row_devices - 1, 2)]
    beyond = beyond + [(b, a) for a, b in beyond]
    near = [(i, i ^ 1) for i in range(4)]
    two_off = [(i, i ^ 2) for i in range(4)]
    middle = [(1, 2), (2, 1)]
    to_end = [(2, 3), (1, 0)]
    from_end = [(0, 1), (3, 2)]

    def edge_rows(packets, groups):
        return [
            [jnp.concatenate([packets[j][side : side + 1] for j in js], axis=0) for js in groups]
            for side in range(2)
        ]

    def send_rows(inner, outer):
        return (
            [lax.ppermute(x, "row", sibling) for x in inner],
            [lax.ppermute(x, "row", beyond) for x in outer],
        )

    def relay(mine, token):
        second = lax.ppermute(mine, "tensor", two_off)
        first = lax.ppermute(mine, "tensor", near)
        across = lax.ppermute(after(mine, second, token), "tensor", middle)
        passed = lax.ppermute(after(second, token), "tensor", to_end)
        return [mine, first, second, across + passed]

    def direct(mine):
        return [mine] + [
            lax.ppermute(mine, "tensor", [(i, i ^ j) for i in range(4)]) for j in range(1, 4)
        ]

    out = None
    weights, token = pl.pallas_call(
        functools.partial(load_kernel, shards=shards, depth=depth),
        out_shape=[
            jax.ShapeDtypeStruct(expand_weight.shape, jnp.bfloat16),
            jax.ShapeDtypeStruct((8, 128), jnp.float32),
        ],
        in_specs=[pl.BlockSpec(memory_space=pl.ANY)],
        out_specs=[VMEM, VMEM],
        scratch_shapes=[pltpu.SemaphoreType.DMA((2, shards, 2))],
        compiler_params=pltpu.CompilerParams(vmem_limit_bytes=36 * MIB),
        name="load_weights",
    )(after(expand_weight, own[0]))
    packets = relay(own[0], token)
    groups = ((0,), (1, 2), (3,))
    edges = edge_rows(packets, groups)
    inner, outer = send_rows(*edges)
    upcoming = direct(after(own[1], edges[0][-1], edges[1][-1]))
    for number, chunk in enumerate(chunks):
        if number:
            packets, groups = list(lax.optimization_barrier((*upcoming, hidden))[:shards]), ((0, 1, 2, 3),)
            inner, outer = send_rows(*edge_rows(packets, groups))
            packets[0] = after(packets[0], far)
        whole = lambda shape: pl.BlockSpec(shape, lambda f, *_: (0,) * len(shape))
        rows = pl.pallas_call(
            functools.partial(own_kernel, chunk=chunk, shards=shards),
            out_shape=jax.ShapeDtypeStruct((2, chunk.tokens, hidden_count), jnp.float32),
            in_specs=[VMEM] * (shards + 3),
            out_specs=VMEM,
            scratch_shapes=[pltpu.VMEM((chunk.tokens, full_depth), jnp.bfloat16)],
            compiler_params=pltpu.CompilerParams(vmem_limit_bytes=16 * MIB),
            cost_estimate=pl.CostEstimate(
                flops=1000,
                bytes_accessed=1000,
                transcendentals=0,
            ),
            name="expand_own",
        )(*packets, masks[number], parameters, weights)
        if number:
            inner[0] = after(inner[0], last_unit)
        hidden = pl.pallas_call(
            functools.partial(hidden_kernel, chunk=chunk, shards=shards, groups=groups),
            out_shape=jax.ShapeDtypeStruct((chunk.tokens, hidden_count), jnp.bfloat16),
            in_specs=[VMEM] * (2 * len(groups) + 4),
            out_specs=VMEM,
            scratch_shapes=[pltpu.VMEM((chunk.tokens, full_depth), jnp.bfloat16)],
            compiler_params=pltpu.CompilerParams(vmem_limit_bytes=16 * MIB),
            cost_estimate=pl.CostEstimate(
                flops=1000,
                bytes_accessed=1000,
                transcendentals=0,
            ),
            name="expand_conv",
        )(*inner, *outer, rows, masks[number], parameters, weights)

        weight_of = lambda j: pl.BlockSpec(
            (depth, hidden_count), lambda f, place, *_: (lax.bitwise_xor(place[0], j), 0)
        )
        cost = pl.CostEstimate(
            flops=2 * chunk.tokens * depth * hidden_count,
            bytes_accessed=2 * depth * hidden_count + 2 * chunk.tokens * hidden_count,
            transcendentals=0,
        )

        def unit(j, *added):
            return pl.pallas_call(
                functools.partial(unit_kernel, chunk=chunk),
                out_shape=jax.ShapeDtypeStruct(chunk.unit, jnp.bfloat16),
                grid_spec=pltpu.PrefetchScalarGridSpec(
                    num_scalar_prefetch=1,
                    grid=(1,),
                    in_specs=[weight_of(j), whole(hidden.shape)] + [whole(chunk.unit)] * len(added),
                    out_specs=whole(chunk.unit),
                ),
                compiler_params=pltpu.CompilerParams(vmem_limit_bytes=16 * MIB),
                cost_estimate=cost,
                name=f"project_{j}",
            )(me, project_turned, hidden, *added)

        if number:
            hidden = after(hidden, *arrived)
        far = unit(3)
        relayed = lax.ppermute(far, "tensor", from_end)
        across = lax.ppermute(far, "tensor", middle)
        close = unit(1)
        relayed, across = lax.optimization_barrier((relayed, across))
        last_unit = unit(2, relayed)
        arrived = [
            across,
            lax.ppermute(last_unit, "tensor", two_off),
            lax.ppermute(after(close, relayed), "tensor", near),
        ]
        extra = [] if out is None else [out]
        out = pl.pallas_call(
            functools.partial(final_kernel, chunk=chunk, sources=len(arrived)),
            out_shape=jax.ShapeDtypeStruct(latents.shape, jnp.bfloat16),
            grid_spec=pltpu.PrefetchScalarGridSpec(
                num_scalar_prefetch=2,
                grid=(1,),
                in_specs=[whole(masks[number].shape), weight_of(0), whole(hidden.shape)]
                + [whole(chunk.unit)] * len(arrived)
                + [whole(latents.shape)] * len(extra),
                out_specs=whole(latents.shape),
            ),
            compiler_params=pltpu.CompilerParams(vmem_limit_bytes=16 * MIB),
            cost_estimate=cost,
            name="finish",
        )(me, clip_width, masks[number], project_turned, hidden, *arrived, *extra)
    return out


def chunks_of(batch_size, col_count, depth):
    widths = slot_widths(batch_size, col_count)
    half = batch_size // 2
    return [Chunk(slots, widths, depth) for slots in (list(range(half)), list(range(half, batch_size)))]


def on_device(latents, clip_height, clip_width, expand_weight, *rest_of):
    batch_size, row_count, col_count, depth = latents.shape
    fits = (
        batch_size >= 2
        and row_count == 2
        and lax.axis_size("row") % 2 == 0
        and lax.axis_size("tensor") == 4
        and depth > LANES
        and (depth - LANES) % GROUP == 0
        and depth % GROUP == 0
        and all(
            c.block in (128, 256, 512) and c.kept % GROUP == 0 and c.left in (0, 64)
            for c in chunks_of(batch_size, col_count, depth)
        )
    )
    run = on_device_packed if fits else on_device_plain
    return run(latents, clip_height, clip_width, expand_weight, *rest_of)


def solution(mesh):
    in_specs = (
        P(None, "row", None, "tensor"),
        P(),
        P(),
        P(None, None, "tensor"),
        P(None, "tensor"),
        P(None, None, None, "tensor"),
        P(None, "tensor"),
        P("tensor", None),
    )
    out_specs = P(None, "row", None, "tensor")
    return jax.shard_map(
        on_device, mesh=mesh, in_specs=in_specs, out_specs=out_specs, check_vma=False
    )
```

```python
import functools

import jax
import jax.numpy as jnp
from jax import lax
from jax.experimental import pallas as pl
from jax.experimental.pallas import tpu as pltpu
from jax.sharding import PartitionSpec as P

LANES = 512
GROUP = 16
TILE = 256


def halo_rows(cells):
    count = lax.axis_size("row")
    ends = count - 1
    head = cells[:, :1]
    tail = cells[:, -1:]
    above = lax.ppermute(tail, "row", [(i, i + 1) for i in range(ends)])
    below = lax.ppermute(head, "row", [(i + 1, i) for i in range(ends)])
    return jnp.concatenate([above, cells, below], axis=1)


def depthwise(padded, depth_weight, depth_bias, row_count, col_count):
    widened = jnp.pad(padded, ((0, 0), (0, 0), (1, 1), (0, 0), (0, 0)))
    out_shape = (widened.shape[0], row_count, col_count) + widened.shape[3:]
    depth_out = jnp.zeros(out_shape, jnp.float32) + depth_bias
    for tap_row in range(3):
        for tap_col in range(3):
            depth_out = (
                depth_out
                + depth_weight[tap_row, tap_col]
                * widened[:, tap_row : tap_row + row_count, tap_col : tap_col + col_count]
            )
    return depth_out


def on_device_plain(
    latents,
    clip_height,
    clip_width,
    expand_weight,
    expand_bias,
    depth_weight,
    depth_bias,
    project_weight,
):
    batch_size, row_count, col_count, depth = latents.shape
    tokens = batch_size * row_count * col_count
    first_row = lax.axis_index("row") * row_count
    row_ids = first_row + jnp.arange(row_count, dtype=jnp.int32)
    col_ids = jnp.arange(col_count, dtype=jnp.int32)
    valid_mask = (
        (row_ids[None, :, None] < clip_height[:, None, None])
        & (col_ids[None, None, :] < clip_width[:, None, None])
    ).astype(jnp.float32)[..., None]
    channels = latents.reshape(tokens, depth).T
    gathered = lax.all_gather(channels, "tensor", axis=0, tiled=True)
    pre_act = jnp.einsum("dt,kdf->tkf", gathered, expand_weight, preferred_element_type=jnp.float32)
    pre_act = pre_act.reshape(batch_size, row_count, col_count, 2, -1)
    expanded = (jax.nn.silu(pre_act + expand_bias) * valid_mask[..., None]).astype(jnp.bfloat16)
    padded = halo_rows(expanded)
    depth_out = depthwise(padded, depth_weight, depth_bias, row_count, col_count)
    hidden = (depth_out[:, :, :, 0] * jax.nn.silu(depth_out[:, :, :, 1])).astype(jnp.bfloat16)
    partial_term = jnp.einsum(
        "tf,fd->dt", hidden.reshape(tokens, -1), project_weight, preferred_element_type=jnp.float32
    ).astype(jnp.bfloat16)
    summed = lax.psum_scatter(partial_term, "tensor", scatter_dimension=0, tiled=True)
    summed = summed.T.reshape(latents.shape).astype(jnp.float32)
    return (summed * valid_mask).astype(jnp.bfloat16)


def slot_clips(width_ref, batch_size):
    narrow, least = jnp.int32(0), width_ref[0]
    for b in range(1, batch_size):
        closer = width_ref[b] < least
        narrow = jnp.where(closer, b, narrow)
        least = jnp.where(closer, width_ref[b], least)
    return [jnp.where(narrow <= s, s + 1, s) for s in range(batch_size - 1)] + [narrow]


def slot_widths(batch_size, col_count):
    return [col_count] * (batch_size - 1) + [col_count // 2]


class Chunk:
    def __init__(self, slots, widths, depth):
        self.slots = slots
        self.widths = [widths[s] for s in slots]
        self.starts = [sum(self.widths[:i]) for i in range(len(slots))]
        self.kept = sum(self.widths)
        self.block = -(-self.kept // 128) * 128
        self.depth, self.rest = depth, depth - LANES
        across = LANES // self.block
        groups = self.rest // GROUP
        self.places = [(g // across * GROUP, g % across * self.block) for g in range(groups)]
        self.lines = self.kept + -(-groups // across) * GROUP
        self.tokens = 2 * self.kept
        self.full, self.left = self.tokens // 128, self.tokens % 128
        self.upper = -(-depth // (2 * GROUP)) * GROUP
        self.unit = (self.full * depth + (self.upper if self.left else 0), 128)

    def clips(self, width_ref, batch_size):
        order = slot_clips(width_ref, batch_size)
        return [order[s] for s in self.slots]

    def mask_column(self, height_ref, width_ref, row_id):
        pieces = []
        clips = self.clips(width_ref, width_ref.shape[0])
        for clip, width in zip(clips, self.widths):
            bound = jnp.where((row_id >= 0) & (row_id < height_ref[clip]), width_ref[clip], 0)
            col = lax.broadcasted_iota(jnp.int32, (width, 128), 0)
            pieces.append((col < bound).astype(jnp.float32))
        return jnp.concatenate(pieces, axis=0)

    def put_unit(self, unit_ref, sums):
        depth, at = self.depth, self.full * self.depth
        for b in range(self.full):
            unit_ref[b * depth : (b + 1) * depth, :] = sums[:, b * 128 : (b + 1) * 128]
        if self.left:
            tail = sums[:, self.full * 128 :]
            lower = depth - self.upper
            unit_ref[at : at + self.upper, : self.left] = tail[: self.upper]
            unit_ref[at : at + lower, self.left :] = tail[self.upper :]
            if lower < self.upper:
                unit_ref[at + lower :, self.left :] = jnp.zeros(
                    (self.upper - lower, 128 - self.left), sums.dtype
                )

    def get_unit(self, unit):
        depth, at = self.depth, self.full * self.depth
        blocks = [unit[b * depth : (b + 1) * depth, :] for b in range(self.full)]
        if self.left:
            lower = depth - self.upper
            blocks.append(
                jnp.concatenate(
                    [unit[at : at + self.upper, : self.left], unit[at : at + lower, self.left :]], axis=0
                )
            )
        return jnp.concatenate(blocks, axis=1)


def parity_of():
    return lax.rem(lax.axis_index("row"), 2)


def row_of(place, parity):
    return jnp.where(parity == 0, (-1, 0, 1, 2)[place], (2, 1, 0, -1)[place])


def silu(v):
    h = 0.5 * v
    return h + h * jnp.tanh(h)


def pack_kernel(height_ref, width_ref, x_ref, *refs, chunks):
    parity = parity_of()
    out_refs, mask_refs = refs[: len(chunks)], refs[len(chunks) :]
    for chunk, out_ref, mask_ref in zip(chunks, out_refs, mask_refs):
        for place in range(4):
            row_id = lax.axis_index("row") * 2 + row_of(place, parity)
            mask_ref[place] = chunk.mask_column(height_ref, width_ref, row_id)
        for place in range(2):
            row = jnp.where(parity == 0, 1 - place, place)
            tails = []
            for clip, width, at in zip(
                chunk.clips(width_ref, x_ref.shape[0]), chunk.widths, chunk.starts
            ):
                out_ref[place, at : at + width, :] = x_ref[clip, row, :width, :LANES]
                tails.append(x_ref[clip, row, :width, LANES:].astype(jnp.float32))
            if chunk.block > chunk.kept:
                tails.append(jnp.zeros((chunk.block - chunk.kept, chunk.rest), jnp.float32))
            turned = jnp.concatenate(tails, axis=0).T.astype(jnp.bfloat16)
            kept = chunk.kept
            out_ref[place, kept:, :] = jnp.zeros((chunk.lines - kept, LANES), jnp.bfloat16)
            for g, (down, over) in enumerate(chunk.places):
                out_ref[place, kept + down : kept + down + GROUP, over : over + chunk.block] = turned[
                    g * GROUP : (g + 1) * GROUP
                ]


def tiles_of(hidden_count):
    return [slice(at, min(at + TILE, hidden_count)) for at in range(0, hidden_count, TILE)]


def gather_rows(x_scr, chunk, rows):
    kept = chunk.kept
    for place, packets in enumerate(rows):
        lines = slice(place * kept, (place + 1) * kept)
        tails = []
        for j, packet in enumerate(packets):
            x_scr[lines, j * LANES : (j + 1) * LANES] = packet[:kept, :]
            for down, over in chunk.places:
                tails.append(packet[kept + down : kept + down + GROUP, over : over + chunk.block])
        turned = jnp.concatenate(tails, axis=0).astype(jnp.float32).T
        x_scr[lines, len(packets) * LANES :] = turned[:kept].astype(jnp.bfloat16)


def load_kernel(w_ref, out_ref, token_ref, sems, *, shards, depth):
    me = lax.axis_index("tensor")
    rest = depth - LANES
    copies = []
    for k in range(2):
        for j in range(shards):
            base = lax.bitwise_xor(me, j) * depth
            for part, (source, size, target) in enumerate(
                ((base, LANES, j * LANES), (base + LANES, rest, shards * LANES + j * rest))
            ):
                copies.append(
                    pltpu.make_async_copy(
                        w_ref.at[k, pl.ds(pl.multiple_of(source, GROUP), size)],
                        out_ref.at[k, pl.ds(target, size)],
                        sems.at[k, j, part],
                    )
                )
    for copy in copies:
        copy.start()
    token_ref[...] = jnp.zeros_like(token_ref)
    for copy in copies:
        copy.wait()


def expand(x_scr, w_ref, par_ref, k, units):
    pre_act = jnp.dot(x_scr[...], w_ref[k, :, units], preferred_element_type=jnp.float32)
    return silu(pre_act + par_ref[18 + k : 19 + k, units])


def masked(cells, mask):
    width = cells.shape[1]
    return cells * jnp.concatenate([mask] * -(-width // 128), axis=1)[:, :width]


def own_kernel(*refs, chunk, shards):
    packet_refs, (mask_ref, par_ref, w_ref, out_ref, x_scr) = refs[:shards], refs[shards:]
    kept = chunk.kept
    gather_rows(x_scr, chunk, [[p.at[1] for p in packet_refs], [p.at[0] for p in packet_refs]])
    mask = jnp.concatenate([mask_ref[1], mask_ref[2]], axis=0)
    for units in tiles_of(w_ref.shape[2]):
        for k in range(2):
            out_ref[k, :, units] = masked(expand(x_scr, w_ref, par_ref, k, units), mask)


def hidden_kernel(*refs, chunk, shards, groups):
    count = len(groups)
    inner_refs, outer_refs = refs[:count], refs[count : 2 * count]
    own_ref, mask_ref, par_ref, w_ref, out_ref, x_scr = refs[2 * count :]
    kept = chunk.kept
    parity = parity_of()
    spots = {j: (g, i) for g, js in enumerate(groups) for i, j in enumerate(js)}
    gather_rows(
        x_scr,
        chunk,
        [[refs_of[spots[j][0]].at[spots[j][1]] for j in range(shards)] for refs_of in (outer_refs, inner_refs)],
    )
    mask = jnp.concatenate([mask_ref[0], mask_ref[3]], axis=0)

    def around(units):
        return [
            masked(expand(x_scr, w_ref, par_ref, k, units), mask) for k in range(2)
        ]

    def convolve(units, cells):
        width = units.stop - units.start
        line = lax.broadcasted_iota(jnp.int32, (kept, width), 0)
        not_first, not_last = None, None
        for at, size in zip(chunk.starts, chunk.widths):
            first, last = line != at, line != at + size - 1
            not_first = first if not_first is None else not_first & first
            not_last = last if not_last is None else not_last & last
        halves = ([], [])
        for k in range(2):
            rows = [
                cells[k][:kept],
                own_ref[k, :kept, units],
                own_ref[k, kept:, units],
                cells[k][kept:],
            ]
            taps = [
                [
                    jnp.where(
                        parity == 0,
                        par_ref[i * 6 + col * 2 + k : i * 6 + col * 2 + k + 1, units],
                        par_ref[(2 - i) * 6 + col * 2 + k : (2 - i) * 6 + col * 2 + k + 1, units],
                    )
                    for col in range(3)
                ]
                for i in range(3)
            ]
            for place in range(2):
                sums = []
                for tap_col in range(3):
                    total = None
                    for i in range(3):
                        term = taps[i][tap_col] * rows[place + i]
                        total = term if total is None else total + term
                    sums.append(total)
                left = jnp.where(not_first, pltpu.roll(sums[0], 1, 0), 0.0)
                right = jnp.where(not_last, pltpu.roll(sums[2], kept - 1, 0), 0.0)
                halves[k].append(sums[1] + left + right + par_ref[20 + k : 21 + k, units])
        for place in range(2):
            hidden = halves[0][place] * silu(halves[1][place])
            out_ref[(1 - place) * kept : (2 - place) * kept, units] = hidden.astype(jnp.bfloat16)

    tiles = tiles_of(w_ref.shape[2])
    cells = around(tiles[0])
    for t, units in enumerate(tiles):
        coming = around(tiles[t + 1]) if t + 1 < len(tiles) else None
        convolve(units, cells)
        cells = coming


def project(weight_ref, hidden_ref, depth, j):
    start = lax.bitwise_xor(lax.axis_index("tensor"), j) * depth
    return lax.dot_general(
        weight_ref[pl.ds(pl.multiple_of(start, GROUP), depth), :],
        hidden_ref[...],
        (((1,), (1,)), ((), ())),
        preferred_element_type=jnp.float32,
    )


def unit_kernel(weight_ref, hidden_ref, *refs, chunk, j):
    out_ref = refs[-1]
    sums = project(weight_ref, hidden_ref, chunk.depth, j)
    for ref in refs[:-1]:
        sums = sums + chunk.get_unit(ref[...].astype(jnp.float32))
    chunk.put_unit(out_ref, sums.astype(jnp.bfloat16))


def final_kernel(width_ref, mask_ref, weight_ref, hidden_ref, *refs, chunk, sources):
    out_ref = refs[-1]
    if len(refs) > sources + 1:
        out_ref[...] = refs[sources][...]
    sums = project(weight_ref, hidden_ref, chunk.depth, 0)
    for ref in refs[:sources]:
        sums = sums + chunk.get_unit(ref[...].astype(jnp.float32))
    cells = sums.T
    parity = parity_of()
    for place in range(2):
        row = jnp.where(parity == 0, 1 - place, place)
        mask = mask_ref[2 - place][:, :1] > 0
        part = cells[place * chunk.kept : (place + 1) * chunk.kept]
        part = jnp.where(mask, part, 0.0).astype(jnp.bfloat16)
        clips = chunk.clips(width_ref, width_ref.shape[0])
        for clip, width, at in zip(clips, chunk.widths, chunk.starts):
            out_ref[clip, row, :width, :] = part[at : at + width]
            if width < out_ref.shape[2]:
                blank = jnp.zeros((out_ref.shape[2] - width, chunk.depth), jnp.bfloat16)
                out_ref[clip, row, width:, :] = blank


VMEM = pl.BlockSpec(memory_space=pltpu.VMEM)
MIB = 1024 * 1024


def after(value, *others):
    return lax.optimization_barrier((value,) + others)[0]


def on_device_packed(
    latents,
    clip_height,
    clip_width,
    expand_weight,
    expand_bias,
    depth_weight,
    depth_bias,
    project_weight,
):
    batch_size, row_count, col_count, depth = latents.shape
    shards, row_devices = lax.axis_size("tensor"), lax.axis_size("row")
    hidden_count = expand_weight.shape[2]
    full_depth = shards * depth
    chunks = chunks_of(batch_size, col_count, depth)
    count = len(chunks)
    packed = pl.pallas_call(
        functools.partial(pack_kernel, chunks=chunks),
        out_shape=[jax.ShapeDtypeStruct((2, c.lines, LANES), jnp.bfloat16) for c in chunks]
        + [jax.ShapeDtypeStruct((4, c.kept, 128), jnp.float32) for c in chunks],
        grid_spec=pltpu.PrefetchScalarGridSpec(
            num_scalar_prefetch=2, grid=(), in_specs=[VMEM], out_specs=[VMEM] * (2 * count)
        ),
        compiler_params=pltpu.CompilerParams(vmem_limit_bytes=16 * MIB),
        name="pack",
    )(clip_height, clip_width, latents)
    own, masks = packed[:count], packed[count:]
    parameters = jnp.concatenate(
        [depth_weight.reshape(18, hidden_count), expand_bias, depth_bias], axis=0
    )
    project_turned = project_weight.T

    sibling = [(i, i ^ 1) for i in range(row_devices)]
    beyond = [(i, i + 1) for i in range(1, row_devices - 1, 2)]
    beyond = beyond + [(b, a) for a, b in beyond]
    near = [(i, i ^ 1) for i in range(4)]
    two_off = [(i, i ^ 2) for i in range(4)]
    middle = [(1, 2), (2, 1)]
    to_end = [(2, 3), (1, 0)]
    from_end = [(0, 1), (3, 2)]

    def edge_rows(packets, groups):
        return [
            [jnp.concatenate([packets[j][side : side + 1] for j in js], axis=0) for js in groups]
            for side in range(2)
        ]

    def send_rows(inner, outer):
        return (
            [lax.ppermute(x, "row", sibling) for x in inner],
            [lax.ppermute(x, "row", beyond) for x in outer],
        )

    def relay(mine, token):
        second = lax.ppermute(mine, "tensor", two_off)
        first = lax.ppermute(mine, "tensor", near)
        across = lax.ppermute(after(mine, second, token), "tensor", middle)
        passed = lax.ppermute(after(second, token), "tensor", to_end)
        return [mine, first, second, across + passed]

    def direct(mine):
        return [mine] + [
            lax.ppermute(mine, "tensor", [(i, i ^ j) for i in range(4)]) for j in range(1, 4)
        ]

    out = None
    weights, token = pl.pallas_call(
        functools.partial(load_kernel, shards=shards, depth=depth),
        out_shape=[
            jax.ShapeDtypeStruct(expand_weight.shape, jnp.bfloat16),
            jax.ShapeDtypeStruct((8, 128), jnp.float32),
        ],
        in_specs=[pl.BlockSpec(memory_space=pl.ANY)],
        out_specs=[VMEM, VMEM],
        scratch_shapes=[pltpu.SemaphoreType.DMA((2, shards, 2))],
        compiler_params=pltpu.CompilerParams(vmem_limit_bytes=36 * MIB),
        name="load_weights",
    )(after(expand_weight, own[0]))
    packets = relay(own[0], token)
    groups = ((0, 1, 2), (3,))
    edges = edge_rows(packets, groups)
    inner, outer = send_rows(*edges)
    upcoming = direct(after(own[1], edges[0][-1], edges[1][-1]))
    for number, chunk in enumerate(chunks):
        if number:
            packets, groups = list(lax.optimization_barrier((*upcoming, hidden))[:shards]), ((0, 1, 2, 3),)
            inner, outer = send_rows(*edge_rows(packets, groups))
            packets[0] = after(packets[0], far)
        rows = pl.pallas_call(
            functools.partial(own_kernel, chunk=chunk, shards=shards),
            out_shape=jax.ShapeDtypeStruct((2, chunk.tokens, hidden_count), jnp.float32),
            in_specs=[VMEM] * (shards + 3),
            out_specs=VMEM,
            scratch_shapes=[pltpu.VMEM((chunk.tokens, full_depth), jnp.bfloat16)],
            compiler_params=pltpu.CompilerParams(vmem_limit_bytes=16 * MIB),
            cost_estimate=pl.CostEstimate(
                flops=1000,
                bytes_accessed=1000,
                transcendentals=0,
            ),
            name="expand_own",
        )(*packets, masks[number], parameters, weights)
        if number:
            inner[0] = after(inner[0], last_unit)
        hidden = pl.pallas_call(
            functools.partial(hidden_kernel, chunk=chunk, shards=shards, groups=groups),
            out_shape=jax.ShapeDtypeStruct((chunk.tokens, hidden_count), jnp.bfloat16),
            in_specs=[VMEM] * (2 * len(groups) + 4),
            out_specs=VMEM,
            scratch_shapes=[pltpu.VMEM((chunk.tokens, full_depth), jnp.bfloat16)],
            compiler_params=pltpu.CompilerParams(vmem_limit_bytes=16 * MIB),
            cost_estimate=pl.CostEstimate(
                flops=1000,
                bytes_accessed=1000,
                transcendentals=0,
            ),
            name="expand_conv",
        )(*inner, *outer, rows, masks[number], parameters, weights)

        cost = pl.CostEstimate(
            flops=2 * chunk.tokens * depth * hidden_count,
            bytes_accessed=2 * depth * hidden_count + 2 * chunk.tokens * hidden_count,
            transcendentals=0,
        )

        def unit(j, *added):
            return pl.pallas_call(
                functools.partial(unit_kernel, chunk=chunk, j=j),
                out_shape=jax.ShapeDtypeStruct(chunk.unit, jnp.bfloat16),
                in_specs=[VMEM] * (2 + len(added)),
                out_specs=VMEM,
                compiler_params=pltpu.CompilerParams(vmem_limit_bytes=16 * MIB),
                cost_estimate=cost,
                name=f"project_{j}",
            )(project_turned, hidden, *added)

        if number:
            hidden = after(hidden, *arrived)
        far = unit(3)
        relayed = lax.ppermute(far, "tensor", from_end)
        across = lax.ppermute(far, "tensor", middle)
        close = unit(1)
        relayed, across = lax.optimization_barrier((relayed, across))
        last_unit = unit(2, relayed)
        arrived = [
            across,
            lax.ppermute(last_unit, "tensor", two_off),
            lax.ppermute(after(close, relayed), "tensor", near),
        ]
        extra = [] if out is None else [out]
        out = pl.pallas_call(
            functools.partial(final_kernel, chunk=chunk, sources=len(arrived)),
            out_shape=jax.ShapeDtypeStruct(latents.shape, jnp.bfloat16),
            grid_spec=pltpu.PrefetchScalarGridSpec(
                num_scalar_prefetch=1,
                grid=(),
                in_specs=[VMEM] * (3 + len(arrived) + len(extra)),
                out_specs=VMEM,
            ),
            compiler_params=pltpu.CompilerParams(vmem_limit_bytes=16 * MIB),
            cost_estimate=cost,
            name="finish",
        )(clip_width, masks[number], project_turned, hidden, *arrived, *extra)
    return out


def chunks_of(batch_size, col_count, depth):
    widths = slot_widths(batch_size, col_count)
    half = batch_size // 2
    return [Chunk(slots, widths, depth) for slots in (list(range(half)), list(range(half, batch_size)))]


def on_device(latents, clip_height, clip_width, expand_weight, *rest_of):
    batch_size, row_count, col_count, depth = latents.shape
    fits = (
        batch_size >= 2
        and row_count == 2
        and lax.axis_size("row") % 2 == 0
        and lax.axis_size("tensor") == 4
        and depth > LANES
        and (depth - LANES) % GROUP == 0
        and depth % GROUP == 0
        and all(
            c.block in (128, 256, 512) and c.kept % GROUP == 0 and c.left in (0, 64)
            for c in chunks_of(batch_size, col_count, depth)
        )
    )
    run = on_device_packed if fits else on_device_plain
    return run(latents, clip_height, clip_width, expand_weight, *rest_of)


def solution(mesh):
    in_specs = (
        P(None, "row", None, "tensor"),
        P(),
        P(),
        P(None, None, "tensor"),
        P(None, "tensor"),
        P(None, None, None, "tensor"),
        P(None, "tensor"),
        P("tensor", None),
    )
    out_specs = P(None, "row", None, "tensor")
    return jax.shard_map(
        on_device, mesh=mesh, in_specs=in_specs, out_specs=out_specs, check_vma=False
    )
```

```python
import functools

import jax
import jax.numpy as jnp
from jax import lax
from jax.experimental import pallas as pl
from jax.experimental.pallas import tpu as pltpu
from jax.sharding import PartitionSpec as P

LANES = 512
GROUP = 16
TILE = 256


def halo_rows(cells):
    count = lax.axis_size("row")
    ends = count - 1
    head = cells[:, :1]
    tail = cells[:, -1:]
    above = lax.ppermute(tail, "row", [(i, i + 1) for i in range(ends)])
    below = lax.ppermute(head, "row", [(i + 1, i) for i in range(ends)])
    return jnp.concatenate([above, cells, below], axis=1)


def depthwise(padded, depth_weight, depth_bias, row_count, col_count):
    widened = jnp.pad(padded, ((0, 0), (0, 0), (1, 1), (0, 0), (0, 0)))
    out_shape = (widened.shape[0], row_count, col_count) + widened.shape[3:]
    depth_out = jnp.zeros(out_shape, jnp.float32) + depth_bias
    for tap_row in range(3):
        for tap_col in range(3):
            depth_out = (
                depth_out
                + depth_weight[tap_row, tap_col]
                * widened[:, tap_row : tap_row + row_count, tap_col : tap_col + col_count]
            )
    return depth_out


def on_device_plain(
    latents,
    clip_height,
    clip_width,
    expand_weight,
    expand_bias,
    depth_weight,
    depth_bias,
    project_weight,
):
    batch_size, row_count, col_count, depth = latents.shape
    tokens = batch_size * row_count * col_count
    first_row = lax.axis_index("row") * row_count
    row_ids = first_row + jnp.arange(row_count, dtype=jnp.int32)
    col_ids = jnp.arange(col_count, dtype=jnp.int32)
    valid_mask = (
        (row_ids[None, :, None] < clip_height[:, None, None])
        & (col_ids[None, None, :] < clip_width[:, None, None])
    ).astype(jnp.float32)[..., None]
    channels = latents.reshape(tokens, depth).T
    gathered = lax.all_gather(channels, "tensor", axis=0, tiled=True)
    pre_act = jnp.einsum("dt,kdf->tkf", gathered, expand_weight, preferred_element_type=jnp.float32)
    pre_act = pre_act.reshape(batch_size, row_count, col_count, 2, -1)
    expanded = (jax.nn.silu(pre_act + expand_bias) * valid_mask[..., None]).astype(jnp.bfloat16)
    padded = halo_rows(expanded)
    depth_out = depthwise(padded, depth_weight, depth_bias, row_count, col_count)
    hidden = (depth_out[:, :, :, 0] * jax.nn.silu(depth_out[:, :, :, 1])).astype(jnp.bfloat16)
    partial_term = jnp.einsum(
        "tf,fd->dt", hidden.reshape(tokens, -1), project_weight, preferred_element_type=jnp.float32
    ).astype(jnp.bfloat16)
    summed = lax.psum_scatter(partial_term, "tensor", scatter_dimension=0, tiled=True)
    summed = summed.T.reshape(latents.shape).astype(jnp.float32)
    return (summed * valid_mask).astype(jnp.bfloat16)


def slot_clips(width_ref, batch_size):
    narrow, least = jnp.int32(0), width_ref[0]
    for b in range(1, batch_size):
        closer = width_ref[b] < least
        narrow = jnp.where(closer, b, narrow)
        least = jnp.where(closer, width_ref[b], least)
    return [jnp.where(narrow <= s, s + 1, s) for s in range(batch_size - 1)] + [narrow]


def slot_widths(batch_size, col_count):
    return [col_count] * (batch_size - 1) + [col_count // 2]


class Chunk:
    def __init__(self, slots, widths, depth):
        self.slots = slots
        self.widths = [widths[s] for s in slots]
        self.starts = [sum(self.widths[:i]) for i in range(len(slots))]
        self.kept = sum(self.widths)
        self.block = -(-self.kept // 128) * 128
        self.depth, self.rest = depth, depth - LANES
        across = LANES // self.block
        groups = self.rest // GROUP
        self.places = [(g // across * GROUP, g % across * self.block) for g in range(groups)]
        self.lines = self.kept + -(-groups // across) * GROUP
        self.tokens = 2 * self.kept
        self.full, self.left = self.tokens // 128, self.tokens % 128
        self.upper = -(-depth // (2 * GROUP)) * GROUP
        self.unit = (self.full * depth + (self.upper if self.left else 0), 128)

    def clips(self, width_ref, batch_size):
        order = slot_clips(width_ref, batch_size)
        return [order[s] for s in self.slots]

    def mask_column(self, height_ref, width_ref, row_id):
        pieces = []
        clips = self.clips(width_ref, width_ref.shape[0])
        for clip, width in zip(clips, self.widths):
            bound = jnp.where((row_id >= 0) & (row_id < height_ref[clip]), width_ref[clip], 0)
            col = lax.broadcasted_iota(jnp.int32, (width, 128), 0)
            pieces.append((col < bound).astype(jnp.float32))
        return jnp.concatenate(pieces, axis=0)

    def put_unit(self, unit_ref, sums):
        depth, at = self.depth, self.full * self.depth
        for b in range(self.full):
            unit_ref[b * depth : (b + 1) * depth, :] = sums[:, b * 128 : (b + 1) * 128]
        if self.left:
            tail = sums[:, self.full * 128 :]
            lower = depth - self.upper
            unit_ref[at : at + self.upper, : self.left] = tail[: self.upper]
            unit_ref[at : at + lower, self.left :] = tail[self.upper :]
            if lower < self.upper:
                unit_ref[at + lower :, self.left :] = jnp.zeros(
                    (self.upper - lower, 128 - self.left), sums.dtype
                )

    def get_unit(self, unit):
        depth, at = self.depth, self.full * self.depth
        blocks = [unit[b * depth : (b + 1) * depth, :] for b in range(self.full)]
        if self.left:
            lower = depth - self.upper
            blocks.append(
                jnp.concatenate(
                    [unit[at : at + self.upper, : self.left], unit[at : at + lower, self.left :]], axis=0
                )
            )
        return jnp.concatenate(blocks, axis=1)


def parity_of():
    return lax.rem(lax.axis_index("row"), 2)


def row_of(place, parity):
    return jnp.where(parity == 0, (-1, 0, 1, 2)[place], (2, 1, 0, -1)[place])


def silu(v):
    h = 0.5 * v
    return h + h * jnp.tanh(h)


def pack_kernel(height_ref, width_ref, x_ref, *refs, chunks):
    parity = parity_of()
    out_refs, mask_refs = refs[: len(chunks)], refs[len(chunks) :]
    for chunk, out_ref, mask_ref in zip(chunks, out_refs, mask_refs):
        for place in range(4):
            row_id = lax.axis_index("row") * 2 + row_of(place, parity)
            mask_ref[place] = chunk.mask_column(height_ref, width_ref, row_id)
        for place in range(2):
            row = jnp.where(parity == 0, 1 - place, place)
            tails = []
            for clip, width, at in zip(
                chunk.clips(width_ref, x_ref.shape[0]), chunk.widths, chunk.starts
            ):
                out_ref[place, at : at + width, :] = x_ref[clip, row, :width, :LANES]
                tails.append(x_ref[clip, row, :width, LANES:].astype(jnp.float32))
            if chunk.block > chunk.kept:
                tails.append(jnp.zeros((chunk.block - chunk.kept, chunk.rest), jnp.float32))
            turned = jnp.concatenate(tails, axis=0).T.astype(jnp.bfloat16)
            kept = chunk.kept
            out_ref[place, kept:, :] = jnp.zeros((chunk.lines - kept, LANES), jnp.bfloat16)
            for g, (down, over) in enumerate(chunk.places):
                out_ref[place, kept + down : kept + down + GROUP, over : over + chunk.block] = turned[
                    g * GROUP : (g + 1) * GROUP
                ]


def tiles_of(hidden_count):
    return [slice(at, min(at + TILE, hidden_count)) for at in range(0, hidden_count, TILE)]


def gather_rows(x_scr, chunk, rows):
    kept = chunk.kept
    for place, packets in enumerate(rows):
        lines = slice(place * kept, (place + 1) * kept)
        tails = []
        for j, packet in enumerate(packets):
            x_scr[lines, j * LANES : (j + 1) * LANES] = packet[:kept, :]
            for down, over in chunk.places:
                tails.append(packet[kept + down : kept + down + GROUP, over : over + chunk.block])
        turned = jnp.concatenate(tails, axis=0).astype(jnp.float32).T
        x_scr[lines, len(packets) * LANES :] = turned[:kept].astype(jnp.bfloat16)


def load_kernel(dw_ref, eb_ref, db_ref, w_ref, out_ref, par_ref, sems, *, shards, depth):
    me = lax.axis_index("tensor")
    rest = depth - LANES
    copies = []
    for k in range(2):
        for j in range(shards):
            base = lax.bitwise_xor(me, j) * depth
            for part, (source, size, target) in enumerate(
                ((base, LANES, j * LANES), (base + LANES, rest, shards * LANES + j * rest))
            ):
                copies.append(
                    pltpu.make_async_copy(
                        w_ref.at[k, pl.ds(pl.multiple_of(source, GROUP), size)],
                        out_ref.at[k, pl.ds(target, size)],
                        sems.at[k, j, part],
                    )
                )
    for copy in copies:
        copy.start()
    for i in range(3):
        for col in range(3):
            par_ref[i * 6 + col * 2 : i * 6 + col * 2 + 2, :] = dw_ref[i, col]
    par_ref[18:20, :] = eb_ref[...]
    par_ref[20:22, :] = db_ref[...]
    for copy in copies:
        copy.wait()


def expand(x_scr, w_ref, par_ref, k, units):
    pre_act = jnp.dot(x_scr[...], w_ref[k, :, units], preferred_element_type=jnp.float32)
    return silu(pre_act + par_ref[18 + k : 19 + k, units])


def masked(cells, mask):
    width = cells.shape[1]
    return cells * jnp.concatenate([mask] * -(-width // 128), axis=1)[:, :width]


def own_kernel(*refs, chunk, shards):
    packet_refs, (mask_ref, par_ref, w_ref, out_ref, x_scr) = refs[:shards], refs[shards:]
    kept = chunk.kept
    gather_rows(x_scr, chunk, [[p.at[1] for p in packet_refs], [p.at[0] for p in packet_refs]])
    mask = jnp.concatenate([mask_ref[1], mask_ref[2]], axis=0)
    for units in tiles_of(w_ref.shape[2]):
        for k in range(2):
            out_ref[k, :, units] = masked(expand(x_scr, w_ref, par_ref, k, units), mask)


def hidden_kernel(*refs, chunk, shards, groups):
    count = len(groups)
    inner_refs, outer_refs = refs[:count], refs[count : 2 * count]
    own_ref, mask_ref, par_ref, w_ref, out_ref, x_scr = refs[2 * count :]
    kept = chunk.kept
    parity = parity_of()
    spots = {j: (g, i) for g, js in enumerate(groups) for i, j in enumerate(js)}
    gather_rows(
        x_scr,
        chunk,
        [[refs_of[spots[j][0]].at[spots[j][1]] for j in range(shards)] for refs_of in (outer_refs, inner_refs)],
    )
    mask = jnp.concatenate([mask_ref[0], mask_ref[3]], axis=0)

    def around(units):
        return [
            masked(expand(x_scr, w_ref, par_ref, k, units), mask) for k in range(2)
        ]

    def convolve(units, cells):
        width = units.stop - units.start
        line = lax.broadcasted_iota(jnp.int32, (kept, width), 0)
        not_first, not_last = None, None
        for at, size in zip(chunk.starts, chunk.widths):
            first, last = line != at, line != at + size - 1
            not_first = first if not_first is None else not_first & first
            not_last = last if not_last is None else not_last & last
        halves = ([], [])
        for k in range(2):
            rows = [
                cells[k][:kept],
                own_ref[k, :kept, units],
                own_ref[k, kept:, units],
                cells[k][kept:],
            ]
            taps = [
                [
                    jnp.where(
                        parity == 0,
                        par_ref[i * 6 + col * 2 + k : i * 6 + col * 2 + k + 1, units],
                        par_ref[(2 - i) * 6 + col * 2 + k : (2 - i) * 6 + col * 2 + k + 1, units],
                    )
                    for col in range(3)
                ]
                for i in range(3)
            ]
            for place in range(2):
                sums = []
                for tap_col in range(3):
                    total = None
                    for i in range(3):
                        term = taps[i][tap_col] * rows[place + i]
                        total = term if total is None else total + term
                    sums.append(total)
                left = jnp.where(not_first, pltpu.roll(sums[0], 1, 0), 0.0)
                right = jnp.where(not_last, pltpu.roll(sums[2], kept - 1, 0), 0.0)
                halves[k].append(sums[1] + left + right + par_ref[20 + k : 21 + k, units])
        for place in range(2):
            hidden = halves[0][place] * silu(halves[1][place])
            out_ref[(1 - place) * kept : (2 - place) * kept, units] = hidden.astype(jnp.bfloat16)

    tiles = tiles_of(w_ref.shape[2])
    cells = around(tiles[0])
    for t, units in enumerate(tiles):
        coming = around(tiles[t + 1]) if t + 1 < len(tiles) else None
        convolve(units, cells)
        cells = coming


def project(weight_ref, hidden_ref, depth, j):
    start = lax.bitwise_xor(lax.axis_index("tensor"), j) * depth
    return lax.dot_general(
        weight_ref[pl.ds(pl.multiple_of(start, GROUP), depth), :],
        hidden_ref[...],
        (((1,), (1,)), ((), ())),
        preferred_element_type=jnp.float32,
    )


def unit_kernel(weight_ref, hidden_ref, *refs, chunk, j):
    out_ref = refs[-1]
    sums = project(weight_ref, hidden_ref, chunk.depth, j)
    for ref in refs[:-1]:
        sums = sums + chunk.get_unit(ref[...].astype(jnp.float32))
    chunk.put_unit(out_ref, sums.astype(jnp.bfloat16))


def final_kernel(width_ref, mask_ref, weight_ref, hidden_ref, *refs, chunk, sources):
    out_ref = refs[-1]
    if len(refs) > sources + 1:
        out_ref[...] = refs[sources][...]
    sums = project(weight_ref, hidden_ref, chunk.depth, 0)
    for ref in refs[:sources]:
        sums = sums + chunk.get_unit(ref[...].astype(jnp.float32))
    cells = sums.T
    parity = parity_of()
    for place in range(2):
        row = jnp.where(parity == 0, 1 - place, place)
        mask = mask_ref[2 - place][:, :1] > 0
        part = cells[place * chunk.kept : (place + 1) * chunk.kept]
        part = jnp.where(mask, part, 0.0).astype(jnp.bfloat16)
        clips = chunk.clips(width_ref, width_ref.shape[0])
        for clip, width, at in zip(clips, chunk.widths, chunk.starts):
            out_ref[clip, row, :width, :] = part[at : at + width]
            if width < out_ref.shape[2]:
                blank = jnp.zeros((out_ref.shape[2] - width, chunk.depth), jnp.bfloat16)
                out_ref[clip, row, width:, :] = blank


VMEM = pl.BlockSpec(memory_space=pltpu.VMEM)
MIB = 1024 * 1024


def after(value, *others):
    return lax.optimization_barrier((value,) + others)[0]


def on_device_packed(
    latents,
    clip_height,
    clip_width,
    expand_weight,
    expand_bias,
    depth_weight,
    depth_bias,
    project_weight,
):
    batch_size, row_count, col_count, depth = latents.shape
    shards, row_devices = lax.axis_size("tensor"), lax.axis_size("row")
    hidden_count = expand_weight.shape[2]
    full_depth = shards * depth
    chunks = chunks_of(batch_size, col_count, depth)
    count = len(chunks)
    packed = pl.pallas_call(
        functools.partial(pack_kernel, chunks=chunks),
        out_shape=[jax.ShapeDtypeStruct((2, c.lines, LANES), jnp.bfloat16) for c in chunks]
        + [jax.ShapeDtypeStruct((4, c.kept, 128), jnp.float32) for c in chunks],
        grid_spec=pltpu.PrefetchScalarGridSpec(
            num_scalar_prefetch=2, grid=(), in_specs=[VMEM], out_specs=[VMEM] * (2 * count)
        ),
        compiler_params=pltpu.CompilerParams(vmem_limit_bytes=16 * MIB),
        name="pack",
    )(clip_height, clip_width, latents)
    own, masks = packed[:count], packed[count:]
    project_turned = project_weight.T

    sibling = [(i, i ^ 1) for i in range(row_devices)]
    beyond = [(i, i + 1) for i in range(1, row_devices - 1, 2)]
    beyond = beyond + [(b, a) for a, b in beyond]
    near = [(i, i ^ 1) for i in range(4)]
    two_off = [(i, i ^ 2) for i in range(4)]
    middle = [(1, 2), (2, 1)]
    to_end = [(2, 3), (1, 0)]
    from_end = [(0, 1), (3, 2)]

    def edge_rows(packets, groups):
        return [
            [jnp.concatenate([packets[j][side : side + 1] for j in js], axis=0) for js in groups]
            for side in range(2)
        ]

    def send_rows(inner, outer):
        return (
            [lax.ppermute(x, "row", sibling) for x in inner],
            [lax.ppermute(x, "row", beyond) for x in outer],
        )

    def relay(mine, *others):
        second = lax.ppermute(mine, "tensor", two_off)
        first = lax.ppermute(mine, "tensor", near)
        across = lax.ppermute(after(mine, second, *others), "tensor", middle)
        passed = lax.ppermute(after(second, *others), "tensor", to_end)
        return [mine, first, second, across + passed]

    def direct(mine):
        return [mine] + [
            lax.ppermute(mine, "tensor", [(i, i ^ j) for i in range(4)]) for j in range(1, 4)
        ]

    out = None
    weights, parameters = pl.pallas_call(
        functools.partial(load_kernel, shards=shards, depth=depth),
        out_shape=[
            jax.ShapeDtypeStruct(expand_weight.shape, jnp.bfloat16),
            jax.ShapeDtypeStruct((22, hidden_count), jnp.float32),
        ],
        in_specs=[VMEM] * 3 + [pl.BlockSpec(memory_space=pl.ANY)],
        out_specs=[VMEM, VMEM],
        scratch_shapes=[pltpu.SemaphoreType.DMA((2, shards, 2))],
        compiler_params=pltpu.CompilerParams(vmem_limit_bytes=36 * MIB),
        name="load_weights",
    )(depth_weight, expand_bias, depth_bias, after(expand_weight, own[0]))
    groups = ((0,), (1, 2), (3,))
    inner, outer = send_rows(*edge_rows(own[:1], groups[:1]))
    packets = relay(own[0], parameters, *inner, *outer)
    edges = edge_rows(packets, groups[1:])
    later = send_rows(*edges)
    inner, outer = inner + later[0], outer + later[1]
    upcoming = direct(after(own[1], edges[0][-1], edges[1][-1]))
    for number, chunk in enumerate(chunks):
        if number:
            packets, groups = list(lax.optimization_barrier((*upcoming, hidden))[:shards]), ((0, 1, 2, 3),)
            inner, outer = send_rows(*edge_rows(packets, groups))
            packets[0] = after(packets[0], far)
        rows = pl.pallas_call(
            functools.partial(own_kernel, chunk=chunk, shards=shards),
            out_shape=jax.ShapeDtypeStruct((2, chunk.tokens, hidden_count), jnp.float32),
            in_specs=[VMEM] * (shards + 3),
            out_specs=VMEM,
            scratch_shapes=[pltpu.VMEM((chunk.tokens, full_depth), jnp.bfloat16)],
            compiler_params=pltpu.CompilerParams(vmem_limit_bytes=16 * MIB),
            cost_estimate=pl.CostEstimate(
                flops=1000,
                bytes_accessed=1000,
                transcendentals=0,
            ),
            name="expand_own",
        )(*packets, masks[number], parameters, weights)
        if number:
            inner[0] = after(inner[0], last_unit)
        hidden = pl.pallas_call(
            functools.partial(hidden_kernel, chunk=chunk, shards=shards, groups=groups),
            out_shape=jax.ShapeDtypeStruct((chunk.tokens, hidden_count), jnp.bfloat16),
            in_specs=[VMEM] * (2 * len(groups) + 4),
            out_specs=VMEM,
            scratch_shapes=[pltpu.VMEM((chunk.tokens, full_depth), jnp.bfloat16)],
            compiler_params=pltpu.CompilerParams(vmem_limit_bytes=16 * MIB),
            cost_estimate=pl.CostEstimate(
                flops=1000,
                bytes_accessed=1000,
                transcendentals=0,
            ),
            name="expand_conv",
        )(*inner, *outer, rows, masks[number], parameters, weights)

        cost = pl.CostEstimate(
            flops=2 * chunk.tokens * depth * hidden_count,
            bytes_accessed=2 * depth * hidden_count + 2 * chunk.tokens * hidden_count,
            transcendentals=0,
        )

        def unit(j, *added):
            return pl.pallas_call(
                functools.partial(unit_kernel, chunk=chunk, j=j),
                out_shape=jax.ShapeDtypeStruct(chunk.unit, jnp.bfloat16),
                in_specs=[VMEM] * (2 + len(added)),
                out_specs=VMEM,
                compiler_params=pltpu.CompilerParams(vmem_limit_bytes=16 * MIB),
                cost_estimate=cost,
                name=f"project_{j}",
            )(project_turned, hidden, *added)

        if number:
            hidden = after(hidden, *arrived)
        far = unit(3)
        relayed = lax.ppermute(far, "tensor", from_end)
        across = lax.ppermute(far, "tensor", middle)
        close = unit(1)
        relayed, across = lax.optimization_barrier((relayed, across))
        last_unit = unit(2, relayed)
        arrived = [
            across,
            lax.ppermute(last_unit, "tensor", two_off),
            lax.ppermute(after(close, relayed), "tensor", near),
        ]
        extra = [] if out is None else [out]
        out = pl.pallas_call(
            functools.partial(final_kernel, chunk=chunk, sources=len(arrived)),
            out_shape=jax.ShapeDtypeStruct(latents.shape, jnp.bfloat16),
            grid_spec=pltpu.PrefetchScalarGridSpec(
                num_scalar_prefetch=1,
                grid=(),
                in_specs=[VMEM] * (3 + len(arrived) + len(extra)),
                out_specs=VMEM,
            ),
            compiler_params=pltpu.CompilerParams(vmem_limit_bytes=16 * MIB),
            cost_estimate=cost,
            name="finish",
        )(clip_width, masks[number], project_turned, hidden, *arrived, *extra)
    return out


def chunks_of(batch_size, col_count, depth):
    widths = slot_widths(batch_size, col_count)
    half = batch_size // 2
    return [Chunk(slots, widths, depth) for slots in (list(range(half)), list(range(half, batch_size)))]


def on_device(latents, clip_height, clip_width, expand_weight, *rest_of):
    batch_size, row_count, col_count, depth = latents.shape
    fits = (
        batch_size >= 2
        and row_count == 2
        and lax.axis_size("row") % 2 == 0
        and lax.axis_size("tensor") == 4
        and depth > LANES
        and (depth - LANES) % GROUP == 0
        and depth % GROUP == 0
        and all(
            c.block in (128, 256, 512) and c.kept % GROUP == 0 and c.left in (0, 64)
            for c in chunks_of(batch_size, col_count, depth)
        )
    )
    run = on_device_packed if fits else on_device_plain
    return run(latents, clip_height, clip_width, expand_weight, *rest_of)


def solution(mesh):
    in_specs = (
        P(None, "row", None, "tensor"),
        P(),
        P(),
        P(None, None, "tensor"),
        P(None, "tensor"),
        P(None, None, None, "tensor"),
        P(None, "tensor"),
        P("tensor", None),
    )
    out_specs = P(None, "row", None, "tensor")
    return jax.shard_map(
        on_device, mesh=mesh, in_specs=in_specs, out_specs=out_specs, check_vma=False
    )
```

```python
import functools

import jax
import jax.numpy as jnp
from jax import lax
from jax.experimental import pallas as pl
from jax.experimental.pallas import tpu as pltpu
from jax.sharding import PartitionSpec as P

LANES = 512
GROUP = 16
TILE = 256


def halo_rows(cells):
    count = lax.axis_size("row")
    ends = count - 1
    head = cells[:, :1]
    tail = cells[:, -1:]
    above = lax.ppermute(tail, "row", [(i, i + 1) for i in range(ends)])
    below = lax.ppermute(head, "row", [(i + 1, i) for i in range(ends)])
    return jnp.concatenate([above, cells, below], axis=1)


def depthwise(padded, depth_weight, depth_bias, row_count, col_count):
    widened = jnp.pad(padded, ((0, 0), (0, 0), (1, 1), (0, 0), (0, 0)))
    out_shape = (widened.shape[0], row_count, col_count) + widened.shape[3:]
    depth_out = jnp.zeros(out_shape, jnp.float32) + depth_bias
    for tap_row in range(3):
        for tap_col in range(3):
            depth_out = (
                depth_out
                + depth_weight[tap_row, tap_col]
                * widened[:, tap_row : tap_row + row_count, tap_col : tap_col + col_count]
            )
    return depth_out


def on_device_plain(
    latents,
    clip_height,
    clip_width,
    expand_weight,
    expand_bias,
    depth_weight,
    depth_bias,
    project_weight,
):
    batch_size, row_count, col_count, depth = latents.shape
    tokens = batch_size * row_count * col_count
    first_row = lax.axis_index("row") * row_count
    row_ids = first_row + jnp.arange(row_count, dtype=jnp.int32)
    col_ids = jnp.arange(col_count, dtype=jnp.int32)
    valid_mask = (
        (row_ids[None, :, None] < clip_height[:, None, None])
        & (col_ids[None, None, :] < clip_width[:, None, None])
    ).astype(jnp.float32)[..., None]
    channels = latents.reshape(tokens, depth).T
    gathered = lax.all_gather(channels, "tensor", axis=0, tiled=True)
    pre_act = jnp.einsum("dt,kdf->tkf", gathered, expand_weight, preferred_element_type=jnp.float32)
    pre_act = pre_act.reshape(batch_size, row_count, col_count, 2, -1)
    expanded = (jax.nn.silu(pre_act + expand_bias) * valid_mask[..., None]).astype(jnp.bfloat16)
    padded = halo_rows(expanded)
    depth_out = depthwise(padded, depth_weight, depth_bias, row_count, col_count)
    hidden = (depth_out[:, :, :, 0] * jax.nn.silu(depth_out[:, :, :, 1])).astype(jnp.bfloat16)
    partial_term = jnp.einsum(
        "tf,fd->dt", hidden.reshape(tokens, -1), project_weight, preferred_element_type=jnp.float32
    ).astype(jnp.bfloat16)
    summed = lax.psum_scatter(partial_term, "tensor", scatter_dimension=0, tiled=True)
    summed = summed.T.reshape(latents.shape).astype(jnp.float32)
    return (summed * valid_mask).astype(jnp.bfloat16)


def slot_clips(width_ref, batch_size):
    narrow, least = jnp.int32(0), width_ref[0]
    for b in range(1, batch_size):
        closer = width_ref[b] < least
        narrow = jnp.where(closer, b, narrow)
        least = jnp.where(closer, width_ref[b], least)
    return [jnp.where(narrow <= s, s + 1, s) for s in range(batch_size - 1)] + [narrow]


def slot_widths(batch_size, col_count):
    return [col_count] * (batch_size - 1) + [col_count // 2]


class Chunk:
    def __init__(self, slots, widths, depth):
        self.slots = slots
        self.widths = [widths[s] for s in slots]
        self.starts = [sum(self.widths[:i]) for i in range(len(slots))]
        self.kept = sum(self.widths)
        self.block = -(-self.kept // 128) * 128
        self.depth, self.rest = depth, depth - LANES
        across = LANES // self.block
        groups = self.rest // GROUP
        self.places = [(g // across * GROUP, g % across * self.block) for g in range(groups)]
        self.lines = self.kept + -(-groups // across) * GROUP
        self.tokens = 2 * self.kept
        self.full, self.left = self.tokens // 128, self.tokens % 128
        self.upper = -(-depth // (2 * GROUP)) * GROUP
        self.unit = (self.full * depth + (self.upper if self.left else 0), 128)

    def clips(self, width_ref, batch_size):
        order = slot_clips(width_ref, batch_size)
        return [order[s] for s in self.slots]

    def mask_column(self, height_ref, width_ref, row_id):
        pieces = []
        clips = self.clips(width_ref, width_ref.shape[0])
        for clip, width in zip(clips, self.widths):
            bound = jnp.where((row_id >= 0) & (row_id < height_ref[clip]), width_ref[clip], 0)
            col = lax.broadcasted_iota(jnp.int32, (width, 128), 0)
            pieces.append((col < bound).astype(jnp.float32))
        return jnp.concatenate(pieces, axis=0)

    def put_unit(self, unit_ref, sums):
        depth, at = self.depth, self.full * self.depth
        for b in range(self.full):
            unit_ref[b * depth : (b + 1) * depth, :] = sums[:, b * 128 : (b + 1) * 128]
        if self.left:
            tail = sums[:, self.full * 128 :]
            lower = depth - self.upper
            unit_ref[at : at + self.upper, : self.left] = tail[: self.upper]
            unit_ref[at : at + lower, self.left :] = tail[self.upper :]
            if lower < self.upper:
                unit_ref[at + lower :, self.left :] = jnp.zeros(
                    (self.upper - lower, 128 - self.left), sums.dtype
                )

    def get_unit(self, unit):
        depth, at = self.depth, self.full * self.depth
        blocks = [unit[b * depth : (b + 1) * depth, :] for b in range(self.full)]
        if self.left:
            lower = depth - self.upper
            blocks.append(
                jnp.concatenate(
                    [unit[at : at + self.upper, : self.left], unit[at : at + lower, self.left :]], axis=0
                )
            )
        return jnp.concatenate(blocks, axis=1)


def parity_of():
    return lax.rem(lax.axis_index("row"), 2)


def row_of(place, parity):
    return jnp.where(parity == 0, (-1, 0, 1, 2)[place], (2, 1, 0, -1)[place])


def silu(v):
    h = 0.5 * v
    return h + h * jnp.tanh(h)


def pack_kernel(height_ref, width_ref, x_ref, *refs, chunks):
    parity = parity_of()
    out_refs, mask_refs = refs[: len(chunks)], refs[len(chunks) :]
    for chunk, out_ref, mask_ref in zip(chunks, out_refs, mask_refs):
        for place in range(4):
            row_id = lax.axis_index("row") * 2 + row_of(place, parity)
            mask_ref[place] = chunk.mask_column(height_ref, width_ref, row_id)
        for place in range(2):
            row = jnp.where(parity == 0, 1 - place, place)
            tails = []
            for clip, width, at in zip(
                chunk.clips(width_ref, x_ref.shape[0]), chunk.widths, chunk.starts
            ):
                out_ref[place, at : at + width, :] = x_ref[clip, row, :width, :LANES]
                tails.append(x_ref[clip, row, :width, LANES:].astype(jnp.float32))
            if chunk.block > chunk.kept:
                tails.append(jnp.zeros((chunk.block - chunk.kept, chunk.rest), jnp.float32))
            turned = jnp.concatenate(tails, axis=0).T.astype(jnp.bfloat16)
            kept = chunk.kept
            out_ref[place, kept:, :] = jnp.zeros((chunk.lines - kept, LANES), jnp.bfloat16)
            for g, (down, over) in enumerate(chunk.places):
                out_ref[place, kept + down : kept + down + GROUP, over : over + chunk.block] = turned[
                    g * GROUP : (g + 1) * GROUP
                ]


def tiles_of(hidden_count):
    return [slice(at, min(at + TILE, hidden_count)) for at in range(0, hidden_count, TILE)]


def gather_rows(x_scr, chunk, rows):
    kept = chunk.kept
    for place, packets in enumerate(rows):
        lines = slice(place * kept, (place + 1) * kept)
        tails = []
        for j, packet in enumerate(packets):
            x_scr[lines, j * LANES : (j + 1) * LANES] = packet[:kept, :]
            for down, over in chunk.places:
                tails.append(packet[kept + down : kept + down + GROUP, over : over + chunk.block])
        turned = jnp.concatenate(tails, axis=0).astype(jnp.float32).T
        x_scr[lines, len(packets) * LANES :] = turned[:kept].astype(jnp.bfloat16)


def load_kernel(dw_ref, eb_ref, db_ref, w_ref, out_ref, par_ref, sems, *, shards, depth):
    me = lax.axis_index("tensor")
    rest = depth - LANES
    copies = []
    for k in range(2):
        for j in range(shards):
            base = lax.bitwise_xor(me, j) * depth
            for part, (source, size, target) in enumerate(
                ((base, LANES, j * LANES), (base + LANES, rest, shards * LANES + j * rest))
            ):
                copies.append(
                    pltpu.make_async_copy(
                        w_ref.at[k, pl.ds(pl.multiple_of(source, GROUP), size)],
                        out_ref.at[k, pl.ds(target, size)],
                        sems.at[k, j, part],
                    )
                )
    for copy in copies:
        copy.start()
    for i in range(3):
        for col in range(3):
            par_ref[i * 6 + col * 2 : i * 6 + col * 2 + 2, :] = dw_ref[i, col]
    par_ref[18:20, :] = eb_ref[...]
    par_ref[20:22, :] = db_ref[...]
    for copy in copies:
        copy.wait()


def expand(x_scr, w_ref, par_ref, k, units):
    pre_act = jnp.dot(x_scr[...], w_ref[k, :, units], preferred_element_type=jnp.float32)
    return silu(pre_act + par_ref[18 + k : 19 + k, units])


def masked(cells, mask):
    width = cells.shape[1]
    return cells * jnp.concatenate([mask] * -(-width // 128), axis=1)[:, :width]


def own_kernel(*refs, chunk, shards):
    packet_refs, (mask_ref, par_ref, w_ref, out_ref, x_scr) = refs[:shards], refs[shards:]
    kept = chunk.kept
    gather_rows(x_scr, chunk, [[p.at[1] for p in packet_refs], [p.at[0] for p in packet_refs]])
    mask = jnp.concatenate([mask_ref[1], mask_ref[2]], axis=0)
    for units in tiles_of(w_ref.shape[2]):
        for k in range(2):
            out_ref[k, :, units] = masked(expand(x_scr, w_ref, par_ref, k, units), mask)


def hidden_kernel(*refs, chunk, shards, groups):
    count = len(groups)
    inner_refs, outer_refs = refs[:count], refs[count : 2 * count]
    own_ref, mask_ref, par_ref, w_ref, out_ref, x_scr = refs[2 * count :]
    kept = chunk.kept
    parity = parity_of()
    spots = {j: (g, i) for g, js in enumerate(groups) for i, j in enumerate(js)}
    gather_rows(
        x_scr,
        chunk,
        [[refs_of[spots[j][0]].at[spots[j][1]] for j in range(shards)] for refs_of in (outer_refs, inner_refs)],
    )
    mask = jnp.concatenate([mask_ref[0], mask_ref[3]], axis=0)

    def around(units):
        return [
            masked(expand(x_scr, w_ref, par_ref, k, units), mask) for k in range(2)
        ]

    def convolve(units, cells):
        width = units.stop - units.start
        line = lax.broadcasted_iota(jnp.int32, (kept, width), 0)
        not_first, not_last = None, None
        for at, size in zip(chunk.starts, chunk.widths):
            first, last = line != at, line != at + size - 1
            not_first = first if not_first is None else not_first & first
            not_last = last if not_last is None else not_last & last
        halves = ([], [])
        for k in range(2):
            rows = [
                cells[k][:kept],
                own_ref[k, :kept, units],
                own_ref[k, kept:, units],
                cells[k][kept:],
            ]
            taps = [
                [
                    jnp.where(
                        parity == 0,
                        par_ref[i * 6 + col * 2 + k : i * 6 + col * 2 + k + 1, units],
                        par_ref[(2 - i) * 6 + col * 2 + k : (2 - i) * 6 + col * 2 + k + 1, units],
                    )
                    for col in range(3)
                ]
                for i in range(3)
            ]
            for place in range(2):
                sums = []
                for tap_col in range(3):
                    total = None
                    for i in range(3):
                        term = taps[i][tap_col] * rows[place + i]
                        total = term if total is None else total + term
                    sums.append(total)
                left = jnp.where(not_first, pltpu.roll(sums[0], 1, 0), 0.0)
                right = jnp.where(not_last, pltpu.roll(sums[2], kept - 1, 0), 0.0)
                halves[k].append(sums[1] + left + right + par_ref[20 + k : 21 + k, units])
        for place in range(2):
            hidden = halves[0][place] * silu(halves[1][place])
            out_ref[(1 - place) * kept : (2 - place) * kept, units] = hidden.astype(jnp.bfloat16)

    tiles = tiles_of(w_ref.shape[2])
    cells = around(tiles[0])
    for t, units in enumerate(tiles):
        coming = around(tiles[t + 1]) if t + 1 < len(tiles) else None
        convolve(units, cells)
        cells = coming


def project(weight_ref, hidden_ref, depth, j):
    start = lax.bitwise_xor(lax.axis_index("tensor"), j) * depth
    return lax.dot_general(
        weight_ref[pl.ds(pl.multiple_of(start, GROUP), depth), :],
        hidden_ref[...],
        (((1,), (1,)), ((), ())),
        preferred_element_type=jnp.float32,
    )


def unit_kernel(weight_ref, hidden_ref, *refs, chunk, j):
    out_ref = refs[-1]
    sums = project(weight_ref, hidden_ref, chunk.depth, j)
    for ref in refs[:-1]:
        sums = sums + chunk.get_unit(ref[...].astype(jnp.float32))
    chunk.put_unit(out_ref, sums.astype(jnp.bfloat16))


def final_kernel(width_ref, mask_ref, weight_ref, hidden_ref, *refs, chunk, sources):
    out_ref = refs[-1]
    if len(refs) > sources + 1:
        out_ref[...] = refs[sources][...]
    sums = project(weight_ref, hidden_ref, chunk.depth, 0)
    for ref in refs[:sources]:
        sums = sums + chunk.get_unit(ref[...].astype(jnp.float32))
    cells = sums.T
    parity = parity_of()
    for place in range(2):
        row = jnp.where(parity == 0, 1 - place, place)
        mask = mask_ref[2 - place][:, :1] > 0
        part = cells[place * chunk.kept : (place + 1) * chunk.kept]
        part = jnp.where(mask, part, 0.0).astype(jnp.bfloat16)
        clips = chunk.clips(width_ref, width_ref.shape[0])
        for clip, width, at in zip(clips, chunk.widths, chunk.starts):
            out_ref[clip, row, :width, :] = part[at : at + width]
            if width < out_ref.shape[2]:
                blank = jnp.zeros((out_ref.shape[2] - width, chunk.depth), jnp.bfloat16)
                out_ref[clip, row, width:, :] = blank


VMEM = pl.BlockSpec(memory_space=pltpu.VMEM)
MIB = 1024 * 1024


def after(value, *others):
    return lax.optimization_barrier((value,) + others)[0]


def on_device_packed(
    latents,
    clip_height,
    clip_width,
    expand_weight,
    expand_bias,
    depth_weight,
    depth_bias,
    project_weight,
):
    batch_size, row_count, col_count, depth = latents.shape
    shards, row_devices = lax.axis_size("tensor"), lax.axis_size("row")
    hidden_count = expand_weight.shape[2]
    full_depth = shards * depth
    chunks = chunks_of(batch_size, col_count, depth)
    count = len(chunks)
    packed = pl.pallas_call(
        functools.partial(pack_kernel, chunks=chunks),
        out_shape=[jax.ShapeDtypeStruct((2, c.lines, LANES), jnp.bfloat16) for c in chunks]
        + [jax.ShapeDtypeStruct((4, c.kept, 128), jnp.float32) for c in chunks],
        grid_spec=pltpu.PrefetchScalarGridSpec(
            num_scalar_prefetch=2, grid=(), in_specs=[VMEM], out_specs=[VMEM] * (2 * count)
        ),
        compiler_params=pltpu.CompilerParams(vmem_limit_bytes=16 * MIB),
        name="pack",
    )(clip_height, clip_width, latents)
    own, masks = packed[:count], packed[count:]
    project_turned = project_weight.T

    sibling = [(i, i ^ 1) for i in range(row_devices)]
    beyond = [(i, i + 1) for i in range(1, row_devices - 1, 2)]
    beyond = beyond + [(b, a) for a, b in beyond]
    near = [(i, i ^ 1) for i in range(4)]
    two_off = [(i, i ^ 2) for i in range(4)]
    opposite = [(i, i ^ 3) for i in range(4)]
    middle = [(1, 2), (2, 1)]
    to_end = [(2, 3), (1, 0)]
    from_end = [(0, 1), (3, 2)]

    def edge_rows(packets, groups):
        return [
            [jnp.concatenate([packets[j][side : side + 1] for j in js], axis=0) for js in groups]
            for side in range(2)
        ]

    def send_rows(inner, outer):
        return (
            [lax.ppermute(x, "row", sibling) for x in inner],
            [lax.ppermute(x, "row", beyond) for x in outer],
        )

    def relay(mine, *others):
        second = lax.ppermute(mine, "tensor", two_off)
        first = lax.ppermute(mine, "tensor", near)
        across = lax.ppermute(after(mine, second, *others), "tensor", middle)
        passed = lax.ppermute(after(second, *others), "tensor", to_end)
        return [mine, first, second, across + passed]

    def direct(mine):
        return [mine] + [
            lax.ppermute(mine, "tensor", [(i, i ^ j) for i in range(4)]) for j in range(1, 4)
        ]

    out = None
    weights, parameters = pl.pallas_call(
        functools.partial(load_kernel, shards=shards, depth=depth),
        out_shape=[
            jax.ShapeDtypeStruct(expand_weight.shape, jnp.bfloat16),
            jax.ShapeDtypeStruct((22, hidden_count), jnp.float32),
        ],
        in_specs=[VMEM] * 3 + [pl.BlockSpec(memory_space=pl.ANY)],
        out_specs=[VMEM, VMEM],
        scratch_shapes=[pltpu.SemaphoreType.DMA((2, shards, 2))],
        compiler_params=pltpu.CompilerParams(vmem_limit_bytes=36 * MIB),
        name="load_weights",
    )(depth_weight, expand_bias, depth_bias, after(expand_weight, own[0]))
    groups = ((0,), (1, 2), (3,))
    inner, outer = send_rows(*edge_rows(own[:1], groups[:1]))
    packets = relay(own[0], parameters, *inner, *outer)
    edges = edge_rows(packets, groups[1:])
    later = send_rows(*edges)
    inner, outer = inner + later[0], outer + later[1]
    upcoming = direct(after(own[1], edges[0][-1], edges[1][-1]))
    for number, chunk in enumerate(chunks):
        if number:
            packets, groups = list(lax.optimization_barrier((*upcoming, hidden))[:shards]), ((0, 1, 2, 3),)
            inner, outer = send_rows(*edge_rows(packets, groups))
            packets[0] = after(packets[0], far)
        rows = pl.pallas_call(
            functools.partial(own_kernel, chunk=chunk, shards=shards),
            out_shape=jax.ShapeDtypeStruct((2, chunk.tokens, hidden_count), jnp.float32),
            in_specs=[VMEM] * (shards + 3),
            out_specs=VMEM,
            scratch_shapes=[pltpu.VMEM((chunk.tokens, full_depth), jnp.bfloat16)],
            compiler_params=pltpu.CompilerParams(vmem_limit_bytes=16 * MIB),
            cost_estimate=pl.CostEstimate(
                flops=1000,
                bytes_accessed=1000,
                transcendentals=0,
            ),
            name="expand_own",
        )(*packets, masks[number], parameters, weights)
        if number:
            inner[0] = after(inner[0], last_unit)
        hidden = pl.pallas_call(
            functools.partial(hidden_kernel, chunk=chunk, shards=shards, groups=groups),
            out_shape=jax.ShapeDtypeStruct((chunk.tokens, hidden_count), jnp.bfloat16),
            in_specs=[VMEM] * (2 * len(groups) + 4),
            out_specs=VMEM,
            scratch_shapes=[pltpu.VMEM((chunk.tokens, full_depth), jnp.bfloat16)],
            compiler_params=pltpu.CompilerParams(vmem_limit_bytes=16 * MIB),
            cost_estimate=pl.CostEstimate(
                flops=1000,
                bytes_accessed=1000,
                transcendentals=0,
            ),
            name="expand_conv",
        )(*inner, *outer, rows, masks[number], parameters, weights)

        cost = pl.CostEstimate(
            flops=2 * chunk.tokens * depth * hidden_count,
            bytes_accessed=2 * depth * hidden_count + 2 * chunk.tokens * hidden_count,
            transcendentals=0,
        )

        def unit(j, *added):
            return pl.pallas_call(
                functools.partial(unit_kernel, chunk=chunk, j=j),
                out_shape=jax.ShapeDtypeStruct(chunk.unit, jnp.bfloat16),
                in_specs=[VMEM] * (2 + len(added)),
                out_specs=VMEM,
                compiler_params=pltpu.CompilerParams(vmem_limit_bytes=16 * MIB),
                cost_estimate=cost,
                name=f"project_{j}",
            )(project_turned, hidden, *added)

        if number:
            units = lax.optimization_barrier((unit(3), unit(2), unit(1), *arrived))[:3]
            arrived = [
                lax.ppermute(u, "tensor", pairs) for u, pairs in zip(units, (opposite, two_off, near))
            ]
        else:
            far = unit(3)
            relayed = lax.ppermute(far, "tensor", from_end)
            across = lax.ppermute(far, "tensor", middle)
            close = unit(1)
            relayed, across = lax.optimization_barrier((relayed, across))
            last_unit = unit(2, relayed)
            arrived = [
                across,
                lax.ppermute(last_unit, "tensor", two_off),
                lax.ppermute(after(close, relayed), "tensor", near),
            ]
        extra = [] if out is None else [out]
        out = pl.pallas_call(
            functools.partial(final_kernel, chunk=chunk, sources=len(arrived)),
            out_shape=jax.ShapeDtypeStruct(latents.shape, jnp.bfloat16),
            grid_spec=pltpu.PrefetchScalarGridSpec(
                num_scalar_prefetch=1,
                grid=(),
                in_specs=[VMEM] * (3 + len(arrived) + len(extra)),
                out_specs=VMEM,
            ),
            compiler_params=pltpu.CompilerParams(vmem_limit_bytes=16 * MIB),
            cost_estimate=cost,
            name="finish",
        )(clip_width, masks[number], project_turned, hidden, *arrived, *extra)
    return out


def chunks_of(batch_size, col_count, depth):
    widths = slot_widths(batch_size, col_count)
    half = batch_size // 2
    return [Chunk(slots, widths, depth) for slots in (list(range(half)), list(range(half, batch_size)))]


def on_device(latents, clip_height, clip_width, expand_weight, *rest_of):
    batch_size, row_count, col_count, depth = latents.shape
    fits = (
        batch_size >= 2
        and row_count == 2
        and lax.axis_size("row") % 2 == 0
        and lax.axis_size("tensor") == 4
        and depth > LANES
        and (depth - LANES) % GROUP == 0
        and depth % GROUP == 0
        and all(
            c.block in (128, 256, 512) and c.kept % GROUP == 0 and c.left in (0, 64)
            for c in chunks_of(batch_size, col_count, depth)
        )
    )
    run = on_device_packed if fits else on_device_plain
    return run(latents, clip_height, clip_width, expand_weight, *rest_of)


def solution(mesh):
    in_specs = (
        P(None, "row", None, "tensor"),
        P(),
        P(),
        P(None, None, "tensor"),
        P(None, "tensor"),
        P(None, None, None, "tensor"),
        P(None, "tensor"),
        P("tensor", None),
    )
    out_specs = P(None, "row", None, "tensor")
    return jax.shard_map(
        on_device, mesh=mesh, in_specs=in_specs, out_specs=out_specs, check_vma=False
    )
```

```python
import functools

import jax
import jax.numpy as jnp
from jax import lax
from jax.experimental import pallas as pl
from jax.experimental.pallas import tpu as pltpu
from jax.sharding import PartitionSpec as P

LANES = 512
GROUP = 16
TILE = 256


def halo_rows(cells):
    count = lax.axis_size("row")
    ends = count - 1
    head = cells[:, :1]
    tail = cells[:, -1:]
    above = lax.ppermute(tail, "row", [(i, i + 1) for i in range(ends)])
    below = lax.ppermute(head, "row", [(i + 1, i) for i in range(ends)])
    return jnp.concatenate([above, cells, below], axis=1)


def depthwise(padded, depth_weight, depth_bias, row_count, col_count):
    widened = jnp.pad(padded, ((0, 0), (0, 0), (1, 1), (0, 0), (0, 0)))
    out_shape = (widened.shape[0], row_count, col_count) + widened.shape[3:]
    depth_out = jnp.zeros(out_shape, jnp.float32) + depth_bias
    for tap_row in range(3):
        for tap_col in range(3):
            depth_out = (
                depth_out
                + depth_weight[tap_row, tap_col]
                * widened[:, tap_row : tap_row + row_count, tap_col : tap_col + col_count]
            )
    return depth_out


def on_device_plain(
    latents,
    clip_height,
    clip_width,
    expand_weight,
    expand_bias,
    depth_weight,
    depth_bias,
    project_weight,
):
    batch_size, row_count, col_count, depth = latents.shape
    tokens = batch_size * row_count * col_count
    first_row = lax.axis_index("row") * row_count
    row_ids = first_row + jnp.arange(row_count, dtype=jnp.int32)
    col_ids = jnp.arange(col_count, dtype=jnp.int32)
    valid_mask = (
        (row_ids[None, :, None] < clip_height[:, None, None])
        & (col_ids[None, None, :] < clip_width[:, None, None])
    ).astype(jnp.float32)[..., None]
    channels = latents.reshape(tokens, depth).T
    gathered = lax.all_gather(channels, "tensor", axis=0, tiled=True)
    pre_act = jnp.einsum("dt,kdf->tkf", gathered, expand_weight, preferred_element_type=jnp.float32)
    pre_act = pre_act.reshape(batch_size, row_count, col_count, 2, -1)
    expanded = (jax.nn.silu(pre_act + expand_bias) * valid_mask[..., None]).astype(jnp.bfloat16)
    padded = halo_rows(expanded)
    depth_out = depthwise(padded, depth_weight, depth_bias, row_count, col_count)
    hidden = (depth_out[:, :, :, 0] * jax.nn.silu(depth_out[:, :, :, 1])).astype(jnp.bfloat16)
    partial_term = jnp.einsum(
        "tf,fd->dt", hidden.reshape(tokens, -1), project_weight, preferred_element_type=jnp.float32
    ).astype(jnp.bfloat16)
    summed = lax.psum_scatter(partial_term, "tensor", scatter_dimension=0, tiled=True)
    summed = summed.T.reshape(latents.shape).astype(jnp.float32)
    return (summed * valid_mask).astype(jnp.bfloat16)


def slot_clips(width_ref, batch_size):
    narrow, least = jnp.int32(0), width_ref[0]
    for b in range(1, batch_size):
        closer = width_ref[b] < least
        narrow = jnp.where(closer, b, narrow)
        least = jnp.where(closer, width_ref[b], least)
    return [jnp.where(narrow <= s, s + 1, s) for s in range(batch_size - 1)] + [narrow]


def slot_widths(batch_size, col_count):
    return [col_count] * (batch_size - 1) + [col_count // 2]


class Chunk:
    def __init__(self, slots, widths, depth):
        self.slots = slots
        self.widths = [widths[s] for s in slots]
        self.starts = [sum(self.widths[:i]) for i in range(len(slots))]
        self.kept = sum(self.widths)
        self.block = -(-self.kept // 128) * 128
        self.depth, self.rest = depth, depth - LANES
        across = LANES // self.block
        groups = self.rest // GROUP
        self.places = [(g // across * GROUP, g % across * self.block) for g in range(groups)]
        self.lines = self.kept + -(-groups // across) * GROUP
        self.tokens = 2 * self.kept
        self.full, self.left = self.tokens // 128, self.tokens % 128
        self.upper = -(-depth // (2 * GROUP)) * GROUP
        self.unit = (self.full * depth + (self.upper if self.left else 0), 128)

    def clips(self, width_ref, batch_size):
        order = slot_clips(width_ref, batch_size)
        return [order[s] for s in self.slots]

    def mask_column(self, height_ref, width_ref, row_id):
        pieces = []
        clips = self.clips(width_ref, width_ref.shape[0])
        for clip, width in zip(clips, self.widths):
            bound = jnp.where((row_id >= 0) & (row_id < height_ref[clip]), width_ref[clip], 0)
            col = lax.broadcasted_iota(jnp.int32, (width, 128), 0)
            pieces.append((col < bound).astype(jnp.float32))
        return jnp.concatenate(pieces, axis=0)

    def put_unit(self, unit_ref, sums):
        depth, at = self.depth, self.full * self.depth
        for b in range(self.full):
            unit_ref[b * depth : (b + 1) * depth, :] = sums[:, b * 128 : (b + 1) * 128]
        if self.left:
            tail = sums[:, self.full * 128 :]
            lower = depth - self.upper
            unit_ref[at : at + self.upper, : self.left] = tail[: self.upper]
            unit_ref[at : at + lower, self.left :] = tail[self.upper :]
            if lower < self.upper:
                unit_ref[at + lower :, self.left :] = jnp.zeros(
                    (self.upper - lower, 128 - self.left), sums.dtype
                )

    def get_unit(self, unit):
        depth, at = self.depth, self.full * self.depth
        blocks = [unit[b * depth : (b + 1) * depth, :] for b in range(self.full)]
        if self.left:
            lower = depth - self.upper
            blocks.append(
                jnp.concatenate(
                    [unit[at : at + self.upper, : self.left], unit[at : at + lower, self.left :]], axis=0
                )
            )
        return jnp.concatenate(blocks, axis=1)


def parity_of():
    return lax.rem(lax.axis_index("row"), 2)


def row_of(place, parity):
    return jnp.where(parity == 0, (-1, 0, 1, 2)[place], (2, 1, 0, -1)[place])


def silu(v):
    h = 0.5 * v
    return h + h * jnp.tanh(h)


def pack_kernel(width_ref, x_ref, *out_refs, chunks):
    parity = parity_of()
    for chunk, out_ref in zip(chunks, out_refs):
        for place in range(2):
            row = jnp.where(parity == 0, 1 - place, place)
            tails = []
            for clip, width, at in zip(
                chunk.clips(width_ref, x_ref.shape[0]), chunk.widths, chunk.starts
            ):
                out_ref[place, at : at + width, :] = x_ref[clip, row, :width, :LANES]
                tails.append(x_ref[clip, row, :width, LANES:].astype(jnp.float32))
            if chunk.block > chunk.kept:
                tails.append(jnp.zeros((chunk.block - chunk.kept, chunk.rest), jnp.float32))
            turned = jnp.concatenate(tails, axis=0).T.astype(jnp.bfloat16)
            kept = chunk.kept
            out_ref[place, kept:, :] = jnp.zeros((chunk.lines - kept, LANES), jnp.bfloat16)
            for g, (down, over) in enumerate(chunk.places):
                out_ref[place, kept + down : kept + down + GROUP, over : over + chunk.block] = turned[
                    g * GROUP : (g + 1) * GROUP
                ]


def tiles_of(hidden_count):
    return [slice(at, min(at + TILE, hidden_count)) for at in range(0, hidden_count, TILE)]


def gather_rows(x_scr, chunk, rows):
    kept = chunk.kept
    for place, packets in enumerate(rows):
        lines = slice(place * kept, (place + 1) * kept)
        tails = []
        for j, packet in enumerate(packets):
            x_scr[lines, j * LANES : (j + 1) * LANES] = packet[:kept, :]
            for down, over in chunk.places:
                tails.append(packet[kept + down : kept + down + GROUP, over : over + chunk.block])
        turned = jnp.concatenate(tails, axis=0).astype(jnp.float32).T
        x_scr[lines, len(packets) * LANES :] = turned[:kept].astype(jnp.bfloat16)


def load_kernel(
    height_ref, width_ref, dw_ref, eb_ref, db_ref, w_ref, out_ref, par_ref, *refs, shards, depth, chunks
):
    mask_refs, sems = refs[:-1], refs[-1]
    me = lax.axis_index("tensor")
    rest = depth - LANES
    copies = []
    for k in range(2):
        for j in range(shards):
            base = lax.bitwise_xor(me, j) * depth
            for part, (source, size, target) in enumerate(
                ((base, LANES, j * LANES), (base + LANES, rest, shards * LANES + j * rest))
            ):
                copies.append(
                    pltpu.make_async_copy(
                        w_ref.at[k, pl.ds(pl.multiple_of(source, GROUP), size)],
                        out_ref.at[k, pl.ds(target, size)],
                        sems.at[k, j, part],
                    )
                )
    for copy in copies:
        copy.start()
    for i in range(3):
        for col in range(3):
            par_ref[i * 6 + col * 2 : i * 6 + col * 2 + 2, :] = dw_ref[i, col]
    parity = parity_of()
    for chunk, mask_ref in zip(chunks, mask_refs):
        for place in range(4):
            row_id = lax.axis_index("row") * 2 + row_of(place, parity)
            mask_ref[place] = chunk.mask_column(height_ref, width_ref, row_id)
    par_ref[18:20, :] = eb_ref[...]
    par_ref[20:22, :] = db_ref[...]
    for copy in copies:
        copy.wait()


def expand(x_scr, w_ref, par_ref, k, units):
    pre_act = jnp.dot(x_scr[...], w_ref[k, :, units], preferred_element_type=jnp.float32)
    return silu(pre_act + par_ref[18 + k : 19 + k, units])


def masked(cells, mask):
    width = cells.shape[1]
    return cells * jnp.concatenate([mask] * -(-width // 128), axis=1)[:, :width]


def own_kernel(*refs, chunk, shards):
    packet_refs, (mask_ref, par_ref, w_ref, out_ref, x_scr) = refs[:shards], refs[shards:]
    kept = chunk.kept
    gather_rows(x_scr, chunk, [[p.at[1] for p in packet_refs], [p.at[0] for p in packet_refs]])
    mask = jnp.concatenate([mask_ref[1], mask_ref[2]], axis=0)
    for units in tiles_of(w_ref.shape[2]):
        for k in range(2):
            out_ref[k, :, units] = masked(expand(x_scr, w_ref, par_ref, k, units), mask)


def hidden_kernel(*refs, chunk, shards, groups):
    count = len(groups)
    inner_refs, outer_refs = refs[:count], refs[count : 2 * count]
    own_ref, mask_ref, par_ref, w_ref, out_ref, x_scr = refs[2 * count :]
    kept = chunk.kept
    parity = parity_of()
    spots = {j: (g, i) for g, js in enumerate(groups) for i, j in enumerate(js)}
    gather_rows(
        x_scr,
        chunk,
        [[refs_of[spots[j][0]].at[spots[j][1]] for j in range(shards)] for refs_of in (outer_refs, inner_refs)],
    )
    mask = jnp.concatenate([mask_ref[0], mask_ref[3]], axis=0)

    def around(units):
        return [
            masked(expand(x_scr, w_ref, par_ref, k, units), mask) for k in range(2)
        ]

    def convolve(units, cells):
        width = units.stop - units.start
        line = lax.broadcasted_iota(jnp.int32, (kept, width), 0)
        not_first, not_last = None, None
        for at, size in zip(chunk.starts, chunk.widths):
            first, last = line != at, line != at + size - 1
            not_first = first if not_first is None else not_first & first
            not_last = last if not_last is None else not_last & last
        halves = ([], [])
        for k in range(2):
            rows = [
                cells[k][:kept],
                own_ref[k, :kept, units],
                own_ref[k, kept:, units],
                cells[k][kept:],
            ]
            taps = [
                [
                    jnp.where(
                        parity == 0,
                        par_ref[i * 6 + col * 2 + k : i * 6 + col * 2 + k + 1, units],
                        par_ref[(2 - i) * 6 + col * 2 + k : (2 - i) * 6 + col * 2 + k + 1, units],
                    )
                    for col in range(3)
                ]
                for i in range(3)
            ]
            for place in range(2):
                sums = []
                for tap_col in range(3):
                    total = None
                    for i in range(3):
                        term = taps[i][tap_col] * rows[place + i]
                        total = term if total is None else total + term
                    sums.append(total)
                left = jnp.where(not_first, pltpu.roll(sums[0], 1, 0), 0.0)
                right = jnp.where(not_last, pltpu.roll(sums[2], kept - 1, 0), 0.0)
                halves[k].append(sums[1] + left + right + par_ref[20 + k : 21 + k, units])
        for place in range(2):
            hidden = halves[0][place] * silu(halves[1][place])
            out_ref[(1 - place) * kept : (2 - place) * kept, units] = hidden.astype(jnp.bfloat16)

    tiles = tiles_of(w_ref.shape[2])
    cells = around(tiles[0])
    for t, units in enumerate(tiles):
        coming = around(tiles[t + 1]) if t + 1 < len(tiles) else None
        convolve(units, cells)
        cells = coming


def project(weight_ref, hidden_ref, depth, j):
    start = lax.bitwise_xor(lax.axis_index("tensor"), j) * depth
    return lax.dot_general(
        weight_ref[pl.ds(pl.multiple_of(start, GROUP), depth), :],
        hidden_ref[...],
        (((1,), (1,)), ((), ())),
        preferred_element_type=jnp.float32,
    )


def unit_kernel(weight_ref, hidden_ref, *refs, chunk, j):
    out_ref = refs[-1]
    sums = project(weight_ref, hidden_ref, chunk.depth, j)
    for ref in refs[:-1]:
        sums = sums + chunk.get_unit(ref[...].astype(jnp.float32))
    chunk.put_unit(out_ref, sums.astype(jnp.bfloat16))


def share_kernel(weight_ref, hidden_ref, out_ref, *, chunk):
    out_ref[...] = project(weight_ref, hidden_ref, chunk.depth, 0)


def final_kernel(width_ref, mask_ref, share_ref, *refs, chunk, sources):
    out_ref = refs[-1]
    if len(refs) > sources + 1:
        out_ref[...] = refs[sources][...]
    sums = share_ref[...]
    for ref in refs[:sources]:
        sums = sums + chunk.get_unit(ref[...].astype(jnp.float32))
    cells = sums.T
    parity = parity_of()
    for place in range(2):
        row = jnp.where(parity == 0, 1 - place, place)
        mask = mask_ref[2 - place][:, :1] > 0
        part = cells[place * chunk.kept : (place + 1) * chunk.kept]
        part = jnp.where(mask, part, 0.0).astype(jnp.bfloat16)
        clips = chunk.clips(width_ref, width_ref.shape[0])
        for clip, width, at in zip(clips, chunk.widths, chunk.starts):
            out_ref[clip, row, :width, :] = part[at : at + width]
            if width < out_ref.shape[2]:
                blank = jnp.zeros((out_ref.shape[2] - width, chunk.depth), jnp.bfloat16)
                out_ref[clip, row, width:, :] = blank


VMEM = pl.BlockSpec(memory_space=pltpu.VMEM)
MIB = 1024 * 1024


def after(value, *others):
    return lax.optimization_barrier((value,) + others)[0]


def on_device_packed(
    latents,
    clip_height,
    clip_width,
    expand_weight,
    expand_bias,
    depth_weight,
    depth_bias,
    project_weight,
):
    batch_size, row_count, col_count, depth = latents.shape
    shards, row_devices = lax.axis_size("tensor"), lax.axis_size("row")
    hidden_count = expand_weight.shape[2]
    full_depth = shards * depth
    chunks = chunks_of(batch_size, col_count, depth)
    count = len(chunks)
    own = pl.pallas_call(
        functools.partial(pack_kernel, chunks=chunks),
        out_shape=[jax.ShapeDtypeStruct((2, c.lines, LANES), jnp.bfloat16) for c in chunks],
        grid_spec=pltpu.PrefetchScalarGridSpec(
            num_scalar_prefetch=1, grid=(), in_specs=[VMEM], out_specs=[VMEM] * count
        ),
        compiler_params=pltpu.CompilerParams(vmem_limit_bytes=16 * MIB),
        name="pack",
    )(clip_width, latents)
    project_turned = project_weight.T

    sibling = [(i, i ^ 1) for i in range(row_devices)]
    beyond = [(i, i + 1) for i in range(1, row_devices - 1, 2)]
    beyond = beyond + [(b, a) for a, b in beyond]
    near = [(i, i ^ 1) for i in range(4)]
    two_off = [(i, i ^ 2) for i in range(4)]
    opposite = [(i, i ^ 3) for i in range(4)]
    middle = [(1, 2), (2, 1)]
    to_end = [(2, 3), (1, 0)]
    from_end = [(0, 1), (3, 2)]

    def edge_rows(packets, groups):
        return [
            [jnp.concatenate([packets[j][side : side + 1] for j in js], axis=0) for js in groups]
            for side in range(2)
        ]

    def send_rows(inner, outer):
        return (
            [lax.ppermute(x, "row", sibling) for x in inner],
            [lax.ppermute(x, "row", beyond) for x in outer],
        )

    def relay(mine, *others):
        second = lax.ppermute(mine, "tensor", two_off)
        first = lax.ppermute(mine, "tensor", near)
        across = lax.ppermute(after(mine, second, *others), "tensor", middle)
        passed = lax.ppermute(after(second, *others), "tensor", to_end)
        return [mine, first, second, across + passed]

    def direct(mine):
        return [mine] + [
            lax.ppermute(mine, "tensor", [(i, i ^ j) for i in range(4)]) for j in range(1, 4)
        ]

    out = None
    weights, parameters, *masks = pl.pallas_call(
        functools.partial(load_kernel, shards=shards, depth=depth, chunks=chunks),
        out_shape=[
            jax.ShapeDtypeStruct(expand_weight.shape, jnp.bfloat16),
            jax.ShapeDtypeStruct((22, hidden_count), jnp.float32),
        ]
        + [jax.ShapeDtypeStruct((4, c.kept, 128), jnp.float32) for c in chunks],
        grid_spec=pltpu.PrefetchScalarGridSpec(
            num_scalar_prefetch=2,
            grid=(),
            in_specs=[VMEM] * 3 + [pl.BlockSpec(memory_space=pl.ANY)],
            out_specs=[VMEM] * (2 + count),
            scratch_shapes=[pltpu.SemaphoreType.DMA((2, shards, 2))],
        ),
        compiler_params=pltpu.CompilerParams(vmem_limit_bytes=36 * MIB),
        name="load_weights",
    )(clip_height, clip_width, depth_weight, expand_bias, depth_bias, after(expand_weight, own[0]))
    groups = ((0,), (1, 2), (3,))
    inner, outer = send_rows(*edge_rows(own[:1], groups[:1]))
    packets = relay(own[0], parameters, *inner, *outer)
    edges = edge_rows(packets, groups[1:])
    later = send_rows(*edges)
    inner, outer = inner + later[0], outer + later[1]
    upcoming = direct(after(own[1], edges[0][-1], edges[1][-1]))
    for number, chunk in enumerate(chunks):
        if number:
            packets, groups = list(lax.optimization_barrier((*upcoming, hidden))[:shards]), ((0, 1, 2, 3),)
            inner, outer = send_rows(*edge_rows(packets, groups))
            packets[0] = after(packets[0], far)
        rows = pl.pallas_call(
            functools.partial(own_kernel, chunk=chunk, shards=shards),
            out_shape=jax.ShapeDtypeStruct((2, chunk.tokens, hidden_count), jnp.float32),
            in_specs=[VMEM] * (shards + 3),
            out_specs=VMEM,
            scratch_shapes=[pltpu.VMEM((chunk.tokens, full_depth), jnp.bfloat16)],
            compiler_params=pltpu.CompilerParams(vmem_limit_bytes=16 * MIB),
            cost_estimate=pl.CostEstimate(
                flops=1000,
                bytes_accessed=1000,
                transcendentals=0,
            ),
            name="expand_own",
        )(*packets, masks[number], parameters, weights)
        if number:
            inner[0] = after(inner[0], last_unit)
        hidden = pl.pallas_call(
            functools.partial(hidden_kernel, chunk=chunk, shards=shards, groups=groups),
            out_shape=jax.ShapeDtypeStruct((chunk.tokens, hidden_count), jnp.bfloat16),
            in_specs=[VMEM] * (2 * len(groups) + 4),
            out_specs=VMEM,
            scratch_shapes=[pltpu.VMEM((chunk.tokens, full_depth), jnp.bfloat16)],
            compiler_params=pltpu.CompilerParams(vmem_limit_bytes=16 * MIB),
            cost_estimate=pl.CostEstimate(
                flops=1000,
                bytes_accessed=1000,
                transcendentals=0,
            ),
            name="expand_conv",
        )(*inner, *outer, rows, masks[number], parameters, weights)

        cost = pl.CostEstimate(
            flops=2 * chunk.tokens * depth * hidden_count,
            bytes_accessed=2 * depth * hidden_count + 2 * chunk.tokens * hidden_count,
            transcendentals=0,
        )

        def unit(j, *added):
            return pl.pallas_call(
                functools.partial(unit_kernel, chunk=chunk, j=j),
                out_shape=jax.ShapeDtypeStruct(chunk.unit, jnp.bfloat16),
                in_specs=[VMEM] * (2 + len(added)),
                out_specs=VMEM,
                compiler_params=pltpu.CompilerParams(vmem_limit_bytes=16 * MIB),
                cost_estimate=cost,
                name=f"project_{j}",
            )(project_turned, hidden, *added)

        far = unit(3)
        relayed = lax.ppermute(far, "tensor", from_end)
        across = lax.ppermute(far, "tensor", middle)
        close = unit(1)
        if number:
            relayed, across = lax.optimization_barrier((relayed, across, out))[:2]
        else:
            relayed, across = lax.optimization_barrier((relayed, across))
        last_unit = unit(2, relayed)
        arrived = [
            across,
            lax.ppermute(last_unit, "tensor", two_off),
            lax.ppermute(after(close, relayed), "tensor", near),
        ]
        share = pl.pallas_call(
            functools.partial(share_kernel, chunk=chunk),
            out_shape=jax.ShapeDtypeStruct((depth, chunk.tokens), jnp.float32),
            in_specs=[VMEM, VMEM],
            out_specs=VMEM,
            compiler_params=pltpu.CompilerParams(vmem_limit_bytes=16 * MIB),
            cost_estimate=cost,
            name="project_0",
        )(project_turned, hidden)
        extra = [] if out is None else [out]
        out = pl.pallas_call(
            functools.partial(final_kernel, chunk=chunk, sources=len(arrived)),
            out_shape=jax.ShapeDtypeStruct(latents.shape, jnp.bfloat16),
            grid_spec=pltpu.PrefetchScalarGridSpec(
                num_scalar_prefetch=1,
                grid=(),
                in_specs=[VMEM] * (2 + len(arrived) + len(extra)),
                out_specs=VMEM,
            ),
            compiler_params=pltpu.CompilerParams(vmem_limit_bytes=16 * MIB),
            cost_estimate=pl.CostEstimate(flops=10**11, bytes_accessed=10**9, transcendentals=0),
            name="finish",
        )(clip_width, masks[number], share, *arrived, *extra)
    return out


def chunks_of(batch_size, col_count, depth):
    widths = slot_widths(batch_size, col_count)
    half = batch_size // 2
    return [Chunk(slots, widths, depth) for slots in (list(range(half)), list(range(half, batch_size)))]


def on_device(latents, clip_height, clip_width, expand_weight, *rest_of):
    batch_size, row_count, col_count, depth = latents.shape
    fits = (
        batch_size >= 2
        and row_count == 2
        and lax.axis_size("row") % 2 == 0
        and lax.axis_size("tensor") == 4
        and depth > LANES
        and (depth - LANES) % GROUP == 0
        and depth % GROUP == 0
        and all(
            c.block in (128, 256, 512) and c.kept % GROUP == 0 and c.left in (0, 64)
            for c in chunks_of(batch_size, col_count, depth)
        )
    )
    run = on_device_packed if fits else on_device_plain
    return run(latents, clip_height, clip_width, expand_weight, *rest_of)


def solution(mesh):
    in_specs = (
        P(None, "row", None, "tensor"),
        P(),
        P(),
        P(None, None, "tensor"),
        P(None, "tensor"),
        P(None, None, None, "tensor"),
        P(None, "tensor"),
        P("tensor", None),
    )
    out_specs = P(None, "row", None, "tensor")
    return jax.shard_map(
        on_device, mesh=mesh, in_specs=in_specs, out_specs=out_specs, check_vma=False
    )
```

```python
import functools

import jax
import jax.numpy as jnp
from jax import lax
from jax.experimental import pallas as pl
from jax.experimental.pallas import tpu as pltpu
from jax.sharding import PartitionSpec as P

LANES = 512
GROUP = 16
TILE = 256


def halo_rows(cells):
    count = lax.axis_size("row")
    ends = count - 1
    head = cells[:, :1]
    tail = cells[:, -1:]
    above = lax.ppermute(tail, "row", [(i, i + 1) for i in range(ends)])
    below = lax.ppermute(head, "row", [(i + 1, i) for i in range(ends)])
    return jnp.concatenate([above, cells, below], axis=1)


def depthwise(padded, depth_weight, depth_bias, row_count, col_count):
    widened = jnp.pad(padded, ((0, 0), (0, 0), (1, 1), (0, 0), (0, 0)))
    out_shape = (widened.shape[0], row_count, col_count) + widened.shape[3:]
    depth_out = jnp.zeros(out_shape, jnp.float32) + depth_bias
    for tap_row in range(3):
        for tap_col in range(3):
            depth_out = (
                depth_out
                + depth_weight[tap_row, tap_col]
                * widened[:, tap_row : tap_row + row_count, tap_col : tap_col + col_count]
            )
    return depth_out


def on_device_plain(
    latents,
    clip_height,
    clip_width,
    expand_weight,
    expand_bias,
    depth_weight,
    depth_bias,
    project_weight,
):
    batch_size, row_count, col_count, depth = latents.shape
    tokens = batch_size * row_count * col_count
    first_row = lax.axis_index("row") * row_count
    row_ids = first_row + jnp.arange(row_count, dtype=jnp.int32)
    col_ids = jnp.arange(col_count, dtype=jnp.int32)
    valid_mask = (
        (row_ids[None, :, None] < clip_height[:, None, None])
        & (col_ids[None, None, :] < clip_width[:, None, None])
    ).astype(jnp.float32)[..., None]
    channels = latents.reshape(tokens, depth).T
    gathered = lax.all_gather(channels, "tensor", axis=0, tiled=True)
    pre_act = jnp.einsum("dt,kdf->tkf", gathered, expand_weight, preferred_element_type=jnp.float32)
    pre_act = pre_act.reshape(batch_size, row_count, col_count, 2, -1)
    expanded = (jax.nn.silu(pre_act + expand_bias) * valid_mask[..., None]).astype(jnp.bfloat16)
    padded = halo_rows(expanded)
    depth_out = depthwise(padded, depth_weight, depth_bias, row_count, col_count)
    hidden = (depth_out[:, :, :, 0] * jax.nn.silu(depth_out[:, :, :, 1])).astype(jnp.bfloat16)
    partial_term = jnp.einsum(
        "tf,fd->dt", hidden.reshape(tokens, -1), project_weight, preferred_element_type=jnp.float32
    ).astype(jnp.bfloat16)
    summed = lax.psum_scatter(partial_term, "tensor", scatter_dimension=0, tiled=True)
    summed = summed.T.reshape(latents.shape).astype(jnp.float32)
    return (summed * valid_mask).astype(jnp.bfloat16)


def slot_clips(width_ref, batch_size):
    narrow, least = jnp.int32(0), width_ref[0]
    for b in range(1, batch_size):
        closer = width_ref[b] < least
        narrow = jnp.where(closer, b, narrow)
        least = jnp.where(closer, width_ref[b], least)
    return [jnp.where(narrow <= s, s + 1, s) for s in range(batch_size - 1)] + [narrow]


def slot_widths(batch_size, col_count):
    return [col_count] * (batch_size - 1) + [col_count // 2]


class Chunk:
    def __init__(self, slots, widths, depth):
        self.slots = slots
        self.widths = [widths[s] for s in slots]
        self.starts = [sum(self.widths[:i]) for i in range(len(slots))]
        self.kept = sum(self.widths)
        self.block = -(-self.kept // 128) * 128
        self.depth, self.rest = depth, depth - LANES
        across = LANES // self.block
        groups = self.rest // GROUP
        self.places = [(g // across * GROUP, g % across * self.block) for g in range(groups)]
        self.lines = self.kept + -(-groups // across) * GROUP
        self.tokens = 2 * self.kept
        self.full, self.left = self.tokens // 128, self.tokens % 128
        self.upper = -(-depth // (2 * GROUP)) * GROUP
        self.unit = (self.full * depth + (self.upper if self.left else 0), 128)

    def clips(self, width_ref, batch_size):
        order = slot_clips(width_ref, batch_size)
        return [order[s] for s in self.slots]

    def mask_column(self, height_ref, width_ref, row_id):
        pieces = []
        clips = self.clips(width_ref, width_ref.shape[0])
        for clip, width in zip(clips, self.widths):
            bound = jnp.where((row_id >= 0) & (row_id < height_ref[clip]), width_ref[clip], 0)
            col = lax.broadcasted_iota(jnp.int32, (width, 128), 0)
            pieces.append((col < bound).astype(jnp.float32))
        return jnp.concatenate(pieces, axis=0)

    def put_unit(self, unit_ref, sums):
        depth, at = self.depth, self.full * self.depth
        for b in range(self.full):
            unit_ref[b * depth : (b + 1) * depth, :] = sums[:, b * 128 : (b + 1) * 128]
        if self.left:
            tail = sums[:, self.full * 128 :]
            lower = depth - self.upper
            unit_ref[at : at + self.upper, : self.left] = tail[: self.upper]
            unit_ref[at : at + lower, self.left :] = tail[self.upper :]
            if lower < self.upper:
                unit_ref[at + lower :, self.left :] = jnp.zeros(
                    (self.upper - lower, 128 - self.left), sums.dtype
                )

    def get_unit(self, unit):
        depth, at = self.depth, self.full * self.depth
        blocks = [unit[b * depth : (b + 1) * depth, :] for b in range(self.full)]
        if self.left:
            lower = depth - self.upper
            blocks.append(
                jnp.concatenate(
                    [unit[at : at + self.upper, : self.left], unit[at : at + lower, self.left :]], axis=0
                )
            )
        return jnp.concatenate(blocks, axis=1)


def parity_of():
    return lax.rem(lax.axis_index("row"), 2)


def row_of(place, parity):
    return jnp.where(parity == 0, (-1, 0, 1, 2)[place], (2, 1, 0, -1)[place])


def silu(v):
    h = 0.5 * v
    return h + h * jnp.tanh(h)


def pack_kernel(width_ref, x_ref, *out_refs, chunks):
    parity = parity_of()
    for chunk, out_ref in zip(chunks, out_refs):
        for place in range(2):
            row = jnp.where(parity == 0, 1 - place, place)
            tails = []
            for clip, width, at in zip(
                chunk.clips(width_ref, x_ref.shape[0]), chunk.widths, chunk.starts
            ):
                out_ref[place, at : at + width, :] = x_ref[clip, row, :width, :LANES]
                tails.append(x_ref[clip, row, :width, LANES:].astype(jnp.float32))
            if chunk.block > chunk.kept:
                tails.append(jnp.zeros((chunk.block - chunk.kept, chunk.rest), jnp.float32))
            turned = jnp.concatenate(tails, axis=0).T.astype(jnp.bfloat16)
            kept = chunk.kept
            out_ref[place, kept:, :] = jnp.zeros((chunk.lines - kept, LANES), jnp.bfloat16)
            for g, (down, over) in enumerate(chunk.places):
                out_ref[place, kept + down : kept + down + GROUP, over : over + chunk.block] = turned[
                    g * GROUP : (g + 1) * GROUP
                ]


def tiles_of(hidden_count):
    return [slice(at, min(at + TILE, hidden_count)) for at in range(0, hidden_count, TILE)]


def gather_rows(x_scr, chunk, rows):
    kept = chunk.kept
    for place, packets in enumerate(rows):
        lines = slice(place * kept, (place + 1) * kept)
        tails = []
        for j, packet in enumerate(packets):
            x_scr[lines, j * LANES : (j + 1) * LANES] = packet[:kept, :]
            for down, over in chunk.places:
                tails.append(packet[kept + down : kept + down + GROUP, over : over + chunk.block])
        turned = jnp.concatenate(tails, axis=0).astype(jnp.float32).T
        x_scr[lines, len(packets) * LANES :] = turned[:kept].astype(jnp.bfloat16)


def load_kernel(w_ref, out_ref, token_ref, sems, *, shards, depth):
    token_ref[...] = jnp.zeros_like(token_ref)
    me = lax.axis_index("tensor")
    rest = depth - LANES
    copies = []
    for k in range(2):
        for j in range(shards):
            base = lax.bitwise_xor(me, j) * depth
            for part, (source, size, target) in enumerate(
                ((base, LANES, j * LANES), (base + LANES, rest, shards * LANES + j * rest))
            ):
                copies.append(
                    pltpu.make_async_copy(
                        w_ref.at[k, pl.ds(pl.multiple_of(source, GROUP), size)],
                        out_ref.at[k, pl.ds(target, size)],
                        sems.at[k, j, part],
                    )
                )
    for copy in copies:
        copy.start()
    for copy in copies:
        copy.wait()


def table_kernel(height_ref, width_ref, dw_ref, eb_ref, db_ref, par_ref, *mask_refs, chunks):
    parity = parity_of()
    for chunk, mask_ref in zip(chunks, mask_refs):
        for place in range(4):
            row_id = lax.axis_index("row") * 2 + row_of(place, parity)
            mask_ref[place] = chunk.mask_column(height_ref, width_ref, row_id)
    for i in range(3):
        for col in range(3):
            par_ref[i * 6 + col * 2 : i * 6 + col * 2 + 2, :] = dw_ref[i, col]
    par_ref[18:20, :] = eb_ref[...]
    par_ref[20:22, :] = db_ref[...]


def expand(x_scr, w_ref, par_ref, k, units):
    pre_act = jnp.dot(x_scr[...], w_ref[k, :, units], preferred_element_type=jnp.float32)
    return silu(pre_act + par_ref[18 + k : 19 + k, units])


def masked(cells, mask):
    width = cells.shape[1]
    return cells * jnp.concatenate([mask] * -(-width // 128), axis=1)[:, :width]


def own_kernel(*refs, chunk, shards):
    packet_refs, (mask_ref, par_ref, w_ref, out_ref, x_scr) = refs[:shards], refs[shards:]
    kept = chunk.kept
    gather_rows(x_scr, chunk, [[p.at[1] for p in packet_refs], [p.at[0] for p in packet_refs]])
    mask = jnp.concatenate([mask_ref[1], mask_ref[2]], axis=0)
    for units in tiles_of(w_ref.shape[2]):
        for k in range(2):
            out_ref[k, :, units] = masked(expand(x_scr, w_ref, par_ref, k, units), mask)


def hidden_kernel(*refs, chunk, shards, groups):
    count = len(groups)
    inner_refs, outer_refs = refs[:count], refs[count : 2 * count]
    own_ref, mask_ref, par_ref, w_ref, out_ref, x_scr = refs[2 * count :]
    kept = chunk.kept
    parity = parity_of()
    spots = {j: (g, i) for g, js in enumerate(groups) for i, j in enumerate(js)}
    gather_rows(
        x_scr,
        chunk,
        [[refs_of[spots[j][0]].at[spots[j][1]] for j in range(shards)] for refs_of in (outer_refs, inner_refs)],
    )
    mask = jnp.concatenate([mask_ref[0], mask_ref[3]], axis=0)

    def around(units):
        return [
            masked(expand(x_scr, w_ref, par_ref, k, units), mask) for k in range(2)
        ]

    def convolve(units, cells):
        width = units.stop - units.start
        line = lax.broadcasted_iota(jnp.int32, (kept, width), 0)
        not_first, not_last = None, None
        for at, size in zip(chunk.starts, chunk.widths):
            first, last = line != at, line != at + size - 1
            not_first = first if not_first is None else not_first & first
            not_last = last if not_last is None else not_last & last
        halves = ([], [])
        for k in range(2):
            rows = [
                cells[k][:kept],
                own_ref[k, :kept, units],
                own_ref[k, kept:, units],
                cells[k][kept:],
            ]
            taps = [
                [
                    jnp.where(
                        parity == 0,
                        par_ref[i * 6 + col * 2 + k : i * 6 + col * 2 + k + 1, units],
                        par_ref[(2 - i) * 6 + col * 2 + k : (2 - i) * 6 + col * 2 + k + 1, units],
                    )
                    for col in range(3)
                ]
                for i in range(3)
            ]
            for place in range(2):
                sums = []
                for tap_col in range(3):
                    total = None
                    for i in range(3):
                        term = taps[i][tap_col] * rows[place + i]
                        total = term if total is None else total + term
                    sums.append(total)
                left = jnp.where(not_first, pltpu.roll(sums[0], 1, 0), 0.0)
                right = jnp.where(not_last, pltpu.roll(sums[2], kept - 1, 0), 0.0)
                halves[k].append(sums[1] + left + right + par_ref[20 + k : 21 + k, units])
        for place in range(2):
            hidden = halves[0][place] * silu(halves[1][place])
            out_ref[(1 - place) * kept : (2 - place) * kept, units] = hidden.astype(jnp.bfloat16)

    tiles = tiles_of(w_ref.shape[2])
    cells = around(tiles[0])
    for t, units in enumerate(tiles):
        coming = around(tiles[t + 1]) if t + 1 < len(tiles) else None
        convolve(units, cells)
        cells = coming


def project(weight_ref, hidden_ref, depth, j):
    start = lax.bitwise_xor(lax.axis_index("tensor"), j) * depth
    return lax.dot_general(
        weight_ref[pl.ds(pl.multiple_of(start, GROUP), depth), :],
        hidden_ref[...],
        (((1,), (1,)), ((), ())),
        preferred_element_type=jnp.float32,
    )


def unit_kernel(weight_ref, hidden_ref, *refs, chunk, j):
    out_ref = refs[-1]
    sums = project(weight_ref, hidden_ref, chunk.depth, j)
    for ref in refs[:-1]:
        sums = sums + chunk.get_unit(ref[...].astype(jnp.float32))
    chunk.put_unit(out_ref, sums.astype(jnp.bfloat16))


def share_kernel(weight_ref, hidden_ref, unit_ref, out_ref, *, chunk):
    sums = project(weight_ref, hidden_ref, chunk.depth, 0)
    out_ref[...] = sums + chunk.get_unit(unit_ref[...].astype(jnp.float32))


def final_kernel(width_ref, mask_ref, share_ref, *refs, chunk, sources):
    out_ref = refs[-1]
    if len(refs) > sources + 1:
        out_ref[...] = refs[sources][...]
    sums = share_ref[...]
    for ref in refs[:sources]:
        sums = sums + chunk.get_unit(ref[...].astype(jnp.float32))
    cells = sums.T
    parity = parity_of()
    for place in range(2):
        row = jnp.where(parity == 0, 1 - place, place)
        mask = mask_ref[2 - place][:, :1] > 0
        part = cells[place * chunk.kept : (place + 1) * chunk.kept]
        part = jnp.where(mask, part, 0.0).astype(jnp.bfloat16)
        clips = chunk.clips(width_ref, width_ref.shape[0])
        for clip, width, at in zip(clips, chunk.widths, chunk.starts):
            out_ref[clip, row, :width, :] = part[at : at + width]
            if width < out_ref.shape[2]:
                blank = jnp.zeros((out_ref.shape[2] - width, chunk.depth), jnp.bfloat16)
                out_ref[clip, row, width:, :] = blank


VMEM = pl.BlockSpec(memory_space=pltpu.VMEM)
MIB = 1024 * 1024


def after(value, *others):
    return lax.optimization_barrier((value,) + others)[0]


def on_device_packed(
    latents,
    clip_height,
    clip_width,
    expand_weight,
    expand_bias,
    depth_weight,
    depth_bias,
    project_weight,
):
    batch_size, row_count, col_count, depth = latents.shape
    shards, row_devices = lax.axis_size("tensor"), lax.axis_size("row")
    hidden_count = expand_weight.shape[2]
    full_depth = shards * depth
    chunks = chunks_of(batch_size, col_count, depth)
    count = len(chunks)
    own = pl.pallas_call(
        functools.partial(pack_kernel, chunks=chunks),
        out_shape=[jax.ShapeDtypeStruct((2, c.lines, LANES), jnp.bfloat16) for c in chunks],
        grid_spec=pltpu.PrefetchScalarGridSpec(
            num_scalar_prefetch=1, grid=(), in_specs=[VMEM], out_specs=[VMEM] * count
        ),
        compiler_params=pltpu.CompilerParams(vmem_limit_bytes=16 * MIB),
        name="pack",
    )(clip_width, latents)
    project_turned = project_weight.T

    sibling = [(i, i ^ 1) for i in range(row_devices)]
    beyond = [(i, i + 1) for i in range(1, row_devices - 1, 2)]
    beyond = beyond + [(b, a) for a, b in beyond]
    near = [(i, i ^ 1) for i in range(4)]
    two_off = [(i, i ^ 2) for i in range(4)]
    opposite = [(i, i ^ 3) for i in range(4)]
    middle = [(1, 2), (2, 1)]
    to_end = [(2, 3), (1, 0)]
    from_end = [(0, 1), (3, 2)]

    def edge_rows(packets, groups):
        return [
            [jnp.concatenate([packets[j][side : side + 1] for j in js], axis=0) for js in groups]
            for side in range(2)
        ]

    def send_rows(inner, outer):
        return (
            [lax.ppermute(x, "row", sibling) for x in inner],
            [lax.ppermute(x, "row", beyond) for x in outer],
        )

    def relay(mine, tables, *others):
        second = lax.ppermute(mine, "tensor", two_off)
        first = lax.ppermute(mine, "tensor", near)
        across = lax.ppermute(after(mine, second, *others), "tensor", middle)
        passed = lax.ppermute(after(second, *others), "tensor", to_end)
        return [mine, first, second, after(across, tables) + passed]

    def direct(mine):
        third, second, first = [
            lax.ppermute(mine, "tensor", pairs) for pairs in (opposite, two_off, near)
        ]
        return [mine, first, second, third]

    out = None
    weights, token = pl.pallas_call(
        functools.partial(load_kernel, shards=shards, depth=depth),
        out_shape=[
            jax.ShapeDtypeStruct(expand_weight.shape, jnp.bfloat16),
            jax.ShapeDtypeStruct((8, 128), jnp.float32),
        ],
        in_specs=[pl.BlockSpec(memory_space=pl.ANY)],
        out_specs=[VMEM, VMEM],
        scratch_shapes=[pltpu.SemaphoreType.DMA((2, shards, 2))],
        compiler_params=pltpu.CompilerParams(vmem_limit_bytes=36 * MIB),
        name="load_weights",
    )(after(expand_weight, own[0]))
    taps = after(depth_weight, token)
    parameters, *masks = pl.pallas_call(
        functools.partial(table_kernel, chunks=chunks),
        out_shape=[jax.ShapeDtypeStruct((22, hidden_count), jnp.float32)]
        + [jax.ShapeDtypeStruct((4, c.kept, 128), jnp.float32) for c in chunks],
        grid_spec=pltpu.PrefetchScalarGridSpec(
            num_scalar_prefetch=2, grid=(), in_specs=[VMEM] * 3, out_specs=[VMEM] * (1 + count)
        ),
        compiler_params=pltpu.CompilerParams(vmem_limit_bytes=16 * MIB),
        name="tables",
    )(clip_height, clip_width, taps, expand_bias, depth_bias)
    groups = ((0,), (1, 2), (3,))
    inner, outer = send_rows(*edge_rows(own[:1], groups[:1]))
    packets = relay(own[0], parameters, token, *inner, *outer)
    edges = edge_rows(packets, groups[1:])
    later = send_rows(*edges)
    inner, outer = inner + later[0], outer + later[1]
    upcoming = direct(after(own[1], edges[0][-1], edges[1][-1]))
    for number, chunk in enumerate(chunks):
        if number:
            packets, groups = list(lax.optimization_barrier((*upcoming, hidden))[:shards]), ((0, 1, 2, 3),)
            inner, outer = send_rows(*edge_rows(packets, groups))
            packets[0] = after(packets[0], far)
        rows = pl.pallas_call(
            functools.partial(own_kernel, chunk=chunk, shards=shards),
            out_shape=jax.ShapeDtypeStruct((2, chunk.tokens, hidden_count), jnp.float32),
            in_specs=[VMEM] * (shards + 3),
            out_specs=VMEM,
            scratch_shapes=[pltpu.VMEM((chunk.tokens, full_depth), jnp.bfloat16)],
            compiler_params=pltpu.CompilerParams(vmem_limit_bytes=16 * MIB),
            cost_estimate=pl.CostEstimate(
                flops=1000,
                bytes_accessed=1000,
                transcendentals=0,
            ),
            name="expand_own",
        )(*packets, masks[number], parameters, weights)
        if number:
            inner[0] = after(inner[0], last_unit)
        hidden = pl.pallas_call(
            functools.partial(hidden_kernel, chunk=chunk, shards=shards, groups=groups),
            out_shape=jax.ShapeDtypeStruct((chunk.tokens, hidden_count), jnp.bfloat16),
            in_specs=[VMEM] * (2 * len(groups) + 4),
            out_specs=VMEM,
            scratch_shapes=[pltpu.VMEM((chunk.tokens, full_depth), jnp.bfloat16)],
            compiler_params=pltpu.CompilerParams(vmem_limit_bytes=16 * MIB),
            cost_estimate=pl.CostEstimate(
                flops=1000,
                bytes_accessed=1000,
                transcendentals=0,
            ),
            name="expand_conv",
        )(*inner, *outer, rows, masks[number], parameters, weights)

        cost = pl.CostEstimate(
            flops=2 * chunk.tokens * depth * hidden_count,
            bytes_accessed=2 * depth * hidden_count + 2 * chunk.tokens * hidden_count,
            transcendentals=0,
        )

        def unit(j, *added):
            return pl.pallas_call(
                functools.partial(unit_kernel, chunk=chunk, j=j),
                out_shape=jax.ShapeDtypeStruct(chunk.unit, jnp.bfloat16),
                in_specs=[VMEM] * (2 + len(added)),
                out_specs=VMEM,
                compiler_params=pltpu.CompilerParams(vmem_limit_bytes=16 * MIB),
                cost_estimate=cost,
                name=f"project_{j}",
            )(project_turned, hidden, *added)

        far = unit(3)
        relayed = lax.ppermute(far, "tensor", from_end)
        across = lax.ppermute(far, "tensor", middle)
        close = unit(1)
        if number:
            relayed, across = lax.optimization_barrier((relayed, across, out))[:2]
        else:
            relayed, across = lax.optimization_barrier((relayed, across))
        last_unit = unit(2, relayed)
        distant = lax.ppermute(last_unit, "tensor", two_off)
        arrived = [across, lax.ppermute(after(close, last_unit), "tensor", near)]
        share = pl.pallas_call(
            functools.partial(share_kernel, chunk=chunk),
            out_shape=jax.ShapeDtypeStruct((depth, chunk.tokens), jnp.float32),
            in_specs=[VMEM] * 3,
            out_specs=VMEM,
            compiler_params=pltpu.CompilerParams(vmem_limit_bytes=16 * MIB),
            cost_estimate=pl.CostEstimate(flops=10**10, bytes_accessed=10**8, transcendentals=0),
            name="project_0",
        )(project_turned, hidden, distant)
        extra = [] if out is None else [out]
        out = pl.pallas_call(
            functools.partial(final_kernel, chunk=chunk, sources=len(arrived)),
            out_shape=jax.ShapeDtypeStruct(latents.shape, jnp.bfloat16),
            grid_spec=pltpu.PrefetchScalarGridSpec(
                num_scalar_prefetch=1,
                grid=(),
                in_specs=[VMEM] * (2 + len(arrived) + len(extra)),
                out_specs=VMEM,
            ),
            compiler_params=pltpu.CompilerParams(vmem_limit_bytes=16 * MIB),
            cost_estimate=pl.CostEstimate(flops=10**11, bytes_accessed=10**9, transcendentals=0),
            name="finish",
        )(clip_width, masks[number], share, *arrived, *extra)
    return out


def chunks_of(batch_size, col_count, depth):
    widths = slot_widths(batch_size, col_count)
    half = batch_size // 2
    return [Chunk(slots, widths, depth) for slots in (list(range(half)), list(range(half, batch_size)))]


def on_device(latents, clip_height, clip_width, expand_weight, *rest_of):
    batch_size, row_count, col_count, depth = latents.shape
    fits = (
        batch_size >= 2
        and row_count == 2
        and lax.axis_size("row") % 2 == 0
        and lax.axis_size("tensor") == 4
        and depth > LANES
        and (depth - LANES) % GROUP == 0
        and depth % GROUP == 0
        and all(
            c.block in (128, 256, 512) and c.kept % GROUP == 0 and c.left in (0, 64)
            for c in chunks_of(batch_size, col_count, depth)
        )
    )
    run = on_device_packed if fits else on_device_plain
    return run(latents, clip_height, clip_width, expand_weight, *rest_of)


def solution(mesh):
    in_specs = (
        P(None, "row", None, "tensor"),
        P(),
        P(),
        P(None, None, "tensor"),
        P(None, "tensor"),
        P(None, None, None, "tensor"),
        P(None, "tensor"),
        P("tensor", None),
    )
    out_specs = P(None, "row", None, "tensor")
    return jax.shard_map(
        on_device, mesh=mesh, in_specs=in_specs, out_specs=out_specs, check_vma=False
    )
```

```python
import functools

import jax
import jax.numpy as jnp
from jax import lax
from jax.experimental import pallas as pl
from jax.experimental.pallas import tpu as pltpu
from jax.sharding import PartitionSpec as P

LANES = 512
GROUP = 16
TILE = 256


def halo_rows(cells):
    count = lax.axis_size("row")
    ends = count - 1
    head = cells[:, :1]
    tail = cells[:, -1:]
    above = lax.ppermute(tail, "row", [(i, i + 1) for i in range(ends)])
    below = lax.ppermute(head, "row", [(i + 1, i) for i in range(ends)])
    return jnp.concatenate([above, cells, below], axis=1)


def depthwise(padded, depth_weight, depth_bias, row_count, col_count):
    widened = jnp.pad(padded, ((0, 0), (0, 0), (1, 1), (0, 0), (0, 0)))
    out_shape = (widened.shape[0], row_count, col_count) + widened.shape[3:]
    depth_out = jnp.zeros(out_shape, jnp.float32) + depth_bias
    for tap_row in range(3):
        for tap_col in range(3):
            depth_out = (
                depth_out
                + depth_weight[tap_row, tap_col]
                * widened[:, tap_row : tap_row + row_count, tap_col : tap_col + col_count]
            )
    return depth_out


def on_device_plain(
    latents,
    clip_height,
    clip_width,
    expand_weight,
    expand_bias,
    depth_weight,
    depth_bias,
    project_weight,
):
    batch_size, row_count, col_count, depth = latents.shape
    tokens = batch_size * row_count * col_count
    first_row = lax.axis_index("row") * row_count
    row_ids = first_row + jnp.arange(row_count, dtype=jnp.int32)
    col_ids = jnp.arange(col_count, dtype=jnp.int32)
    valid_mask = (
        (row_ids[None, :, None] < clip_height[:, None, None])
        & (col_ids[None, None, :] < clip_width[:, None, None])
    ).astype(jnp.float32)[..., None]
    channels = latents.reshape(tokens, depth).T
    gathered = lax.all_gather(channels, "tensor", axis=0, tiled=True)
    pre_act = jnp.einsum("dt,kdf->tkf", gathered, expand_weight, preferred_element_type=jnp.float32)
    pre_act = pre_act.reshape(batch_size, row_count, col_count, 2, -1)
    expanded = (jax.nn.silu(pre_act + expand_bias) * valid_mask[..., None]).astype(jnp.bfloat16)
    padded = halo_rows(expanded)
    depth_out = depthwise(padded, depth_weight, depth_bias, row_count, col_count)
    hidden = (depth_out[:, :, :, 0] * jax.nn.silu(depth_out[:, :, :, 1])).astype(jnp.bfloat16)
    partial_term = jnp.einsum(
        "tf,fd->dt", hidden.reshape(tokens, -1), project_weight, preferred_element_type=jnp.float32
    ).astype(jnp.bfloat16)
    summed = lax.psum_scatter(partial_term, "tensor", scatter_dimension=0, tiled=True)
    summed = summed.T.reshape(latents.shape).astype(jnp.float32)
    return (summed * valid_mask).astype(jnp.bfloat16)


def slot_clips(width_ref, batch_size):
    narrow, least = jnp.int32(0), width_ref[0]
    for b in range(1, batch_size):
        closer = width_ref[b] < least
        narrow = jnp.where(closer, b, narrow)
        least = jnp.where(closer, width_ref[b], least)
    return [jnp.where(narrow <= s, s + 1, s) for s in range(batch_size - 1)] + [narrow]


def slot_widths(batch_size, col_count):
    return [col_count] * (batch_size - 1) + [col_count // 2]


class Chunk:
    def __init__(self, slots, widths, depth):
        self.slots = slots
        self.widths = [widths[s] for s in slots]
        self.starts = [sum(self.widths[:i]) for i in range(len(slots))]
        self.kept = sum(self.widths)
        self.block = -(-self.kept // 128) * 128
        self.depth, self.rest = depth, depth - LANES
        across = LANES // self.block
        groups = self.rest // GROUP
        self.places = [(g // across * GROUP, g % across * self.block) for g in range(groups)]
        self.lines = self.kept + -(-groups // across) * GROUP
        self.tokens = 2 * self.kept
        self.full, self.left = self.tokens // 128, self.tokens % 128
        self.upper = -(-depth // (2 * GROUP)) * GROUP
        self.unit = (self.full * depth + (self.upper if self.left else 0), 128)

    def clips(self, width_ref, batch_size):
        order = slot_clips(width_ref, batch_size)
        return [order[s] for s in self.slots]

    def mask_column(self, height_ref, width_ref, row_id):
        pieces = []
        clips = self.clips(width_ref, width_ref.shape[0])
        for clip, width in zip(clips, self.widths):
            bound = jnp.where((row_id >= 0) & (row_id < height_ref[clip]), width_ref[clip], 0)
            col = lax.broadcasted_iota(jnp.int32, (width, 128), 0)
            pieces.append((col < bound).astype(jnp.float32))
        return jnp.concatenate(pieces, axis=0)

    def put_unit(self, unit_ref, sums):
        depth, at = self.depth, self.full * self.depth
        for b in range(self.full):
            unit_ref[b * depth : (b + 1) * depth, :] = sums[:, b * 128 : (b + 1) * 128]
        if self.left:
            tail = sums[:, self.full * 128 :]
            lower = depth - self.upper
            unit_ref[at : at + self.upper, : self.left] = tail[: self.upper]
            unit_ref[at : at + lower, self.left :] = tail[self.upper :]
            if lower < self.upper:
                unit_ref[at + lower :, self.left :] = jnp.zeros(
                    (self.upper - lower, 128 - self.left), sums.dtype
                )

    def get_unit(self, unit):
        depth, at = self.depth, self.full * self.depth
        blocks = [unit[b * depth : (b + 1) * depth, :] for b in range(self.full)]
        if self.left:
            lower = depth - self.upper
            blocks.append(
                jnp.concatenate(
                    [unit[at : at + self.upper, : self.left], unit[at : at + lower, self.left :]], axis=0
                )
            )
        return jnp.concatenate(blocks, axis=1)


def parity_of():
    return lax.rem(lax.axis_index("row"), 2)


def row_of(place, parity):
    return jnp.where(parity == 0, (-1, 0, 1, 2)[place], (2, 1, 0, -1)[place])


def silu(v):
    h = 0.5 * v
    return h + h * jnp.tanh(h)


def pack_kernel(width_ref, x_ref, *out_refs, chunks):
    parity = parity_of()
    for chunk, out_ref in zip(chunks, out_refs):
        for place in range(2):
            row = jnp.where(parity == 0, 1 - place, place)
            tails = []
            for clip, width, at in zip(
                chunk.clips(width_ref, x_ref.shape[0]), chunk.widths, chunk.starts
            ):
                out_ref[place, at : at + width, :] = x_ref[clip, row, :width, :LANES]
                tails.append(x_ref[clip, row, :width, LANES:].astype(jnp.float32))
            if chunk.block > chunk.kept:
                tails.append(jnp.zeros((chunk.block - chunk.kept, chunk.rest), jnp.float32))
            turned = jnp.concatenate(tails, axis=0).T.astype(jnp.bfloat16)
            kept = chunk.kept
            out_ref[place, kept:, :] = jnp.zeros((chunk.lines - kept, LANES), jnp.bfloat16)
            for g, (down, over) in enumerate(chunk.places):
                out_ref[place, kept + down : kept + down + GROUP, over : over + chunk.block] = turned[
                    g * GROUP : (g + 1) * GROUP
                ]


def tiles_of(hidden_count):
    return [slice(at, min(at + TILE, hidden_count)) for at in range(0, hidden_count, TILE)]


def gather_rows(x_scr, chunk, rows):
    kept = chunk.kept
    for place, packets in enumerate(rows):
        lines = slice(place * kept, (place + 1) * kept)
        tails = []
        for j, packet in enumerate(packets):
            x_scr[lines, j * LANES : (j + 1) * LANES] = packet[:kept, :]
            for down, over in chunk.places:
                tails.append(packet[kept + down : kept + down + GROUP, over : over + chunk.block])
        turned = jnp.concatenate(tails, axis=0).astype(jnp.float32).T
        x_scr[lines, len(packets) * LANES :] = turned[:kept].astype(jnp.bfloat16)


def load_kernel(w_ref, out_ref, token_ref, sems, *, shards, depth):
    token_ref[...] = jnp.zeros_like(token_ref)
    me = lax.axis_index("tensor")
    rest = depth - LANES
    copies = []
    for k in range(2):
        for j in range(shards):
            base = lax.bitwise_xor(me, j) * depth
            for part, (source, size, target) in enumerate(
                ((base, LANES, j * LANES), (base + LANES, rest, shards * LANES + j * rest))
            ):
                copies.append(
                    pltpu.make_async_copy(
                        w_ref.at[k, pl.ds(pl.multiple_of(source, GROUP), size)],
                        out_ref.at[k, pl.ds(target, size)],
                        sems.at[k, j, part],
                    )
                )
    for copy in copies:
        copy.start()
    for copy in copies:
        copy.wait()


def table_kernel(height_ref, width_ref, dw_ref, eb_ref, db_ref, par_ref, *mask_refs, chunks):
    parity = parity_of()
    for chunk, mask_ref in zip(chunks, mask_refs):
        for place in range(4):
            row_id = lax.axis_index("row") * 2 + row_of(place, parity)
            mask_ref[place] = chunk.mask_column(height_ref, width_ref, row_id)
    for i in range(3):
        for col in range(3):
            par_ref[i * 6 + col * 2 : i * 6 + col * 2 + 2, :] = dw_ref[i, col]
    par_ref[18:20, :] = eb_ref[...]
    par_ref[20:22, :] = db_ref[...]


def expand(x_scr, w_ref, par_ref, k, units):
    pre_act = jnp.dot(x_scr[...], w_ref[k, :, units], preferred_element_type=jnp.float32)
    return silu(pre_act + par_ref[18 + k : 19 + k, units])


def masked(cells, mask):
    width = cells.shape[1]
    return cells * jnp.concatenate([mask] * -(-width // 128), axis=1)[:, :width]


def own_kernel(*refs, chunk, shards):
    packet_refs, (mask_ref, par_ref, w_ref, out_ref, x_scr) = refs[:shards], refs[shards:]
    kept = chunk.kept
    gather_rows(x_scr, chunk, [[p.at[1] for p in packet_refs], [p.at[0] for p in packet_refs]])
    mask = jnp.concatenate([mask_ref[1], mask_ref[2]], axis=0)
    for units in tiles_of(w_ref.shape[2]):
        for k in range(2):
            out_ref[k, :, units] = masked(expand(x_scr, w_ref, par_ref, k, units), mask)


def hidden_kernel(*refs, chunk, shards, groups):
    count = len(groups)
    inner_refs, outer_refs = refs[:count], refs[count : 2 * count]
    own_ref, mask_ref, par_ref, w_ref, out_ref, x_scr = refs[2 * count :]
    kept = chunk.kept
    parity = parity_of()
    spots = {j: (g, i) for g, js in enumerate(groups) for i, j in enumerate(js)}
    gather_rows(
        x_scr,
        chunk,
        [[refs_of[spots[j][0]].at[spots[j][1]] for j in range(shards)] for refs_of in (outer_refs, inner_refs)],
    )
    mask = jnp.concatenate([mask_ref[0], mask_ref[3]], axis=0)

    def around(units):
        return [
            masked(expand(x_scr, w_ref, par_ref, k, units), mask) for k in range(2)
        ]

    def convolve(units, cells):
        width = units.stop - units.start
        line = lax.broadcasted_iota(jnp.int32, (kept, width), 0)
        not_first, not_last = None, None
        for at, size in zip(chunk.starts, chunk.widths):
            first, last = line != at, line != at + size - 1
            not_first = first if not_first is None else not_first & first
            not_last = last if not_last is None else not_last & last
        halves = ([], [])
        for k in range(2):
            rows = [
                cells[k][:kept],
                own_ref[k, :kept, units],
                own_ref[k, kept:, units],
                cells[k][kept:],
            ]
            taps = [
                [
                    jnp.where(
                        parity == 0,
                        par_ref[i * 6 + col * 2 + k : i * 6 + col * 2 + k + 1, units],
                        par_ref[(2 - i) * 6 + col * 2 + k : (2 - i) * 6 + col * 2 + k + 1, units],
                    )
                    for col in range(3)
                ]
                for i in range(3)
            ]
            for place in range(2):
                sums = []
                for tap_col in range(3):
                    total = None
                    for i in range(3):
                        term = taps[i][tap_col] * rows[place + i]
                        total = term if total is None else total + term
                    sums.append(total)
                left = jnp.where(not_first, pltpu.roll(sums[0], 1, 0), 0.0)
                right = jnp.where(not_last, pltpu.roll(sums[2], kept - 1, 0), 0.0)
                halves[k].append(sums[1] + left + right + par_ref[20 + k : 21 + k, units])
        for place in range(2):
            hidden = halves[0][place] * silu(halves[1][place])
            out_ref[(1 - place) * kept : (2 - place) * kept, units] = hidden.astype(jnp.bfloat16)

    tiles = tiles_of(w_ref.shape[2])
    cells = around(tiles[0])
    for t, units in enumerate(tiles):
        coming = around(tiles[t + 1]) if t + 1 < len(tiles) else None
        convolve(units, cells)
        cells = coming


def project(weight_ref, hidden_ref, depth, j):
    start = lax.bitwise_xor(lax.axis_index("tensor"), j) * depth
    return lax.dot_general(
        weight_ref[pl.ds(pl.multiple_of(start, GROUP), depth), :],
        hidden_ref[...],
        (((1,), (1,)), ((), ())),
        preferred_element_type=jnp.float32,
    )


def unit_kernel(weight_ref, hidden_ref, *refs, chunk, j):
    out_ref = refs[-1]
    sums = project(weight_ref, hidden_ref, chunk.depth, j)
    for ref in refs[:-1]:
        sums = sums + chunk.get_unit(ref[...].astype(jnp.float32))
    chunk.put_unit(out_ref, sums.astype(jnp.bfloat16))


def share_kernel(weight_ref, hidden_ref, unit_ref, out_ref, *, chunk):
    sums = project(weight_ref, hidden_ref, chunk.depth, 0)
    out_ref[...] = sums + chunk.get_unit(unit_ref[...].astype(jnp.float32))


def final_kernel(width_ref, mask_ref, share_ref, *refs, chunk, sources):
    out_ref = refs[-1]
    if len(refs) > sources + 1:
        out_ref[...] = refs[sources][...]
    sums = share_ref[...]
    for ref in refs[:sources]:
        sums = sums + chunk.get_unit(ref[...].astype(jnp.float32))
    cells = sums.T
    parity = parity_of()
    for place in range(2):
        row = jnp.where(parity == 0, 1 - place, place)
        mask = mask_ref[2 - place][:, :1] > 0
        part = cells[place * chunk.kept : (place + 1) * chunk.kept]
        part = jnp.where(mask, part, 0.0).astype(jnp.bfloat16)
        clips = chunk.clips(width_ref, width_ref.shape[0])
        for clip, width, at in zip(clips, chunk.widths, chunk.starts):
            out_ref[clip, row, :width, :] = part[at : at + width]
            if width < out_ref.shape[2]:
                blank = jnp.zeros((out_ref.shape[2] - width, chunk.depth), jnp.bfloat16)
                out_ref[clip, row, width:, :] = blank


VMEM = pl.BlockSpec(memory_space=pltpu.VMEM)
MIB = 1024 * 1024


def after(value, *others):
    return lax.optimization_barrier((value,) + others)[0]


def on_device_packed(
    latents,
    clip_height,
    clip_width,
    expand_weight,
    expand_bias,
    depth_weight,
    depth_bias,
    project_weight,
):
    batch_size, row_count, col_count, depth = latents.shape
    shards, row_devices = lax.axis_size("tensor"), lax.axis_size("row")
    hidden_count = expand_weight.shape[2]
    full_depth = shards * depth
    chunks = chunks_of(batch_size, col_count, depth)
    count = len(chunks)
    own = pl.pallas_call(
        functools.partial(pack_kernel, chunks=chunks),
        out_shape=[jax.ShapeDtypeStruct((2, c.lines, LANES), jnp.bfloat16) for c in chunks],
        grid_spec=pltpu.PrefetchScalarGridSpec(
            num_scalar_prefetch=1, grid=(), in_specs=[VMEM], out_specs=[VMEM] * count
        ),
        compiler_params=pltpu.CompilerParams(vmem_limit_bytes=16 * MIB),
        name="pack",
    )(clip_width, latents)
    project_turned = project_weight.T

    sibling = [(i, i ^ 1) for i in range(row_devices)]
    beyond = [(i, i + 1) for i in range(1, row_devices - 1, 2)]
    beyond = beyond + [(b, a) for a, b in beyond]
    near = [(i, i ^ 1) for i in range(4)]
    two_off = [(i, i ^ 2) for i in range(4)]
    opposite = [(i, i ^ 3) for i in range(4)]
    middle = [(1, 2), (2, 1)]
    to_end = [(2, 3), (1, 0)]
    from_end = [(0, 1), (3, 2)]

    def edge_rows(packets, groups):
        return [
            [jnp.concatenate([packets[j][side : side + 1] for j in js], axis=0) for js in groups]
            for side in range(2)
        ]

    def send_rows(inner, outer):
        return (
            [lax.ppermute(x, "row", sibling) for x in inner],
            [lax.ppermute(x, "row", beyond) for x in outer],
        )

    def relay(mine, tables, *others):
        second = lax.ppermute(mine, "tensor", two_off)
        first = lax.ppermute(mine, "tensor", near)
        across = lax.ppermute(after(mine, second, *others), "tensor", middle)
        passed = lax.ppermute(after(second, *others), "tensor", to_end)
        return [mine, first, second, after(across, tables) + passed]

    def direct(mine):
        third, second, first = [
            lax.ppermute(mine, "tensor", pairs) for pairs in (opposite, two_off, near)
        ]
        return [mine, first, second, third]

    out = None
    weights, token = pl.pallas_call(
        functools.partial(load_kernel, shards=shards, depth=depth),
        out_shape=[
            jax.ShapeDtypeStruct(expand_weight.shape, jnp.bfloat16),
            jax.ShapeDtypeStruct((8, 128), jnp.float32),
        ],
        in_specs=[pl.BlockSpec(memory_space=pl.ANY)],
        out_specs=[VMEM, VMEM],
        scratch_shapes=[pltpu.SemaphoreType.DMA((2, shards, 2))],
        compiler_params=pltpu.CompilerParams(vmem_limit_bytes=36 * MIB),
        name="load_weights",
    )(after(expand_weight, own[0]))
    taps = after(depth_weight, token)
    parameters, *masks = pl.pallas_call(
        functools.partial(table_kernel, chunks=chunks),
        out_shape=[jax.ShapeDtypeStruct((22, hidden_count), jnp.float32)]
        + [jax.ShapeDtypeStruct((4, c.kept, 128), jnp.float32) for c in chunks],
        grid_spec=pltpu.PrefetchScalarGridSpec(
            num_scalar_prefetch=2, grid=(), in_specs=[VMEM] * 3, out_specs=[VMEM] * (1 + count)
        ),
        compiler_params=pltpu.CompilerParams(vmem_limit_bytes=16 * MIB),
        name="tables",
    )(clip_height, clip_width, taps, expand_bias, depth_bias)
    groups = ((0,), (1, 2), (3,))
    inner, outer = send_rows(*edge_rows(own[:1], groups[:1]))
    packets = relay(own[0], parameters, token, *inner, *outer)
    edges = edge_rows(packets, groups[1:])
    later = send_rows(*edges)
    inner, outer = inner + later[0], outer + later[1]
    upcoming = direct(after(own[1], edges[0][-1], edges[1][-1]))
    for number, chunk in enumerate(chunks):
        if number:
            packets, groups = list(lax.optimization_barrier((*upcoming, hidden))[:shards]), ((0, 1, 2, 3),)
            inner, outer = send_rows(*edge_rows(packets, groups))
            packets[0] = after(packets[0], far)
        rows = pl.pallas_call(
            functools.partial(own_kernel, chunk=chunk, shards=shards),
            out_shape=jax.ShapeDtypeStruct((2, chunk.tokens, hidden_count), jnp.float32),
            in_specs=[VMEM] * (shards + 3),
            out_specs=VMEM,
            scratch_shapes=[pltpu.VMEM((chunk.tokens, full_depth), jnp.bfloat16)],
            compiler_params=pltpu.CompilerParams(vmem_limit_bytes=16 * MIB),
            cost_estimate=pl.CostEstimate(
                flops=1000,
                bytes_accessed=1000,
                transcendentals=0,
            ),
            name="expand_own",
        )(*packets, masks[number], parameters, weights)
        if number:
            inner[0] = after(inner[0], last_unit)
        hidden = pl.pallas_call(
            functools.partial(hidden_kernel, chunk=chunk, shards=shards, groups=groups),
            out_shape=jax.ShapeDtypeStruct((chunk.tokens, hidden_count), jnp.bfloat16),
            in_specs=[VMEM] * (2 * len(groups) + 4),
            out_specs=VMEM,
            scratch_shapes=[pltpu.VMEM((chunk.tokens, full_depth), jnp.bfloat16)],
            compiler_params=pltpu.CompilerParams(vmem_limit_bytes=16 * MIB),
            cost_estimate=pl.CostEstimate(
                flops=1000,
                bytes_accessed=1000,
                transcendentals=0,
            ),
            name="expand_conv",
        )(*inner, *outer, rows, masks[number], parameters, weights)

        cost = pl.CostEstimate(
            flops=2 * chunk.tokens * depth * hidden_count,
            bytes_accessed=2 * depth * hidden_count + 2 * chunk.tokens * hidden_count,
            transcendentals=0,
        )

        def unit(j, *added):
            return pl.pallas_call(
                functools.partial(unit_kernel, chunk=chunk, j=j),
                out_shape=jax.ShapeDtypeStruct(chunk.unit, jnp.bfloat16),
                in_specs=[VMEM] * (2 + len(added)),
                out_specs=VMEM,
                compiler_params=pltpu.CompilerParams(vmem_limit_bytes=16 * MIB),
                cost_estimate=cost,
                name=f"project_{j}",
            )(project_turned, hidden, *added)

        far = unit(3)
        relayed = lax.ppermute(far, "tensor", from_end)
        across = lax.ppermute(far, "tensor", middle)
        close = unit(1)
        if number:
            relayed = after(relayed, out)
        else:
            relayed, across = lax.optimization_barrier((relayed, across))
        last_unit = unit(2, relayed)
        distant = lax.ppermute(last_unit, "tensor", two_off)
        close = after(close, last_unit, across) if number else after(close, last_unit)
        arrived = [across, lax.ppermute(close, "tensor", near)]
        share = pl.pallas_call(
            functools.partial(share_kernel, chunk=chunk),
            out_shape=jax.ShapeDtypeStruct((depth, chunk.tokens), jnp.float32),
            in_specs=[VMEM] * 3,
            out_specs=VMEM,
            compiler_params=pltpu.CompilerParams(vmem_limit_bytes=16 * MIB),
            cost_estimate=pl.CostEstimate(flops=10**10, bytes_accessed=10**8, transcendentals=0),
            name="project_0",
        )(project_turned, hidden, distant)
        extra = [] if out is None else [out]
        out = pl.pallas_call(
            functools.partial(final_kernel, chunk=chunk, sources=len(arrived)),
            out_shape=jax.ShapeDtypeStruct(latents.shape, jnp.bfloat16),
            grid_spec=pltpu.PrefetchScalarGridSpec(
                num_scalar_prefetch=1,
                grid=(),
                in_specs=[VMEM] * (2 + len(arrived) + len(extra)),
                out_specs=VMEM,
            ),
            compiler_params=pltpu.CompilerParams(vmem_limit_bytes=16 * MIB),
            cost_estimate=pl.CostEstimate(flops=10**11, bytes_accessed=10**9, transcendentals=0),
            name="finish",
        )(clip_width, masks[number], share, *arrived, *extra)
    return out


def chunks_of(batch_size, col_count, depth):
    widths = slot_widths(batch_size, col_count)
    half = batch_size // 2
    return [Chunk(slots, widths, depth) for slots in (list(range(half)), list(range(half, batch_size)))]


def on_device(latents, clip_height, clip_width, expand_weight, *rest_of):
    batch_size, row_count, col_count, depth = latents.shape
    fits = (
        batch_size >= 2
        and row_count == 2
        and lax.axis_size("row") % 2 == 0
        and lax.axis_size("tensor") == 4
        and depth > LANES
        and (depth - LANES) % GROUP == 0
        and depth % GROUP == 0
        and all(
            c.block in (128, 256, 512) and c.kept % GROUP == 0 and c.left in (0, 64)
            for c in chunks_of(batch_size, col_count, depth)
        )
    )
    run = on_device_packed if fits else on_device_plain
    return run(latents, clip_height, clip_width, expand_weight, *rest_of)


def solution(mesh):
    in_specs = (
        P(None, "row", None, "tensor"),
        P(),
        P(),
        P(None, None, "tensor"),
        P(None, "tensor"),
        P(None, None, None, "tensor"),
        P(None, "tensor"),
        P("tensor", None),
    )
    out_specs = P(None, "row", None, "tensor")
    return jax.shard_map(
        on_device, mesh=mesh, in_specs=in_specs, out_specs=out_specs, check_vma=False
    )
```

```python
import functools

import jax
import jax.numpy as jnp
from jax import lax
from jax.experimental import pallas as pl
from jax.experimental.pallas import tpu as pltpu
from jax.sharding import PartitionSpec as P

LANES = 512
GROUP = 16
TILE = 256


def halo_rows(cells):
    count = lax.axis_size("row")
    ends = count - 1
    head = cells[:, :1]
    tail = cells[:, -1:]
    above = lax.ppermute(tail, "row", [(i, i + 1) for i in range(ends)])
    below = lax.ppermute(head, "row", [(i + 1, i) for i in range(ends)])
    return jnp.concatenate([above, cells, below], axis=1)


def depthwise(padded, depth_weight, depth_bias, row_count, col_count):
    widened = jnp.pad(padded, ((0, 0), (0, 0), (1, 1), (0, 0), (0, 0)))
    out_shape = (widened.shape[0], row_count, col_count) + widened.shape[3:]
    depth_out = jnp.zeros(out_shape, jnp.float32) + depth_bias
    for tap_row in range(3):
        for tap_col in range(3):
            depth_out = (
                depth_out
                + depth_weight[tap_row, tap_col]
                * widened[:, tap_row : tap_row + row_count, tap_col : tap_col + col_count]
            )
    return depth_out


def on_device_plain(
    latents,
    clip_height,
    clip_width,
    expand_weight,
    expand_bias,
    depth_weight,
    depth_bias,
    project_weight,
):
    batch_size, row_count, col_count, depth = latents.shape
    tokens = batch_size * row_count * col_count
    first_row = lax.axis_index("row") * row_count
    row_ids = first_row + jnp.arange(row_count, dtype=jnp.int32)
    col_ids = jnp.arange(col_count, dtype=jnp.int32)
    valid_mask = (
        (row_ids[None, :, None] < clip_height[:, None, None])
        & (col_ids[None, None, :] < clip_width[:, None, None])
    ).astype(jnp.float32)[..., None]
    channels = latents.reshape(tokens, depth).T
    gathered = lax.all_gather(channels, "tensor", axis=0, tiled=True)
    pre_act = jnp.einsum("dt,kdf->tkf", gathered, expand_weight, preferred_element_type=jnp.float32)
    pre_act = pre_act.reshape(batch_size, row_count, col_count, 2, -1)
    expanded = (jax.nn.silu(pre_act + expand_bias) * valid_mask[..., None]).astype(jnp.bfloat16)
    padded = halo_rows(expanded)
    depth_out = depthwise(padded, depth_weight, depth_bias, row_count, col_count)
    hidden = (depth_out[:, :, :, 0] * jax.nn.silu(depth_out[:, :, :, 1])).astype(jnp.bfloat16)
    partial_term = jnp.einsum(
        "tf,fd->dt", hidden.reshape(tokens, -1), project_weight, preferred_element_type=jnp.float32
    ).astype(jnp.bfloat16)
    summed = lax.psum_scatter(partial_term, "tensor", scatter_dimension=0, tiled=True)
    summed = summed.T.reshape(latents.shape).astype(jnp.float32)
    return (summed * valid_mask).astype(jnp.bfloat16)


def slot_clips(width_ref, batch_size):
    narrow, least = jnp.int32(0), width_ref[0]
    for b in range(1, batch_size):
        closer = width_ref[b] < least
        narrow = jnp.where(closer, b, narrow)
        least = jnp.where(closer, width_ref[b], least)
    return [jnp.where(narrow <= s, s + 1, s) for s in range(batch_size - 1)] + [narrow]


def slot_widths(batch_size, col_count):
    return [col_count] * (batch_size - 1) + [col_count // 2]


class Chunk:
    def __init__(self, slots, widths, depth):
        self.slots = slots
        self.widths = [widths[s] for s in slots]
        self.starts = [sum(self.widths[:i]) for i in range(len(slots))]
        self.kept = sum(self.widths)
        self.block = -(-self.kept // 128) * 128
        self.depth, self.rest = depth, depth - LANES
        across = LANES // self.block
        groups = self.rest // GROUP
        self.places = [(g // across * GROUP, g % across * self.block) for g in range(groups)]
        self.lines = self.kept + -(-groups // across) * GROUP
        self.tokens = 2 * self.kept
        self.full, self.left = self.tokens // 128, self.tokens % 128
        self.upper = -(-depth // (2 * GROUP)) * GROUP
        self.unit = (self.full * depth + (self.upper if self.left else 0), 128)

    def clips(self, width_ref, batch_size):
        order = slot_clips(width_ref, batch_size)
        return [order[s] for s in self.slots]

    def mask_column(self, height_ref, width_ref, row_id):
        pieces = []
        clips = self.clips(width_ref, width_ref.shape[0])
        for clip, width in zip(clips, self.widths):
            bound = jnp.where((row_id >= 0) & (row_id < height_ref[clip]), width_ref[clip], 0)
            col = lax.broadcasted_iota(jnp.int32, (width, 128), 0)
            pieces.append((col < bound).astype(jnp.float32))
        return jnp.concatenate(pieces, axis=0)

    def put_unit(self, unit_ref, sums):
        depth, at = self.depth, self.full * self.depth
        for b in range(self.full):
            unit_ref[b * depth : (b + 1) * depth, :] = sums[:, b * 128 : (b + 1) * 128]
        if self.left:
            tail = sums[:, self.full * 128 :]
            lower = depth - self.upper
            unit_ref[at : at + self.upper, : self.left] = tail[: self.upper]
            unit_ref[at : at + lower, self.left :] = tail[self.upper :]
            if lower < self.upper:
                unit_ref[at + lower :, self.left :] = jnp.zeros(
                    (self.upper - lower, 128 - self.left), sums.dtype
                )

    def get_unit(self, unit):
        depth, at = self.depth, self.full * self.depth
        blocks = [unit[b * depth : (b + 1) * depth, :] for b in range(self.full)]
        if self.left:
            lower = depth - self.upper
            blocks.append(
                jnp.concatenate(
                    [unit[at : at + self.upper, : self.left], unit[at : at + lower, self.left :]], axis=0
                )
            )
        return jnp.concatenate(blocks, axis=1)


def parity_of():
    return lax.rem(lax.axis_index("row"), 2)


def row_of(place, parity):
    return jnp.where(parity == 0, (-1, 0, 1, 2)[place], (2, 1, 0, -1)[place])


def silu(v):
    h = 0.5 * v
    return h + h * jnp.tanh(h)


def pack_kernel(width_ref, x_ref, *out_refs, chunks):
    parity = parity_of()
    for chunk, out_ref in zip(chunks, out_refs):
        for place in range(2):
            row = jnp.where(parity == 0, 1 - place, place)
            tails = []
            for clip, width, at in zip(
                chunk.clips(width_ref, x_ref.shape[0]), chunk.widths, chunk.starts
            ):
                out_ref[place, at : at + width, :] = x_ref[clip, row, :width, :LANES]
                tails.append(x_ref[clip, row, :width, LANES:].astype(jnp.float32))
            if chunk.block > chunk.kept:
                tails.append(jnp.zeros((chunk.block - chunk.kept, chunk.rest), jnp.float32))
            turned = jnp.concatenate(tails, axis=0).T.astype(jnp.bfloat16)
            kept = chunk.kept
            out_ref[place, kept:, :] = jnp.zeros((chunk.lines - kept, LANES), jnp.bfloat16)
            for g, (down, over) in enumerate(chunk.places):
                out_ref[place, kept + down : kept + down + GROUP, over : over + chunk.block] = turned[
                    g * GROUP : (g + 1) * GROUP
                ]


def tiles_of(hidden_count):
    return [slice(at, min(at + TILE, hidden_count)) for at in range(0, hidden_count, TILE)]


def gather_rows(x_scr, chunk, rows):
    kept = chunk.kept
    for place, packets in enumerate(rows):
        lines = slice(place * kept, (place + 1) * kept)
        tails = []
        for j, packet in enumerate(packets):
            x_scr[lines, j * LANES : (j + 1) * LANES] = packet[:kept, :]
            for down, over in chunk.places:
                tails.append(packet[kept + down : kept + down + GROUP, over : over + chunk.block])
        turned = jnp.concatenate(tails, axis=0).astype(jnp.float32).T
        x_scr[lines, len(packets) * LANES :] = turned[:kept].astype(jnp.bfloat16)


def load_kernel(w_ref, out_ref, token_ref, sems, *, shards, depth):
    token_ref[...] = jnp.zeros_like(token_ref)
    me = lax.axis_index("tensor")
    rest = depth - LANES
    copies = []
    for k in range(2):
        for j in range(shards):
            base = lax.bitwise_xor(me, j) * depth
            for part, (source, size, target) in enumerate(
                ((base, LANES, j * LANES), (base + LANES, rest, shards * LANES + j * rest))
            ):
                copies.append(
                    pltpu.make_async_copy(
                        w_ref.at[k, pl.ds(pl.multiple_of(source, GROUP), size)],
                        out_ref.at[k, pl.ds(target, size)],
                        sems.at[k, j, part],
                    )
                )
    for copy in copies:
        copy.start()
    for copy in copies:
        copy.wait()


def table_kernel(height_ref, width_ref, dw_ref, eb_ref, db_ref, par_ref, *mask_refs, chunks):
    parity = parity_of()
    for chunk, mask_ref in zip(chunks, mask_refs):
        for place in range(4):
            row_id = lax.axis_index("row") * 2 + row_of(place, parity)
            mask_ref[place] = chunk.mask_column(height_ref, width_ref, row_id)
    for i in range(3):
        for col in range(3):
            par_ref[i * 6 + col * 2 : i * 6 + col * 2 + 2, :] = dw_ref[i, col]
    par_ref[18:20, :] = eb_ref[...]
    par_ref[20:22, :] = db_ref[...]


def expand(x_scr, w_ref, par_ref, k, units):
    pre_act = jnp.dot(x_scr[...], w_ref[k, :, units], preferred_element_type=jnp.float32)
    return silu(pre_act + par_ref[18 + k : 19 + k, units])


def masked(cells, mask):
    width = cells.shape[1]
    return cells * jnp.concatenate([mask] * -(-width // 128), axis=1)[:, :width]


def own_kernel(*refs, chunk, shards):
    packet_refs, (mask_ref, par_ref, w_ref, out_ref, x_scr) = refs[:shards], refs[shards:]
    kept = chunk.kept
    gather_rows(x_scr, chunk, [[p.at[1] for p in packet_refs], [p.at[0] for p in packet_refs]])
    mask = jnp.concatenate([mask_ref[1], mask_ref[2]], axis=0)
    for units in tiles_of(w_ref.shape[2]):
        for k in range(2):
            out_ref[k, :, units] = masked(expand(x_scr, w_ref, par_ref, k, units), mask)


def hidden_kernel(*refs, chunk, shards, groups):
    count = len(groups)
    inner_refs, outer_refs = refs[:count], refs[count : 2 * count]
    own_ref, mask_ref, par_ref, w_ref, out_ref, x_scr = refs[2 * count :]
    kept = chunk.kept
    parity = parity_of()
    spots = {j: (g, i) for g, js in enumerate(groups) for i, j in enumerate(js)}
    gather_rows(
        x_scr,
        chunk,
        [[refs_of[spots[j][0]].at[spots[j][1]] for j in range(shards)] for refs_of in (outer_refs, inner_refs)],
    )
    mask = jnp.concatenate([mask_ref[0], mask_ref[3]], axis=0)

    def around(units):
        return [
            masked(expand(x_scr, w_ref, par_ref, k, units), mask) for k in range(2)
        ]

    def convolve(units, cells):
        width = units.stop - units.start
        line = lax.broadcasted_iota(jnp.int32, (kept, width), 0)
        not_first, not_last = None, None
        for at, size in zip(chunk.starts, chunk.widths):
            first, last = line != at, line != at + size - 1
            not_first = first if not_first is None else not_first & first
            not_last = last if not_last is None else not_last & last
        halves = ([], [])
        for k in range(2):
            rows = [
                cells[k][:kept],
                own_ref[k, :kept, units],
                own_ref[k, kept:, units],
                cells[k][kept:],
            ]
            taps = [
                [
                    jnp.where(
                        parity == 0,
                        par_ref[i * 6 + col * 2 + k : i * 6 + col * 2 + k + 1, units],
                        par_ref[(2 - i) * 6 + col * 2 + k : (2 - i) * 6 + col * 2 + k + 1, units],
                    )
                    for col in range(3)
                ]
                for i in range(3)
            ]
            for place in range(2):
                sums = []
                for tap_col in range(3):
                    total = None
                    for i in range(3):
                        term = taps[i][tap_col] * rows[place + i]
                        total = term if total is None else total + term
                    sums.append(total)
                left = jnp.where(not_first, pltpu.roll(sums[0], 1, 0), 0.0)
                right = jnp.where(not_last, pltpu.roll(sums[2], kept - 1, 0), 0.0)
                halves[k].append(sums[1] + left + right + par_ref[20 + k : 21 + k, units])
        for place in range(2):
            hidden = halves[0][place] * silu(halves[1][place])
            out_ref[(1 - place) * kept : (2 - place) * kept, units] = hidden.astype(jnp.bfloat16)

    tiles = tiles_of(w_ref.shape[2])
    cells = around(tiles[0])
    for t, units in enumerate(tiles):
        coming = around(tiles[t + 1]) if t + 1 < len(tiles) else None
        convolve(units, cells)
        cells = coming


def project(weight_ref, hidden_ref, depth, j):
    start = lax.bitwise_xor(lax.axis_index("tensor"), j) * depth
    return lax.dot_general(
        weight_ref[pl.ds(pl.multiple_of(start, GROUP), depth), :],
        hidden_ref[...],
        (((1,), (1,)), ((), ())),
        preferred_element_type=jnp.float32,
    )


def unit_kernel(weight_ref, hidden_ref, *refs, chunk, j):
    out_ref = refs[-1]
    sums = project(weight_ref, hidden_ref, chunk.depth, j)
    for ref in refs[:-1]:
        sums = sums + chunk.get_unit(ref[...].astype(jnp.float32))
    chunk.put_unit(out_ref, sums.astype(jnp.bfloat16))


def share_kernel(weight_ref, hidden_ref, unit_ref, out_ref, *, chunk):
    sums = project(weight_ref, hidden_ref, chunk.depth, 0)
    out_ref[...] = sums + chunk.get_unit(unit_ref[...].astype(jnp.float32))


def final_kernel(width_ref, mask_ref, share_ref, *refs, chunk, sources):
    out_ref = refs[-1]
    if len(refs) > sources + 1:
        out_ref[...] = refs[sources][...]
    sums = share_ref[...]
    for ref in refs[:sources]:
        sums = sums + chunk.get_unit(ref[...].astype(jnp.float32))
    cells = sums.T
    parity = parity_of()
    for place in range(2):
        row = jnp.where(parity == 0, 1 - place, place)
        mask = mask_ref[2 - place][:, :1] > 0
        part = cells[place * chunk.kept : (place + 1) * chunk.kept]
        part = jnp.where(mask, part, 0.0).astype(jnp.bfloat16)
        clips = chunk.clips(width_ref, width_ref.shape[0])
        for clip, width, at in zip(clips, chunk.widths, chunk.starts):
            out_ref[clip, row, :width, :] = part[at : at + width]
            if width < out_ref.shape[2]:
                blank = jnp.zeros((out_ref.shape[2] - width, chunk.depth), jnp.bfloat16)
                out_ref[clip, row, width:, :] = blank


VMEM = pl.BlockSpec(memory_space=pltpu.VMEM)
MIB = 1024 * 1024


def after(value, *others):
    return lax.optimization_barrier((value,) + others)[0]


def on_device_packed(
    latents,
    clip_height,
    clip_width,
    expand_weight,
    expand_bias,
    depth_weight,
    depth_bias,
    project_weight,
):
    batch_size, row_count, col_count, depth = latents.shape
    shards, row_devices = lax.axis_size("tensor"), lax.axis_size("row")
    hidden_count = expand_weight.shape[2]
    full_depth = shards * depth
    chunks = chunks_of(batch_size, col_count, depth)
    count = len(chunks)
    own = pl.pallas_call(
        functools.partial(pack_kernel, chunks=chunks),
        out_shape=[jax.ShapeDtypeStruct((2, c.lines, LANES), jnp.bfloat16) for c in chunks],
        grid_spec=pltpu.PrefetchScalarGridSpec(
            num_scalar_prefetch=1, grid=(), in_specs=[VMEM], out_specs=[VMEM] * count
        ),
        compiler_params=pltpu.CompilerParams(vmem_limit_bytes=16 * MIB),
        name="pack",
    )(clip_width, latents)
    project_turned = project_weight.T

    sibling = [(i, i ^ 1) for i in range(row_devices)]
    beyond = [(i, i + 1) for i in range(1, row_devices - 1, 2)]
    beyond = beyond + [(b, a) for a, b in beyond]
    near = [(i, i ^ 1) for i in range(4)]
    two_off = [(i, i ^ 2) for i in range(4)]
    opposite = [(i, i ^ 3) for i in range(4)]
    middle = [(1, 2), (2, 1)]
    to_end = [(2, 3), (1, 0)]
    from_end = [(0, 1), (3, 2)]

    def edge_rows(packets, groups):
        return [
            [jnp.concatenate([packets[j][side : side + 1] for j in js], axis=0) for js in groups]
            for side in range(2)
        ]

    def send_rows(inner, outer):
        return (
            [lax.ppermute(x, "row", sibling) for x in inner],
            [lax.ppermute(x, "row", beyond) for x in outer],
        )

    def relay(mine, tables, *others):
        second = lax.ppermute(mine, "tensor", two_off)
        first = lax.ppermute(mine, "tensor", near)
        across = lax.ppermute(after(mine, second, *others), "tensor", middle)
        passed = lax.ppermute(after(second, *others), "tensor", to_end)
        return [mine, first, second, after(across, tables) + passed]

    def direct(mine):
        third, second, first = [
            lax.ppermute(mine, "tensor", pairs) for pairs in (opposite, two_off, near)
        ]
        return [mine, first, second, third]

    out = None
    weights, token = pl.pallas_call(
        functools.partial(load_kernel, shards=shards, depth=depth),
        out_shape=[
            jax.ShapeDtypeStruct(expand_weight.shape, jnp.bfloat16),
            jax.ShapeDtypeStruct((8, 128), jnp.float32),
        ],
        in_specs=[pl.BlockSpec(memory_space=pl.ANY)],
        out_specs=[VMEM, VMEM],
        scratch_shapes=[pltpu.SemaphoreType.DMA((2, shards, 2))],
        compiler_params=pltpu.CompilerParams(vmem_limit_bytes=36 * MIB),
        name="load_weights",
    )(after(expand_weight, own[0]))
    taps = after(depth_weight, token)
    parameters, *masks = pl.pallas_call(
        functools.partial(table_kernel, chunks=chunks),
        out_shape=[jax.ShapeDtypeStruct((22, hidden_count), jnp.float32)]
        + [jax.ShapeDtypeStruct((4, c.kept, 128), jnp.float32) for c in chunks],
        grid_spec=pltpu.PrefetchScalarGridSpec(
            num_scalar_prefetch=2, grid=(), in_specs=[VMEM] * 3, out_specs=[VMEM] * (1 + count)
        ),
        compiler_params=pltpu.CompilerParams(vmem_limit_bytes=16 * MIB),
        name="tables",
    )(clip_height, clip_width, taps, expand_bias, depth_bias)
    groups = ((0,), (1, 2), (3,))
    inner, outer = send_rows(*edge_rows(own[:1], groups[:1]))
    early = send_rows(*edge_rows(own[1:], groups[:1]))
    packets = relay(own[0], parameters, token, *inner, *outer, *early[0], *early[1])
    edges = edge_rows(packets, groups[1:])
    later = send_rows(*edges)
    inner, outer = inner + later[0], outer + later[1]
    upcoming = direct(after(own[1], edges[0][-1], edges[1][-1]))
    for number, chunk in enumerate(chunks):
        if number:
            packets, groups = list(lax.optimization_barrier((*upcoming, hidden))[:shards]), ((0,), (1, 2, 3))
            later = send_rows(*edge_rows(packets, groups[1:]))
            inner, outer = early[0] + later[0], early[1] + later[1]
            packets[0] = after(packets[0], far)
        rows = pl.pallas_call(
            functools.partial(own_kernel, chunk=chunk, shards=shards),
            out_shape=jax.ShapeDtypeStruct((2, chunk.tokens, hidden_count), jnp.float32),
            in_specs=[VMEM] * (shards + 3),
            out_specs=VMEM,
            scratch_shapes=[pltpu.VMEM((chunk.tokens, full_depth), jnp.bfloat16)],
            compiler_params=pltpu.CompilerParams(vmem_limit_bytes=16 * MIB),
            cost_estimate=pl.CostEstimate(
                flops=1000,
                bytes_accessed=1000,
                transcendentals=0,
            ),
            name="expand_own",
        )(*packets, masks[number], parameters, weights)
        if number:
            inner[0] = after(inner[0], last_unit)
        hidden = pl.pallas_call(
            functools.partial(hidden_kernel, chunk=chunk, shards=shards, groups=groups),
            out_shape=jax.ShapeDtypeStruct((chunk.tokens, hidden_count), jnp.bfloat16),
            in_specs=[VMEM] * (2 * len(groups) + 4),
            out_specs=VMEM,
            scratch_shapes=[pltpu.VMEM((chunk.tokens, full_depth), jnp.bfloat16)],
            compiler_params=pltpu.CompilerParams(vmem_limit_bytes=16 * MIB),
            cost_estimate=pl.CostEstimate(
                flops=1000,
                bytes_accessed=1000,
                transcendentals=0,
            ),
            name="expand_conv",
        )(*inner, *outer, rows, masks[number], parameters, weights)

        cost = pl.CostEstimate(
            flops=2 * chunk.tokens * depth * hidden_count,
            bytes_accessed=2 * depth * hidden_count + 2 * chunk.tokens * hidden_count,
            transcendentals=0,
        )

        def unit(j, *added):
            return pl.pallas_call(
                functools.partial(unit_kernel, chunk=chunk, j=j),
                out_shape=jax.ShapeDtypeStruct(chunk.unit, jnp.bfloat16),
                in_specs=[VMEM] * (2 + len(added)),
                out_specs=VMEM,
                compiler_params=pltpu.CompilerParams(vmem_limit_bytes=16 * MIB),
                cost_estimate=cost,
                name=f"project_{j}",
            )(project_turned, hidden, *added)

        far = unit(3)
        relayed = lax.ppermute(far, "tensor", from_end)
        across = lax.ppermute(far, "tensor", middle)
        close = unit(1)
        if number:
            relayed = after(relayed, out)
        else:
            relayed, across = lax.optimization_barrier((relayed, across))
        last_unit = unit(2, relayed)
        distant = lax.ppermute(last_unit, "tensor", two_off)
        close = after(close, last_unit, across) if number else after(close, last_unit)
        arrived = [across, lax.ppermute(close, "tensor", near)]
        share = pl.pallas_call(
            functools.partial(share_kernel, chunk=chunk),
            out_shape=jax.ShapeDtypeStruct((depth, chunk.tokens), jnp.float32),
            in_specs=[VMEM] * 3,
            out_specs=VMEM,
            compiler_params=pltpu.CompilerParams(vmem_limit_bytes=16 * MIB),
            cost_estimate=pl.CostEstimate(flops=10**10, bytes_accessed=10**8, transcendentals=0),
            name="project_0",
        )(project_turned, hidden, distant)
        extra = [] if out is None else [out]
        out = pl.pallas_call(
            functools.partial(final_kernel, chunk=chunk, sources=len(arrived)),
            out_shape=jax.ShapeDtypeStruct(latents.shape, jnp.bfloat16),
            grid_spec=pltpu.PrefetchScalarGridSpec(
                num_scalar_prefetch=1,
                grid=(),
                in_specs=[VMEM] * (2 + len(arrived) + len(extra)),
                out_specs=VMEM,
            ),
            compiler_params=pltpu.CompilerParams(vmem_limit_bytes=16 * MIB),
            cost_estimate=pl.CostEstimate(flops=10**11, bytes_accessed=10**9, transcendentals=0),
            name="finish",
        )(clip_width, masks[number], share, *arrived, *extra)
    return out


def chunks_of(batch_size, col_count, depth):
    widths = slot_widths(batch_size, col_count)
    half = batch_size // 2
    return [Chunk(slots, widths, depth) for slots in (list(range(half)), list(range(half, batch_size)))]


def on_device(latents, clip_height, clip_width, expand_weight, *rest_of):
    batch_size, row_count, col_count, depth = latents.shape
    fits = (
        batch_size >= 2
        and row_count == 2
        and lax.axis_size("row") % 2 == 0
        and lax.axis_size("tensor") == 4
        and depth > LANES
        and (depth - LANES) % GROUP == 0
        and depth % GROUP == 0
        and all(
            c.block in (128, 256, 512) and c.kept % GROUP == 0 and c.left in (0, 64)
            for c in chunks_of(batch_size, col_count, depth)
        )
    )
    run = on_device_packed if fits else on_device_plain
    return run(latents, clip_height, clip_width, expand_weight, *rest_of)


def solution(mesh):
    in_specs = (
        P(None, "row", None, "tensor"),
        P(),
        P(),
        P(None, None, "tensor"),
        P(None, "tensor"),
        P(None, None, None, "tensor"),
        P(None, "tensor"),
        P("tensor", None),
    )
    out_specs = P(None, "row", None, "tensor")
    return jax.shard_map(
        on_device, mesh=mesh, in_specs=in_specs, out_specs=out_specs, check_vma=False
    )
```

```python
import functools

import jax
import jax.numpy as jnp
from jax import lax
from jax.experimental import pallas as pl
from jax.experimental.pallas import tpu as pltpu
from jax.sharding import PartitionSpec as P

LANES = 512
GROUP = 16
TILE = 256


def halo_rows(cells):
    count = lax.axis_size("row")
    ends = count - 1
    head = cells[:, :1]
    tail = cells[:, -1:]
    above = lax.ppermute(tail, "row", [(i, i + 1) for i in range(ends)])
    below = lax.ppermute(head, "row", [(i + 1, i) for i in range(ends)])
    return jnp.concatenate([above, cells, below], axis=1)


def depthwise(padded, depth_weight, depth_bias, row_count, col_count):
    widened = jnp.pad(padded, ((0, 0), (0, 0), (1, 1), (0, 0), (0, 0)))
    out_shape = (widened.shape[0], row_count, col_count) + widened.shape[3:]
    depth_out = jnp.zeros(out_shape, jnp.float32) + depth_bias
    for tap_row in range(3):
        for tap_col in range(3):
            depth_out = (
                depth_out
                + depth_weight[tap_row, tap_col]
                * widened[:, tap_row : tap_row + row_count, tap_col : tap_col + col_count]
            )
    return depth_out


def on_device_plain(
    latents,
    clip_height,
    clip_width,
    expand_weight,
    expand_bias,
    depth_weight,
    depth_bias,
    project_weight,
):
    batch_size, row_count, col_count, depth = latents.shape
    tokens = batch_size * row_count * col_count
    first_row = lax.axis_index("row") * row_count
    row_ids = first_row + jnp.arange(row_count, dtype=jnp.int32)
    col_ids = jnp.arange(col_count, dtype=jnp.int32)
    valid_mask = (
        (row_ids[None, :, None] < clip_height[:, None, None])
        & (col_ids[None, None, :] < clip_width[:, None, None])
    ).astype(jnp.float32)[..., None]
    channels = latents.reshape(tokens, depth).T
    gathered = lax.all_gather(channels, "tensor", axis=0, tiled=True)
    pre_act = jnp.einsum("dt,kdf->tkf", gathered, expand_weight, preferred_element_type=jnp.float32)
    pre_act = pre_act.reshape(batch_size, row_count, col_count, 2, -1)
    expanded = (jax.nn.silu(pre_act + expand_bias) * valid_mask[..., None]).astype(jnp.bfloat16)
    padded = halo_rows(expanded)
    depth_out = depthwise(padded, depth_weight, depth_bias, row_count, col_count)
    hidden = (depth_out[:, :, :, 0] * jax.nn.silu(depth_out[:, :, :, 1])).astype(jnp.bfloat16)
    partial_term = jnp.einsum(
        "tf,fd->dt", hidden.reshape(tokens, -1), project_weight, preferred_element_type=jnp.float32
    ).astype(jnp.bfloat16)
    summed = lax.psum_scatter(partial_term, "tensor", scatter_dimension=0, tiled=True)
    summed = summed.T.reshape(latents.shape).astype(jnp.float32)
    return (summed * valid_mask).astype(jnp.bfloat16)


def slot_clips(width_ref, batch_size):
    narrow, least = jnp.int32(0), width_ref[0]
    for b in range(1, batch_size):
        closer = width_ref[b] < least
        narrow = jnp.where(closer, b, narrow)
        least = jnp.where(closer, width_ref[b], least)
    return [jnp.where(narrow <= s, s + 1, s) for s in range(batch_size - 1)] + [narrow]


def slot_widths(batch_size, col_count):
    return [col_count] * (batch_size - 1) + [col_count // 2]


class Chunk:
    def __init__(self, slots, widths, depth):
        self.slots = slots
        self.widths = [widths[s] for s in slots]
        self.starts = [sum(self.widths[:i]) for i in range(len(slots))]
        self.kept = sum(self.widths)
        self.block = -(-self.kept // 128) * 128
        self.depth, self.rest = depth, depth - LANES
        across = LANES // self.block
        groups = self.rest // GROUP
        self.places = [(g // across * GROUP, g % across * self.block) for g in range(groups)]
        self.lines = self.kept + -(-groups // across) * GROUP
        self.tokens = 2 * self.kept
        self.full, self.left = self.tokens // 128, self.tokens % 128
        self.upper = -(-depth // (2 * GROUP)) * GROUP
        self.unit = (self.full * depth + (self.upper if self.left else 0), 128)

    def clips(self, width_ref, batch_size):
        order = slot_clips(width_ref, batch_size)
        return [order[s] for s in self.slots]

    def mask_column(self, height_ref, width_ref, row_id):
        pieces = []
        clips = self.clips(width_ref, width_ref.shape[0])
        for clip, width in zip(clips, self.widths):
            bound = jnp.where((row_id >= 0) & (row_id < height_ref[clip]), width_ref[clip], 0)
            col = lax.broadcasted_iota(jnp.int32, (width, 128), 0)
            pieces.append((col < bound).astype(jnp.float32))
        return jnp.concatenate(pieces, axis=0)

    def put_unit(self, unit_ref, sums):
        depth, at = self.depth, self.full * self.depth
        for b in range(self.full):
            unit_ref[b * depth : (b + 1) * depth, :] = sums[:, b * 128 : (b + 1) * 128]
        if self.left:
            tail = sums[:, self.full * 128 :]
            lower = depth - self.upper
            unit_ref[at : at + self.upper, : self.left] = tail[: self.upper]
            unit_ref[at : at + lower, self.left :] = tail[self.upper :]
            if lower < self.upper:
                unit_ref[at + lower :, self.left :] = jnp.zeros(
                    (self.upper - lower, 128 - self.left), sums.dtype
                )

    def get_unit(self, unit):
        depth, at = self.depth, self.full * self.depth
        blocks = [unit[b * depth : (b + 1) * depth, :] for b in range(self.full)]
        if self.left:
            lower = depth - self.upper
            blocks.append(
                jnp.concatenate(
                    [unit[at : at + self.upper, : self.left], unit[at : at + lower, self.left :]], axis=0
                )
            )
        return jnp.concatenate(blocks, axis=1)


def parity_of():
    return lax.rem(lax.axis_index("row"), 2)


def row_of(place, parity):
    return jnp.where(parity == 0, (-1, 0, 1, 2)[place], (2, 1, 0, -1)[place])


def silu(v):
    h = 0.5 * v
    return h + h * jnp.tanh(h)


def pack_kernel(width_ref, x_ref, *out_refs, chunks):
    parity = parity_of()
    for chunk, out_ref in zip(chunks, out_refs):
        for place in range(2):
            row = jnp.where(parity == 0, 1 - place, place)
            tails = []
            for clip, width, at in zip(
                chunk.clips(width_ref, x_ref.shape[0]), chunk.widths, chunk.starts
            ):
                out_ref[place, at : at + width, :] = x_ref[clip, row, :width, :LANES]
                tails.append(x_ref[clip, row, :width, LANES:].astype(jnp.float32))
            if chunk.block > chunk.kept:
                tails.append(jnp.zeros((chunk.block - chunk.kept, chunk.rest), jnp.float32))
            turned = jnp.concatenate(tails, axis=0).T.astype(jnp.bfloat16)
            kept = chunk.kept
            out_ref[place, kept:, :] = jnp.zeros((chunk.lines - kept, LANES), jnp.bfloat16)
            for g, (down, over) in enumerate(chunk.places):
                out_ref[place, kept + down : kept + down + GROUP, over : over + chunk.block] = turned[
                    g * GROUP : (g + 1) * GROUP
                ]


def tiles_of(hidden_count):
    return [slice(at, min(at + TILE, hidden_count)) for at in range(0, hidden_count, TILE)]


def gather_rows(x_scr, chunk, rows):
    kept = chunk.kept
    for place, packets in enumerate(rows):
        lines = slice(place * kept, (place + 1) * kept)
        tails = []
        for j, packet in enumerate(packets):
            x_scr[lines, j * LANES : (j + 1) * LANES] = packet[:kept, :]
            for down, over in chunk.places:
                tails.append(packet[kept + down : kept + down + GROUP, over : over + chunk.block])
        turned = jnp.concatenate(tails, axis=0).astype(jnp.float32).T
        x_scr[lines, len(packets) * LANES :] = turned[:kept].astype(jnp.bfloat16)


def load_kernel(w_ref, out_ref, token_ref, sems, *, shards, depth):
    token_ref[...] = jnp.zeros_like(token_ref)
    me = lax.axis_index("tensor")
    rest = depth - LANES
    copies = []
    for k in range(2):
        for j in range(shards):
            base = lax.bitwise_xor(me, j) * depth
            for part, (source, size, target) in enumerate(
                ((base, LANES, j * LANES), (base + LANES, rest, shards * LANES + j * rest))
            ):
                copies.append(
                    pltpu.make_async_copy(
                        w_ref.at[k, pl.ds(pl.multiple_of(source, GROUP), size)],
                        out_ref.at[k, pl.ds(target, size)],
                        sems.at[k, j, part],
                    )
                )
    for copy in copies:
        copy.start()
    for copy in copies:
        copy.wait()


def table_kernel(height_ref, width_ref, dw_ref, eb_ref, db_ref, par_ref, *mask_refs, chunks):
    parity = parity_of()
    for chunk, mask_ref in zip(chunks, mask_refs):
        for place in range(4):
            row_id = lax.axis_index("row") * 2 + row_of(place, parity)
            mask_ref[place] = chunk.mask_column(height_ref, width_ref, row_id)
    for i in range(3):
        for col in range(3):
            par_ref[i * 6 + col * 2 : i * 6 + col * 2 + 2, :] = dw_ref[i, col]
    par_ref[18:20, :] = eb_ref[...]
    par_ref[20:22, :] = db_ref[...]


def expand(x_scr, w_ref, par_ref, k, units):
    pre_act = jnp.dot(x_scr[...], w_ref[k, :, units], preferred_element_type=jnp.float32)
    return silu(pre_act + par_ref[18 + k : 19 + k, units])


def masked(cells, mask):
    width = cells.shape[1]
    return cells * jnp.concatenate([mask] * -(-width // 128), axis=1)[:, :width]


def own_kernel(*refs, chunk, shards):
    packet_refs, (mask_ref, par_ref, w_ref, out_ref, x_scr) = refs[:shards], refs[shards:]
    kept = chunk.kept
    gather_rows(x_scr, chunk, [[p.at[1] for p in packet_refs], [p.at[0] for p in packet_refs]])
    mask = jnp.concatenate([mask_ref[1], mask_ref[2]], axis=0)
    for units in tiles_of(w_ref.shape[2]):
        for k in range(2):
            out_ref[k, :, units] = masked(expand(x_scr, w_ref, par_ref, k, units), mask)


def hidden_kernel(*refs, chunk, shards, groups):
    count = len(groups)
    inner_refs, outer_refs = refs[:count], refs[count : 2 * count]
    own_ref, mask_ref, par_ref, w_ref, out_ref, x_scr = refs[2 * count :]
    kept = chunk.kept
    parity = parity_of()
    spots = {j: (g, i) for g, js in enumerate(groups) for i, j in enumerate(js)}
    gather_rows(
        x_scr,
        chunk,
        [[refs_of[spots[j][0]].at[spots[j][1]] for j in range(shards)] for refs_of in (outer_refs, inner_refs)],
    )
    mask = jnp.concatenate([mask_ref[0], mask_ref[3]], axis=0)

    def around(units):
        return [
            masked(expand(x_scr, w_ref, par_ref, k, units), mask) for k in range(2)
        ]

    def convolve(units, cells):
        width = units.stop - units.start
        line = lax.broadcasted_iota(jnp.int32, (kept, width), 0)
        not_first, not_last = None, None
        for at, size in zip(chunk.starts, chunk.widths):
            first, last = line != at, line != at + size - 1
            not_first = first if not_first is None else not_first & first
            not_last = last if not_last is None else not_last & last
        halves = ([], [])
        for k in range(2):
            rows = [
                cells[k][:kept],
                own_ref[k, :kept, units],
                own_ref[k, kept:, units],
                cells[k][kept:],
            ]
            taps = [
                [
                    jnp.where(
                        parity == 0,
                        par_ref[i * 6 + col * 2 + k : i * 6 + col * 2 + k + 1, units],
                        par_ref[(2 - i) * 6 + col * 2 + k : (2 - i) * 6 + col * 2 + k + 1, units],
                    )
                    for col in range(3)
                ]
                for i in range(3)
            ]
            for place in range(2):
                sums = []
                for tap_col in range(3):
                    total = None
                    for i in range(3):
                        term = taps[i][tap_col] * rows[place + i]
                        total = term if total is None else total + term
                    sums.append(total)
                left = jnp.where(not_first, pltpu.roll(sums[0], 1, 0), 0.0)
                right = jnp.where(not_last, pltpu.roll(sums[2], kept - 1, 0), 0.0)
                halves[k].append(sums[1] + left + right + par_ref[20 + k : 21 + k, units])
        for place in range(2):
            hidden = halves[0][place] * silu(halves[1][place])
            out_ref[(1 - place) * kept : (2 - place) * kept, units] = hidden.astype(jnp.bfloat16)

    tiles = tiles_of(w_ref.shape[2])
    cells = around(tiles[0])
    for t, units in enumerate(tiles):
        coming = around(tiles[t + 1]) if t + 1 < len(tiles) else None
        convolve(units, cells)
        cells = coming


def project(weight_ref, hidden_ref, depth, j):
    start = lax.bitwise_xor(lax.axis_index("tensor"), j) * depth
    return lax.dot_general(
        weight_ref[pl.ds(pl.multiple_of(start, GROUP), depth), :],
        hidden_ref[...],
        (((1,), (1,)), ((), ())),
        preferred_element_type=jnp.float32,
    )


def unit_kernel(weight_ref, hidden_ref, *refs, chunk, j):
    out_ref = refs[-1]
    sums = project(weight_ref, hidden_ref, chunk.depth, j)
    for ref in refs[:-1]:
        sums = sums + chunk.get_unit(ref[...].astype(jnp.float32))
    chunk.put_unit(out_ref, sums.astype(jnp.bfloat16))


def share_kernel(weight_ref, hidden_ref, unit_ref, out_ref, *, chunk):
    sums = project(weight_ref, hidden_ref, chunk.depth, 0)
    out_ref[...] = sums + chunk.get_unit(unit_ref[...].astype(jnp.float32))


def final_kernel(width_ref, mask_ref, share_ref, *refs, chunk, sources):
    out_ref = refs[-1]
    if len(refs) > sources + 1:
        out_ref[...] = refs[sources][...]
    sums = share_ref[...]
    for ref in refs[:sources]:
        sums = sums + chunk.get_unit(ref[...].astype(jnp.float32))
    cells = sums.T
    parity = parity_of()
    for place in range(2):
        row = jnp.where(parity == 0, 1 - place, place)
        mask = mask_ref[2 - place][:, :1] > 0
        part = cells[place * chunk.kept : (place + 1) * chunk.kept]
        part = jnp.where(mask, part, 0.0).astype(jnp.bfloat16)
        clips = chunk.clips(width_ref, width_ref.shape[0])
        for clip, width, at in zip(clips, chunk.widths, chunk.starts):
            out_ref[clip, row, :width, :] = part[at : at + width]
            if width < out_ref.shape[2]:
                blank = jnp.zeros((out_ref.shape[2] - width, chunk.depth), jnp.bfloat16)
                out_ref[clip, row, width:, :] = blank


VMEM = pl.BlockSpec(memory_space=pltpu.VMEM)
MIB = 1024 * 1024


def after(value, *others):
    return lax.optimization_barrier((value,) + others)[0]


def on_device_packed(
    latents,
    clip_height,
    clip_width,
    expand_weight,
    expand_bias,
    depth_weight,
    depth_bias,
    project_weight,
):
    batch_size, row_count, col_count, depth = latents.shape
    shards, row_devices = lax.axis_size("tensor"), lax.axis_size("row")
    hidden_count = expand_weight.shape[2]
    full_depth = shards * depth
    chunks = chunks_of(batch_size, col_count, depth)
    count = len(chunks)
    own = pl.pallas_call(
        functools.partial(pack_kernel, chunks=chunks),
        out_shape=[jax.ShapeDtypeStruct((2, c.lines, LANES), jnp.bfloat16) for c in chunks],
        grid_spec=pltpu.PrefetchScalarGridSpec(
            num_scalar_prefetch=1, grid=(), in_specs=[VMEM], out_specs=[VMEM] * count
        ),
        compiler_params=pltpu.CompilerParams(vmem_limit_bytes=16 * MIB),
        name="pack",
    )(clip_width, latents)
    project_turned = project_weight.T

    sibling = [(i, i ^ 1) for i in range(row_devices)]
    beyond = [(i, i + 1) for i in range(1, row_devices - 1, 2)]
    beyond = beyond + [(b, a) for a, b in beyond]
    near = [(i, i ^ 1) for i in range(4)]
    two_off = [(i, i ^ 2) for i in range(4)]
    opposite = [(i, i ^ 3) for i in range(4)]
    middle = [(1, 2), (2, 1)]
    to_end = [(2, 3), (1, 0)]
    from_end = [(0, 1), (3, 2)]

    def edge_rows(packets, groups):
        return [
            [jnp.concatenate([packets[j][side : side + 1] for j in js], axis=0) for js in groups]
            for side in range(2)
        ]

    def send_rows(inner, outer):
        return (
            [lax.ppermute(x, "row", sibling) for x in inner],
            [lax.ppermute(x, "row", beyond) for x in outer],
        )

    def relay(mine, tables, *others):
        second = lax.ppermute(mine, "tensor", two_off)
        first = lax.ppermute(mine, "tensor", near)
        across = lax.ppermute(after(mine, second, first, *others), "tensor", middle)
        passed = lax.ppermute(after(second, first, *others), "tensor", to_end)
        return [mine, first, second, after(across, tables) + passed]

    def direct(mine):
        third, second, first = [
            lax.ppermute(mine, "tensor", pairs) for pairs in (opposite, two_off, near)
        ]
        return [mine, first, second, third]

    out = None
    weights, token = pl.pallas_call(
        functools.partial(load_kernel, shards=shards, depth=depth),
        out_shape=[
            jax.ShapeDtypeStruct(expand_weight.shape, jnp.bfloat16),
            jax.ShapeDtypeStruct((8, 128), jnp.float32),
        ],
        in_specs=[pl.BlockSpec(memory_space=pl.ANY)],
        out_specs=[VMEM, VMEM],
        scratch_shapes=[pltpu.SemaphoreType.DMA((2, shards, 2))],
        compiler_params=pltpu.CompilerParams(vmem_limit_bytes=36 * MIB),
        name="load_weights",
    )(after(expand_weight, own[0]))
    taps = after(depth_weight, token)
    parameters, *masks = pl.pallas_call(
        functools.partial(table_kernel, chunks=chunks),
        out_shape=[jax.ShapeDtypeStruct((22, hidden_count), jnp.float32)]
        + [jax.ShapeDtypeStruct((4, c.kept, 128), jnp.float32) for c in chunks],
        grid_spec=pltpu.PrefetchScalarGridSpec(
            num_scalar_prefetch=2, grid=(), in_specs=[VMEM] * 3, out_specs=[VMEM] * (1 + count)
        ),
        compiler_params=pltpu.CompilerParams(vmem_limit_bytes=16 * MIB),
        name="tables",
    )(clip_height, clip_width, taps, expand_bias, depth_bias)
    groups = ((0,), (1, 2), (3,))
    inner, outer = send_rows(*edge_rows(own[:1], groups[:1]))
    early = send_rows(*edge_rows(own[1:], groups[:1]))
    packets = relay(own[0], parameters, token, *inner, *outer, *early[0], *early[1])
    edges = edge_rows(packets, groups[1:])
    later = send_rows(*edges)
    inner, outer = inner + later[0], outer + later[1]
    upcoming = direct(after(own[1], edges[0][-1], edges[1][-1]))
    for number, chunk in enumerate(chunks):
        if number:
            packets, groups = list(lax.optimization_barrier((*upcoming, hidden))[:shards]), ((0,), (1, 2, 3))
            later = send_rows(*edge_rows(packets, groups[1:]))
            inner, outer = early[0] + later[0], early[1] + later[1]
            packets[0] = after(packets[0], far)
        rows = pl.pallas_call(
            functools.partial(own_kernel, chunk=chunk, shards=shards),
            out_shape=jax.ShapeDtypeStruct((2, chunk.tokens, hidden_count), jnp.float32),
            in_specs=[VMEM] * (shards + 3),
            out_specs=VMEM,
            scratch_shapes=[pltpu.VMEM((chunk.tokens, full_depth), jnp.bfloat16)],
            compiler_params=pltpu.CompilerParams(vmem_limit_bytes=16 * MIB),
            cost_estimate=pl.CostEstimate(
                flops=1000,
                bytes_accessed=1000,
                transcendentals=0,
            ),
            name="expand_own",
        )(*packets, masks[number], parameters, weights)
        if number:
            inner[0] = after(inner[0], last_unit)
        hidden = pl.pallas_call(
            functools.partial(hidden_kernel, chunk=chunk, shards=shards, groups=groups),
            out_shape=jax.ShapeDtypeStruct((chunk.tokens, hidden_count), jnp.bfloat16),
            in_specs=[VMEM] * (2 * len(groups) + 4),
            out_specs=VMEM,
            scratch_shapes=[pltpu.VMEM((chunk.tokens, full_depth), jnp.bfloat16)],
            compiler_params=pltpu.CompilerParams(vmem_limit_bytes=16 * MIB),
            cost_estimate=pl.CostEstimate(
                flops=1000,
                bytes_accessed=1000,
                transcendentals=0,
            ),
            name="expand_conv",
        )(*inner, *outer, rows, masks[number], parameters, weights)

        cost = pl.CostEstimate(
            flops=2 * chunk.tokens * depth * hidden_count,
            bytes_accessed=2 * depth * hidden_count + 2 * chunk.tokens * hidden_count,
            transcendentals=0,
        )

        def unit(j, *added):
            return pl.pallas_call(
                functools.partial(unit_kernel, chunk=chunk, j=j),
                out_shape=jax.ShapeDtypeStruct(chunk.unit, jnp.bfloat16),
                in_specs=[VMEM] * (2 + len(added)),
                out_specs=VMEM,
                compiler_params=pltpu.CompilerParams(vmem_limit_bytes=16 * MIB),
                cost_estimate=cost,
                name=f"project_{j}",
            )(project_turned, hidden, *added)

        far = unit(3)
        relayed = lax.ppermute(far, "tensor", from_end)
        across = lax.ppermute(far, "tensor", middle)
        close = unit(1)
        if number:
            relayed = after(relayed, out)
        else:
            relayed, across = lax.optimization_barrier((relayed, across))
        last_unit = unit(2, relayed)
        distant = lax.ppermute(last_unit, "tensor", two_off)
        close = after(close, last_unit, across) if number else after(close, last_unit)
        arrived = [across, lax.ppermute(close, "tensor", near)]
        share = pl.pallas_call(
            functools.partial(share_kernel, chunk=chunk),
            out_shape=jax.ShapeDtypeStruct((depth, chunk.tokens), jnp.float32),
            in_specs=[VMEM] * 3,
            out_specs=VMEM,
            compiler_params=pltpu.CompilerParams(vmem_limit_bytes=16 * MIB),
            cost_estimate=pl.CostEstimate(flops=10**10, bytes_accessed=10**8, transcendentals=0),
            name="project_0",
        )(project_turned, hidden, distant)
        extra = [] if out is None else [out]
        out = pl.pallas_call(
            functools.partial(final_kernel, chunk=chunk, sources=len(arrived)),
            out_shape=jax.ShapeDtypeStruct(latents.shape, jnp.bfloat16),
            grid_spec=pltpu.PrefetchScalarGridSpec(
                num_scalar_prefetch=1,
                grid=(),
                in_specs=[VMEM] * (2 + len(arrived) + len(extra)),
                out_specs=VMEM,
            ),
            compiler_params=pltpu.CompilerParams(vmem_limit_bytes=16 * MIB),
            cost_estimate=pl.CostEstimate(flops=10**11, bytes_accessed=10**9, transcendentals=0),
            name="finish",
        )(clip_width, masks[number], share, *arrived, *extra)
    return out


def chunks_of(batch_size, col_count, depth):
    widths = slot_widths(batch_size, col_count)
    half = batch_size // 2
    return [Chunk(slots, widths, depth) for slots in (list(range(half)), list(range(half, batch_size)))]


def on_device(latents, clip_height, clip_width, expand_weight, *rest_of):
    batch_size, row_count, col_count, depth = latents.shape
    fits = (
        batch_size >= 2
        and row_count == 2
        and lax.axis_size("row") % 2 == 0
        and lax.axis_size("tensor") == 4
        and depth > LANES
        and (depth - LANES) % GROUP == 0
        and depth % GROUP == 0
        and all(
            c.block in (128, 256, 512) and c.kept % GROUP == 0 and c.left in (0, 64)
            for c in chunks_of(batch_size, col_count, depth)
        )
    )
    run = on_device_packed if fits else on_device_plain
    return run(latents, clip_height, clip_width, expand_weight, *rest_of)


def solution(mesh):
    in_specs = (
        P(None, "row", None, "tensor"),
        P(),
        P(),
        P(None, None, "tensor"),
        P(None, "tensor"),
        P(None, None, None, "tensor"),
        P(None, "tensor"),
        P("tensor", None),
    )
    out_specs = P(None, "row", None, "tensor")
    return jax.shard_map(
        on_device, mesh=mesh, in_specs=in_specs, out_specs=out_specs, check_vma=False
    )
```
